128 devices in a mesh: dp: 4 (over x), ep: 16 (over y_lo, z, core), tp: 2 (over y_hi).
Axes of the slice: x: 4, y: 4 (y_hi: 2, y_lo: 2; y = y_hi * 2 + y_lo), z: 4, core: 2. Of those that a mesh axis runs over, the one named last changes fastest.
Arguments:
- tokens: bfloat16 [8192, 1280], P(('dp', 'ep')), may hold values from -6 to 6
- grad_out: bfloat16 [8192, 1280], P(('dp', 'ep')), may hold values from -6 to 6
- doc_ids: int32 [4, 2048], P('dp'), may hold values from 0 to 1, never falling along the last dimension, each value on 1 to 1280 neighbouring positions
- piece_starts: int32 [4, 2], P('dp'), may hold values from 0 to 1792, as said below
- piece_ends: int32 [4, 2], P('dp'), may hold values from 256 to 2048, as said below
- routes: int32 [8192, 7], P(('dp', 'ep')), may hold values from 0 to 62, all different within a row; in each aligned block of 128 rows (0 to 127, 128 to 255, ...) at most 16 rows name the same one
- norm1_gain: float32 [1280], replicated, may hold values from 0.5 to 1.5
- norm2_gain: float32 [1280], replicated, may hold values from 0.5 to 1.5
- query_weight: bfloat16 [1280, 1280], P(None, 'tp'), may hold values from -0.15625 to 0.15625
- key_weight: bfloat16 [1280, 1280], P(None, 'tp'), may hold values from -0.15625 to 0.15625
- value_weight: bfloat16 [1280, 1280], P(None, 'tp'), may hold values from -0.15625 to 0.15625
- output_weight: bfloat16 [1280, 1280], P('tp'), may hold values from -1.5 to 1.5
- router_weight: bfloat16 [1280, 63], replicated, may hold values from -0.079589844 to 0.079589844
- shared_gate: bfloat16 [1280, 896], P(None, 'tp'), may hold values from -0.15625 to 0.15625
- shared_up: bfloat16 [1280, 896], P(None, 'tp'), may hold values from -0.15625 to 0.15625
- shared_down: bfloat16 [896, 1280], P('tp'), may hold values from -0.375 to 0.375
- expert_gate: bfloat16 [64, 1280, 896], P('ep', None, 'tp'), may hold values from -0.15625 to 0.15625
- expert_up: bfloat16 [64, 1280, 896], P('ep', None, 'tp'), may hold values from -0.15625 to 0.15625
- expert_down: bfloat16 [64, 896, 1280], P('ep', 'tp'), may hold values from -0.75 to 0.75
Outputs:
- output: bfloat16 [8192, 1280], P(('dp', 'ep'))
- grad_tokens: float32 [8192, 1280], P(('dp', 'ep'))
- grad_norm1_gain: float32 [1280], P(('dp', 'ep'))
- grad_norm2_gain: float32 [1280], P(('dp', 'ep'))
- grad_query_weight: float32 [1280, 1280], P(('dp', 'ep'), 'tp')
- grad_key_weight: float32 [1280, 1280], P(('dp', 'ep'), 'tp')
- grad_value_weight: float32 [1280, 1280], P(('dp', 'ep'), 'tp')
- grad_output_weight: float32 [1280, 1280], P('tp', ('dp', 'ep'))
- grad_router_weight: float32 [1280, 63], P(('dp', 'ep'))
- grad_shared_gate: float32 [1280, 896], P(('dp', 'ep'), 'tp')
- grad_shared_up: float32 [1280, 896], P(('dp', 'ep'), 'tp')
- grad_shared_down: float32 [896, 1280], P('tp', ('dp', 'ep'))
- grad_expert_gate: float32 [64, 1280, 896], P('ep', 'dp', 'tp')
- grad_expert_up: float32 [64, 1280, 896], P('ep', 'dp', 'tp')
- grad_expert_down: float32 [64, 896, 1280], P('ep', 'tp', 'dp')
The draws below stay inside these ranges and needn't reach their ends.
Inputs may be any that keep to these rules, and one draw needn't show every extreme that they name: `doc_ids`: document numbers never fall along a row; a document has at most 1280 tokens. `piece_starts`: piece k of a row starts at k * 1024 or at k * 1024 + 768. `piece_ends`: each end is its piece's start plus 256. `routes`: A token names 7 different experts; within the tokens of one device no expert is named more than 16 times.
All inputs are finite; a program needn't handle non-finite values.
Results may differ from the reference program's by a relative error of at most 0.02.
Values may be sent and summed in bfloat16 or wider, within the bound.
No kernel may reach another device: no remote copies, remote signals or barrier semaphores. Data moves between devices by JAX's collectives and lax.ppermute only.
A program may use at most 320 MiB of HBM per device.

```python
import math
import jax
import jax.numpy as jnp
import numpy as np
from jax import lax

D = 1280
HEADS = 10
HEAD_DIM = 128
FF = 896
EXPERTS = 63
TOPK = 7
SLOTS = 64
DOC = 1024
PIECE = 256
ROWS = 128
CAPACITY = 16
GROUP = 2048
GROUPS = 4
TOKENS = 8192
DOCS = 2
DOC_MOST = 1280
PIECES = 2
N_TP = 2


def piece_layout(key):
    offsets_on = jax.random.randint(jax.random.fold_in(key, 11), (GROUPS, PIECES), 0, 2)
    offsets_on = offsets_on.at[0, 0].set(0).at[0, PIECES - 1].set(1)
    region = jnp.arange(PIECES, dtype=jnp.int32)[None, :] * DOC
    starts = region + offsets_on * (DOC - PIECE)
    return (starts.astype(jnp.int32), (starts + PIECE).astype(jnp.int32))


def draw_piece_starts(key, part):
    return piece_layout(key)[0]


def draw_piece_ends(key, part):
    return piece_layout(key)[1]


def block_levels(rng, shape, split, least, high):
    level, own = 1.0, jax.random.fold_in(rng, 6)
    for axis_at, blocks in split:
        draws = jnp.exp(jax.random.uniform(jax.random.fold_in(own, axis_at), (blocks,), jnp.float32, least / len(split), high / len(split)))
        level = level * jnp.repeat(draws, shape[axis_at] // blocks).reshape([-1 if axis == axis_at else 1 for axis in range(len(shape))])
    return level


def split_up(number_of, total, reach, lean):
    weights = [(1 << 20) // math.isqrt(standing ** lean) + 1 for standing in range(2, number_of + 1)]
    surplus, counts = total - reach - (number_of - 1), [1] * (number_of - 1)
    while surplus > 0:
        movable = [i for i in range(number_of - 1) if counts[i] < reach]
        mass, left = sum([weights[i] for i in movable]), surplus
        for i in movable:
            extra = min(reach - counts[i], max(1, left * weights[i] // mass), surplus)
            counts[i] = counts[i] + extra
            surplus = surplus - extra
    return np.array([reach] + counts)


def uneven_parts(rng, amount, total, reach, lean):
    if amount == 2:
        one = jax.random.randint(rng, (), max(1, total - reach), min(reach, total - 1) + 1)
        return jnp.stack([one, total - one])
    tallies = jnp.asarray(split_up(amount, total, reach, lean), jnp.int32)
    twos = (amount - 1) // 2
    source_of, receiver = tallies[1:1 + 2 * twos:2], tallies[2:2 + 2 * twos:2]
    slack = jnp.minimum(source_of - 1, reach - receiver)
    moved = jax.random.randint(jax.random.fold_in(rng, 1), (twos,), 0, 1 << 20) % (slack + 1)
    tallies = tallies.at[1:1 + 2 * twos:2].set(source_of - moved).at[2:2 + 2 * twos:2].set(receiver + moved)
    return tallies[jax.random.permutation(jax.random.fold_in(rng, 2), amount)]


def deal_out(stream_key, own, number, rows, amount, top, most, skew):
    order = jax.random.permutation(stream_key, amount)
    crowded, usual = load_shares(amount, rows * top, most, skew, True), load_shares(amount, rows * top, most, skew, False)
    places = jnp.arange(amount)

    def named(tallies, turn):
        used = int((tallies > 0).sum())
        fixed = max(1, used // 4)
        passed = fixed + (places - fixed + turn * (used - fixed)) % max(1, amount - fixed)
        return jnp.zeros((amount,), jnp.int32).at[order[jnp.where(places < fixed, places, passed)]].set(jnp.asarray(tallies, jnp.int32))

    tallies = jnp.where(number % 4 == 0, named(crowded, number // 4), named(usual, number - number // 4 - 1))
    mixed = jax.random.permutation(jax.random.fold_in(own, 3), amount)
    donor, receiver = mixed[0:amount // 2 * 2:2], mixed[1:amount // 2 * 2:2]
    margin = jnp.minimum(tallies[donor] - 1, most - tallies[receiver]) // 2
    margin = jnp.where((donor == order[0]) | (receiver == order[0]) | (tallies[receiver] == 0), 0, jnp.maximum(margin, 0))
    passed = jax.random.randint(jax.random.fold_in(own, 4), (amount // 2,), 0, 1 << 20) % (margin + 1)
    tallies = tallies.at[donor].add(-passed).at[receiver].add(passed)
    labels = jnp.searchsorted(jnp.cumsum(tallies), jnp.arange(rows * top), side="right").astype(jnp.int32)
    listing = labels.reshape(top, rows).T
    listing = listing[jax.random.permutation(jax.random.fold_in(own, 1), rows)]
    turn = jax.random.randint(jax.random.fold_in(own, 2), (rows, 1), 0, top)
    return jnp.take_along_axis(listing, (jnp.arange(top)[None, :] + turn) % top, axis=1)


def load_shares(count, total, most, skew, full):
    weights = [(1 << 20) // math.isqrt(grade ** skew) + 1 for grade in range(1, count + 1)]
    largest = most if full else min(most, max(-(-total // count), total * weights[0] // sum(weights)))
    least = 1 if total - largest >= count - 1 else 0
    holding, spare = [largest] + [least] * (count - 1), total - largest - least * (count - 1)
    while spare > 0:
        movable = [i for i in range(1, count) if holding[i] < largest] or [i for i in range(1, count) if holding[i] < most]
        whole, remaining = sum([weights[i] for i in movable]), spare
        for i in movable:
            extra = min(most - holding[i], max(1, remaining * weights[i] // whole), spare)
            holding[i] = holding[i] + extra
            spare = spare - extra
    return np.array(holding)


def normal_values(own_key, dims, scale, reach, cuts=(), kind=jnp.bfloat16):
    entries = jax.random.normal(own_key, dims, jnp.float32) * scale
    if len(cuts) > 0:
        entries = block_levels(own_key, dims, cuts, -0.22, 0.18) * entries
    return jnp.clip(entries, min=-reach, max=reach).astype(kind)


def setup_inputs(seed: int = 0) -> dict:
    key_of = jax.random.split(jax.random.key(seed), 20)
    tokens = normal_values(key_of[0], (TOKENS, D), 1.0, 6.0, ((0, 64),))
    grad_out = normal_values(key_of[1], (TOKENS, D), 1.0, 6.0, ((0, 64),))
    doc_ids = jax.vmap(lambda own: jnp.searchsorted(jnp.cumsum(uneven_parts(own, DOCS, GROUP, DOC_MOST, 2)), jnp.arange(GROUP), side="right"))(jax.random.split(key_of[2], GROUPS)).reshape((GROUPS, GROUP)).astype(jnp.int32)
    piece_starts = draw_piece_starts(jax.random.fold_in(key_of[19], 71), 0)
    piece_ends = draw_piece_ends(jax.random.fold_in(key_of[19], 71), 0)
    routes_keys = jax.random.split(jax.random.fold_in(key_of[5], 1), TOKENS // ROWS)
    routes_turns = jax.random.permutation(jax.random.fold_in(key_of[5], 3), TOKENS // ROWS)
    routes = jax.vmap(lambda own, number: deal_out(jax.random.fold_in(key_of[5], 2), own, number, ROWS, EXPERTS, TOPK, CAPACITY, 0))(routes_keys, routes_turns).reshape((TOKENS, TOPK))
    norm1_gain = jnp.clip(1.0 + 0.1 * jax.random.normal(key_of[6], (D,), jnp.float32), 0.5, 1.5)
    norm2_gain = jnp.clip(1.0 + 0.1 * jax.random.normal(key_of[7], (D,), jnp.float32), 0.5, 1.5)
    query_weight = normal_values(key_of[8], (D, HEADS * HEAD_DIM), D ** -0.5, 0.15625, ((1, 2),))
    key_weight = normal_values(key_of[9], (D, HEADS * HEAD_DIM), D ** -0.5, 0.15625, ((1, 2),))
    value_weight = normal_values(key_of[10], (D, HEADS * HEAD_DIM), D ** -0.5, 0.15625, ((1, 2),))
    output_weight = normal_values(key_of[11], (HEADS * HEAD_DIM, D), 16 ** -0.5, 1.5, ((0, 2),))
    router_weight = normal_values(key_of[12], (D, EXPERTS), 0.014, 0.079589844)
    shared_gate = normal_values(key_of[13], (D, FF), D ** -0.5, 0.15625, ((1, 2),))
    shared_up = normal_values(key_of[14], (D, FF), D ** -0.5, 0.15625, ((1, 2),))
    shared_down = normal_values(key_of[15], (FF, D), (FF // 4) ** -0.5, 0.375, ((0, 2),))
    expert_gate = normal_values(key_of[16], (SLOTS, D, FF), D ** -0.5, 0.15625, ((0, 16), (2, 2)))
    expert_up = normal_values(key_of[17], (SLOTS, D, FF), D ** -0.5, 0.15625, ((0, 16), (2, 2)))
    expert_down = normal_values(key_of[18], (SLOTS, FF, D), (FF // 16) ** -0.5, 0.75, ((0, 16), (1, 2)))
    return dict(tokens=tokens, grad_out=grad_out, doc_ids=doc_ids, piece_starts=piece_starts, piece_ends=piece_ends, routes=routes, norm1_gain=norm1_gain, norm2_gain=norm2_gain, query_weight=query_weight, key_weight=key_weight, value_weight=value_weight, output_weight=output_weight, router_weight=router_weight, shared_gate=shared_gate, shared_up=shared_up, shared_down=shared_down, expert_gate=expert_gate, expert_up=expert_up, expert_down=expert_down)


EPSILON = 1e-06
NEG_FILL = -1e+30
BASE = 10000.0
HIGH = lax.Precision.HIGHEST

@jax.custom_vjp
def low(v):
    return lax.optimization_barrier(v.astype(jnp.bfloat16)).astype(jnp.float32)

@jax.custom_vjp
def low_back(v):
    return v

def low_keep(v):
    return (low(v), None)

def low_pass(kept, grad):
    return (grad,)

def back_keep(v):
    return (v, None)

def back_low(kept, grad):
    return (low(grad),)
low.defvjp(low_keep, low_pass)
low_back.defvjp(back_keep, back_low)

def rotation_tables(positions, width):
    half = width // 2
    frequency = BASE ** (-(jnp.arange(half, dtype=jnp.float32) * 2.0) / width)
    angles = positions.astype(jnp.float32)[:, None] * frequency[None, :]
    return (jnp.cos(angles)[:, None, :], jnp.sin(angles)[:, None, :])

def rotate(values, cosine, sine):
    half = values.shape[-1] // 2
    first = values[..., :half]
    second = values[..., half:]
    return jnp.concatenate([first * cosine - second * sine, first * sine + second * cosine], axis=-1)

def rms_unit(values):
    return values * lax.rsqrt(lax.optimization_barrier(jnp.mean(values * values, axis=-1, keepdims=True)) + EPSILON)

def attention_mask(query_pos, key_pos, query_doc, key_doc, starts, ends):
    same_doc = query_doc[:, None] == key_doc[None, :]
    causal = key_pos[None, :] <= query_pos[:, None]
    query_in = ((query_pos[:, None] >= starts[None, :]) & (query_pos[:, None] < ends[None, :])).astype(jnp.float32)
    key_in = ((key_pos[:, None] >= starts[None, :]) & (key_pos[:, None] < ends[None, :])).astype(jnp.float32)
    together = jnp.dot(query_in, key_in.T, precision=HIGH) > 0.5
    return same_doc & (causal | together)

def group_attention(operands):
    query, keys, values, docs, starts, ends = operands
    block = math.gcd(512, GROUP)
    positions = jnp.arange(GROUP, dtype=jnp.int32)
    scale = HEAD_DIM ** (-0.5)

    def one_block(index):
        first = index * block
        query_block = lax.dynamic_slice_in_dim(query, first, block, 0)
        query_pos = lax.dynamic_slice_in_dim(positions, first, block, 0)
        query_doc = lax.dynamic_slice_in_dim(docs, first, block, 0)
        raw = low_back(jnp.einsum('qhd,khd->hqk', query_block, keys, precision=HIGH))
        visible = attention_mask(query_pos, positions, query_doc, docs, starts, ends)
        weights = low(jax.nn.softmax(jnp.where(visible[None], raw * scale, NEG_FILL), axis=-1))
        return low_back(low(jnp.einsum('hqk,khd->qhd', weights, values, precision=HIGH)))
    blocks = lax.map(jax.checkpoint(one_block), jnp.arange(GROUP // block, dtype=jnp.int32))
    return blocks.reshape(GROUP, HEADS, HEAD_DIM)

def reference(tokens, grad_out, doc_ids, piece_starts, piece_ends, routes, norm1_gain, norm2_gain, query_weight, key_weight, value_weight, output_weight, router_weight, shared_gate, shared_up, shared_down, expert_gate, expert_up, expert_down):

    def forward(inputs, gain_one, gain_two, w_query, w_key, w_value, w_output, w_router, w_shared_gate, w_shared_up, w_shared_down, w_expert_gate, w_expert_up, w_expert_down):
        normed_one = low(rms_unit(inputs) * gain_one)
        positions = jnp.arange(TOKENS, dtype=jnp.int32) % GROUP
        cosine, sine = rotation_tables(positions, HEAD_DIM)
        query_pre = low_back(jnp.dot(normed_one, w_query, precision=HIGH)).reshape(TOKENS, HEADS, HEAD_DIM)
        key_pre = low_back(jnp.dot(normed_one, w_key, precision=HIGH)).reshape(TOKENS, HEADS, HEAD_DIM)
        query = low(rotate(query_pre, cosine, sine))
        keys = low(rotate(key_pre, cosine, sine))
        values = low(low_back(jnp.dot(normed_one, w_value, precision=HIGH))).reshape(TOKENS, HEADS, HEAD_DIM)
        grouped = (query.reshape(GROUPS, GROUP, HEADS, HEAD_DIM), keys.reshape(GROUPS, GROUP, HEADS, HEAD_DIM), values.reshape(GROUPS, GROUP, HEADS, HEAD_DIM), doc_ids, piece_starts, piece_ends)
        attended = lax.map(group_attention, grouped).reshape(TOKENS, HEADS * HEAD_DIM)
        residual = inputs + low_back(jnp.dot(attended, w_output, precision=HIGH))
        normed_two = low(rms_unit(residual) * gain_two)
        logits = low_back(jnp.dot(normed_two, w_router, precision=HIGH))
        route_hot = (routes[:, :, None] == jnp.arange(EXPERTS, dtype=jnp.int32)[None, None, :]).astype(jnp.float32)
        gates = jax.nn.softmax(lax.optimization_barrier(jnp.sum(route_hot * logits[:, None, :], axis=2)), axis=1)
        shared_gate_pre = low_back(jnp.dot(normed_two, w_shared_gate, precision=HIGH))
        shared_up_pre = low_back(jnp.dot(normed_two, w_shared_up, precision=HIGH))
        shared_hidden = low(jax.nn.silu(shared_gate_pre) * shared_up_pre)
        shared_out = low_back(jnp.dot(shared_hidden, w_shared_down, precision=HIGH))
        half = FF // N_TP

        def routed_block(operands):
            normed, block_routes, block_gates = operands
            flat_routes = block_routes.reshape(ROWS * TOPK)
            slot_hot = (flat_routes[:, None] == jnp.arange(SLOTS, dtype=jnp.int32)[None, :]).astype(jnp.int32)
            slot_index = lax.optimization_barrier(jnp.sum(slot_hot * jnp.cumsum(slot_hot, axis=0), axis=1)) - 1
            position = flat_routes * CAPACITY + slot_index
            assigned = ROWS * TOPK
            owner = jnp.full((SLOTS * CAPACITY,), assigned, jnp.int32).at[position].set(jnp.arange(assigned, dtype=jnp.int32))
            padded = jnp.concatenate([normed, jnp.zeros((1, D), jnp.float32)], axis=0)
            buffer = padded[owner // TOPK].reshape(SLOTS, CAPACITY, D)
            result = jnp.zeros((SLOTS, CAPACITY, D), jnp.float32)
            for group in range(N_TP):
                rows_in = low_back(buffer)
                gate_pre = low_back(jnp.einsum('scd,sdf->scf', rows_in, w_expert_gate[:, :, group * half:(group + 1) * half], precision=HIGH))
                up_pre = low_back(jnp.einsum('scd,sdf->scf', rows_in, w_expert_up[:, :, group * half:(group + 1) * half], precision=HIGH))
                hidden = low(jax.nn.silu(gate_pre) * up_pre)
                result = result + low(jnp.einsum('scf,sfd->scd', hidden, w_expert_down[:, group * half:(group + 1) * half, :], precision=HIGH))
            result = low_back(result)
            picked = result.reshape(SLOTS * CAPACITY, D)[position].reshape(ROWS, TOPK, D)
            return lax.optimization_barrier(jnp.sum(block_gates[:, :, None] * picked, axis=1))
        count = TOKENS // ROWS
        routed = lax.map(jax.checkpoint(routed_block), (normed_two.reshape(count, ROWS, D), routes.reshape(count, ROWS, TOPK), gates.reshape(count, ROWS, TOPK)))
        return residual + shared_out + routed.reshape(TOKENS, D)
    result, pullback = jax.vjp(forward, tokens.astype(jnp.float32), norm1_gain, norm2_gain, query_weight.astype(jnp.float32), key_weight.astype(jnp.float32), value_weight.astype(jnp.float32), output_weight.astype(jnp.float32), router_weight.astype(jnp.float32), shared_gate.astype(jnp.float32), shared_up.astype(jnp.float32), shared_down.astype(jnp.float32), expert_gate.astype(jnp.float32), expert_up.astype(jnp.float32), expert_down.astype(jnp.float32))
    grads = pullback(grad_out.astype(jnp.float32))
    return (result.astype(jnp.bfloat16), grads[0], grads[1], grads[2], grads[3], grads[4], grads[5], grads[6], grads[7], grads[8], grads[9], grads[10], grads[11], grads[12], grads[13])
```

```python
import jax
import jax.numpy as jnp
from jax import lax
from jax.experimental import pallas as pl
from jax.experimental.pallas import tpu as pltpu
from jax.sharding import Mesh, PartitionSpec as P

F32 = jnp.float32
BF16 = jnp.bfloat16
HEAD_DIM = 128
TOPK = 7
EPSILON = 1e-06
NEG_FILL = -1e30
BASE = 10000.0
SCALE = HEAD_DIM ** (-0.5)

T = 128
D = 1280
HEADS = 5
HW = HEADS * HEAD_DIM
FF = 448
E = 4
CAP = 16
BLOCKS = 16
KEYS = 1280
EXTRA = 128

EP = ("yl", "z", "c")
VMEM = pl.BlockSpec(memory_space=pltpu.VMEM)
SMEM = pl.BlockSpec(memory_space=pltpu.SMEM)
ANY = pl.BlockSpec(memory_space=pl.ANY)


def params(mib, **more):
    return pltpu.CompilerParams(vmem_limit_bytes=mib << 20, **more)


def cost(flops, moved):
    return pl.CostEstimate(flops=int(flops), bytes_accessed=int(moved), transcendentals=0)


def dot(a, b):
    return lax.dot_general(a, b, (((1,), (0,)), ((), ())), preferred_element_type=F32)


def dot_nt(a, b):
    return lax.dot_general(a, b, (((1,), (1,)), ((), ())), preferred_element_type=F32)


def dot_tn(a, b):
    return lax.dot_general(a, b, (((0,), (0,)), ((), ())), preferred_element_type=F32)


def split3(v):
    first = v.astype(BF16)
    rest = v - first.astype(F32)
    second = rest.astype(BF16)
    return first, second, (rest - second.astype(F32)).astype(BF16)


def lanes(shape):
    return lax.broadcasted_iota(jnp.int32, shape, 1)


def rows(shape):
    return lax.broadcasted_iota(jnp.int32, shape, 0)


def turn(values, cosine, sine):
    parts = []
    for h in range(HEADS):
        z = values[:, h * 128 : (h + 1) * 128]
        parts.append(z * cosine + pltpu.roll(z, 64, 1) * sine)
    return jnp.concatenate(parts, axis=1)


def per_token(columns):
    lane = lanes((T, EXTRA))
    out = jnp.zeros((T, EXTRA), F32)
    for j, column in enumerate(columns):
        out = jnp.where(lane == j, column.astype(F32), out)
    return out.astype(BF16)


def project_kernel(x_ref, g_ref, wq_ref, wk_ref, wv_ref, cos_ref, sin_ref, routes_ref, dy_ref, h1_ref, q_ref, kv_ref, dyp_ref, hot_ref):
    x = x_ref[...].astype(F32)
    inverse = lax.rsqrt(jnp.mean(x * x, axis=1, keepdims=True) + EPSILON)
    h1 = (x * inverse * g_ref[...]).astype(BF16)
    h1_ref[...] = h1
    cosine, sine = cos_ref[...], sin_ref[...]
    kv_ref[:, :HW] = turn(dot(h1, wk_ref[...]), cosine, sine).astype(BF16)
    kv_ref[:, HW:] = dot(h1, wv_ref[...]).astype(BF16)
    q_ref[...] = turn(dot(h1, wq_ref[...]), cosine, sine).astype(BF16)
    lane = lanes((T, EXTRA))
    routes = routes_ref[...]
    hot = jnp.zeros((T, EXTRA), F32)
    for j in range(TOPK):
        hot = jnp.where(lane == routes[:, j : j + 1], 1.0, hot)
    hot_ref[...] = hot
    before = (lanes((T, T)) < rows((T, T))).astype(BF16)
    slot = dot(before, hot.astype(BF16))
    dyp_ref[:, :D] = dy_ref[...]
    dyp_ref[:, D:] = jnp.where(hot > 0.5, slot, -1.0).astype(BF16)


def project(x, gain, wq, wk, wv, cosine, sine, routes, dy):
    return pl.pallas_call(
        project_kernel,
        out_shape=(
            jax.ShapeDtypeStruct((T, D), BF16),
            jax.ShapeDtypeStruct((T, HW), BF16),
            jax.ShapeDtypeStruct((T, 2 * HW), BF16),
            jax.ShapeDtypeStruct((T, D + EXTRA), BF16),
            jax.ShapeDtypeStruct((T, EXTRA), F32),
        ),
        in_specs=[VMEM] * 9,
        out_specs=(VMEM,) * 5,
        compiler_params=params(24),
        cost_estimate=cost(2 * T * D * 3 * HW, 6e6),
        name="project",
    )(x, gain, wq, wk, wv, cosine, sine, routes, dy)


def attend_kernel(at_ref, q_ref, kv_hbm, bias_ref, wo_ref, o_ref, part_ref, qp_ref, kvs, sem):
    start = pl.multiple_of(at_ref[0], 128)
    copy = pltpu.make_async_copy(kv_hbm.at[pl.ds(start, KEYS), :], kvs, sem)
    copy.start()
    copy.wait()
    stats, outs = [], []
    for h in range(HEADS):
        q = q_ref[:, h * 128 : (h + 1) * 128]
        s = dot_nt(q, kvs[:, h * 128 : (h + 1) * 128]) * SCALE + bias_ref[...]
        high = jnp.max(s, axis=1, keepdims=True)
        e = jnp.exp(s - high)
        total = jnp.sum(e, axis=1, keepdims=True)
        p = (e * (1.0 / total)).astype(BF16)
        outs.append(dot(p, kvs[:, HW + h * 128 : HW + (h + 1) * 128]))
        stats += list(split3((high + jnp.log(total)) * (-1.0 / SCALE)))
    o = jnp.concatenate(outs, axis=1)
    o_ref[...] = o
    part_ref[...] = dot(o.astype(BF16), wo_ref[...]).astype(BF16)
    qp_ref[:, :HW] = q_ref[...]
    qp_ref[:, HW:] = per_token(stats)


def attend(at, q, kv_all, bias, wo):
    return pl.pallas_call(
        attend_kernel,
        out_shape=(
            jax.ShapeDtypeStruct((T, HW), F32),
            jax.ShapeDtypeStruct((T, D), BF16),
            jax.ShapeDtypeStruct((T, HW + EXTRA), BF16),
        ),
        in_specs=[SMEM, VMEM, ANY, VMEM, VMEM],
        out_specs=(VMEM,) * 3,
        scratch_shapes=[pltpu.VMEM((KEYS, 2 * HW), BF16), pltpu.SemaphoreType.DMA],
        compiler_params=params(32),
        cost_estimate=cost(4 * T * KEYS * HW + 2 * T * HW * D, 6e6),
        name="attend",
    )(at, q, kv_all, bias, wo)


def gate_kernel(x_ref, a_ref, b_ref, g_ref, wr_ref, hot_ref, r_ref, h2p_ref, gates_ref):
    r = x_ref[...].astype(F32) + (a_ref[...].astype(F32) + b_ref[...].astype(F32))
    r_ref[...] = r
    inverse = lax.rsqrt(jnp.mean(r * r, axis=1, keepdims=True) + EPSILON)
    h2 = (r * inverse * g_ref[...]).astype(BF16)
    hot = hot_ref[...] > 0.5
    logits = jnp.where(hot, dot(h2, wr_ref[...]), NEG_FILL)
    e = jnp.where(hot, jnp.exp(logits - jnp.max(logits, axis=1, keepdims=True)), 0.0)
    gates = e / jnp.sum(e, axis=1, keepdims=True)
    gates_ref[...] = gates
    first = gates.astype(BF16).astype(F32)
    h2p_ref[:, :D] = h2
    h2p_ref[:, D:] = (first + pltpu.roll(gates - first, 64, 1)).astype(BF16)


def gate(x, a, b, gain, wr, hot):
    return pl.pallas_call(
        gate_kernel,
        out_shape=(
            jax.ShapeDtypeStruct((T, D), F32),
            jax.ShapeDtypeStruct((T, D + EXTRA), BF16),
            jax.ShapeDtypeStruct((T, EXTRA), F32),
        ),
        in_specs=[VMEM] * 6,
        out_specs=(VMEM,) * 3,
        compiler_params=params(16),
        cost_estimate=cost(2 * T * D * 128, 2e6),
        name="gate",
    )(x, a, b, gain, wr, hot)


def silu_parts(gate_pre):
    sigmoid = 1.0 / (1.0 + jnp.exp(-gate_pre))
    return gate_pre * sigmoid, sigmoid * (1.0 + gate_pre * (1.0 - sigmoid))


def shared_kernel(h2p_ref, dy_ref, wg_ref, wu_ref, wd_ref, out_ref, dh_ref, sh_ref, dsg_ref, dsu_ref):
    h2 = h2p_ref[:, :D]
    sg = dot(h2, wg_ref[...])
    su = dot(h2, wu_ref[...])
    act, slope = silu_parts(sg)
    sh = (act * su).astype(BF16)
    sh_ref[...] = sh
    out_ref[...] = dot(sh, wd_ref[...])
    dsh = dot_nt(dy_ref[...], wd_ref[...])
    dsg = (dsh * su * slope).astype(BF16)
    dsu = (dsh * act).astype(BF16)
    dsg_ref[...] = dsg
    dsu_ref[...] = dsu
    dh_ref[...] = dot_nt(dsg, wg_ref[...]) + dot_nt(dsu, wu_ref[...])


def shared(h2p, dy, wg, wu, wd):
    hidden = jax.ShapeDtypeStruct((T, FF), BF16)
    return pl.pallas_call(
        shared_kernel,
        out_shape=(jax.ShapeDtypeStruct((T, D), F32), jax.ShapeDtypeStruct((T, D), F32), hidden, hidden, hidden),
        in_specs=[VMEM] * 5,
        out_specs=(VMEM,) * 5,
        compiler_params=params(24),
        cost_estimate=cost(12 * T * D * FF, 5e6),
        name="shared",
    )(h2p, dy, wg, wu, wd)


def block_of(rank, entry, other):
    yl, z, c = rank // 8, (rank // 2) % 4, rank % 2
    dz = (0, 3, 1, 2)[entry % 4]
    return (((yl + entry // 4) % 2) * 4 + (z + dz) % 4) * 2 + (c + other) % 2


def experts_kernel(
    rank_ref, h2_ref, dy_ref, wg_ref, wu_ref, wd_ref,
    xb_ref, dyo_ref, eh_ref, dgu_ref, own_ref, oth_ref, yown_ref, yoth_ref,
    pt, xs, dys, gs, ys, dbs,
):
    e = pl.program_id(0)
    rank = rank_ref[0]

    @pl.when(e == 0)
    def _():
        spread = (rows((EXTRA, E * CAP)) == rank * E + lanes((EXTRA, E * CAP)) // CAP).astype(BF16)
        place = (lanes((T, E * CAP)) % CAP).astype(F32)
        named = rank * E + rows((E * CAP, EXTRA)) // CAP
        column = lanes((E * CAP, EXTRA))
        mine = (column == named) | (column == named + 64)

        def one(k, carry):
            at = pl.ds(pl.multiple_of(k * T, T), T)
            slot = dot(dy_ref[at, D:], spread)
            hot = (slot == place).astype(BF16)
            pt[k] = hot
            x = dot_tn(hot, h2_ref[at, :])
            dy = dot_tn(hot, dy_ref[at, :D]).astype(BF16)
            g = jnp.sum(jnp.where(mine, x[:, D:], 0.0), axis=1, keepdims=True)
            g = jnp.broadcast_to(g, (E * CAP, 128))
            x = x[:, :D].astype(BF16)
            for i in range(E):
                to = pl.ds(pl.multiple_of(k * CAP, CAP), CAP)
                xs[i, to, :] = x[i * CAP : (i + 1) * CAP]
                dys[i, to, :] = dy[i * CAP : (i + 1) * CAP]
                gs[i, to, :] = g[i * CAP : (i + 1) * CAP]
            return carry

        lax.fori_loop(0, BLOCKS, one, 0)

    x = xs[e]
    eg = dot(x, wg_ref[0])
    eu = dot(x, wu_ref[0])
    act, slope = silu_parts(eg)
    eh = (act * eu).astype(BF16)
    y = dot(eh, wd_ref[0]).astype(BF16).astype(F32)
    g = gs[e][:, :1]
    dy = dys[e].astype(F32)
    dgate = jnp.sum(dy * y, axis=1, keepdims=True)
    ys[e] = (g * y).astype(BF16)
    dyg = (g * dy).astype(BF16)
    deh = dot_nt(dyg, wd_ref[0])
    deg = (deh * eu * slope).astype(BF16)
    deu = (deh * act).astype(BF16)
    db = dot_nt(deg, wg_ref[0]) + dot_nt(deu, wu_ref[0])
    dbs[e, :, :D] = db.astype(BF16)
    column = lanes((BLOCKS * CAP, EXTRA))
    first = dgate.astype(BF16).astype(F32)
    own_column = rank * E + e
    placed = jnp.where(column == own_column, first, jnp.where(column == own_column + 64, dgate - first, 0.0))
    dbs[e, :, D:] = placed.astype(BF16)
    xb_ref[0] = x
    dyo_ref[0] = dyg
    dgu_ref[0] = jnp.concatenate([deg, deu], axis=1)
    none = jnp.zeros((BLOCKS * CAP, FF), BF16)

    @pl.when(e % 2 == 0)
    def _():
        eh_ref[0] = jnp.concatenate([eh, none], axis=1)

    @pl.when(e % 2 == 1)
    def _():
        eh_ref[0] = jnp.concatenate([none, eh], axis=1)

    @pl.when(e == E - 1)
    def _():
        for other, to, yto in ((0, own_ref, yown_ref), (1, oth_ref, yoth_ref)):
            for j in range(8):
                k = block_of(rank, j, other)
                hot = pt[k]
                at = pl.ds(pl.multiple_of(k * CAP, CAP), CAP)
                to[j] = dot(hot, jnp.concatenate([dbs[i, at, :] for i in range(E)], axis=0)).astype(BF16)
                yto[j] = dot(hot, jnp.concatenate([ys[i, at, :] for i in range(E)], axis=0)).astype(BF16)


def experts(rank, h2_all, dy_all, wg, wu, wd):
    n = BLOCKS * CAP
    per = lambda shape: pl.BlockSpec((1, *shape), lambda e: (e, 0, 0))
    whole = lambda shape: pl.BlockSpec(shape, lambda e: (0,) * len(shape), pipeline_mode=pl.Buffered(1))
    return pl.pallas_call(
        experts_kernel,
        out_shape=(
            jax.ShapeDtypeStruct((E, n, D), BF16),
            jax.ShapeDtypeStruct((E, n, D), BF16),
            jax.ShapeDtypeStruct((E, n, 2 * FF), BF16),
            jax.ShapeDtypeStruct((E, n, 2 * FF), BF16),
            jax.ShapeDtypeStruct((8, T, D + EXTRA), BF16),
            jax.ShapeDtypeStruct((8, T, D + EXTRA), BF16),
            jax.ShapeDtypeStruct((8, T, D), BF16),
            jax.ShapeDtypeStruct((8, T, D), BF16),
        ),
        grid=(E,),
        in_specs=[
            SMEM,
            whole((BLOCKS * T, D + EXTRA)),
            whole((BLOCKS * T, D + EXTRA)),
            per((D, FF)),
            per((D, FF)),
            per((FF, D)),
        ],
        out_specs=(
            per((n, D)), per((n, D)), per((n, 2 * FF)), per((n, 2 * FF)),
            whole((8, T, D + EXTRA)), whole((8, T, D + EXTRA)), whole((8, T, D)), whole((8, T, D)),
        ),
        scratch_shapes=[
            pltpu.VMEM((BLOCKS, T, E * CAP), BF16),
            pltpu.VMEM((E, n, D), BF16),
            pltpu.VMEM((E, n, D), BF16),
            pltpu.VMEM((E, n, 128), F32),
            pltpu.VMEM((E, n, D), BF16),
            pltpu.VMEM((E, n, D + EXTRA), BF16),
        ],
        compiler_params=params(58, dimension_semantics=("arbitrary",)),
        cost_estimate=cost(2 * E * n * D * FF * 7, 5e7),
        name="experts",
    )(rank, h2_all, dy_all, wg, wu, wd)


def expert_grads_kernel(x_ref, dy_ref, eh_ref, dgu_ref, gu_ref, down_ref):
    gu_ref[:, : 2 * FF] = dot_tn(x_ref[0], dgu_ref[0]).astype(BF16)
    gu_ref[:, 2 * FF :] = dot_tn(x_ref[1], dgu_ref[1]).astype(BF16)
    down_ref[...] = (dot_tn(dy_ref[0], eh_ref[0]) + dot_tn(dy_ref[1], eh_ref[1])).astype(BF16)


def expert_grads(x, dy, eh, dgu):
    n = BLOCKS * CAP
    per = lambda width: pl.BlockSpec((2, n, width), lambda p: (p, 0, 0))
    return pl.pallas_call(
        expert_grads_kernel,
        out_shape=(
            jax.ShapeDtypeStruct((D, E * 2 * FF), BF16),
            jax.ShapeDtypeStruct((D, E * FF), BF16),
        ),
        grid=(E // 2,),
        in_specs=[per(D), per(D), per(2 * FF), per(2 * FF)],
        out_specs=(
            pl.BlockSpec((D, 4 * FF), lambda p: (0, p)),
            pl.BlockSpec((D, 2 * FF), lambda p: (0, p)),
        ),
        compiler_params=params(56, dimension_semantics=("arbitrary",)),
        cost_estimate=cost(2 * E * n * D * FF * 3, 3e7),
        name="expert_grads",
    )(x, dy, eh, dgu)


def middle_kernel(a_ref, b_ref, r_ref, dy_ref, h2p_ref, gates_ref, g_ref, wr_ref, wo_ref, o_ref, dr_ref, da_ref, dop_ref, dlog_ref, gain_ref):
    both = a_ref[...].astype(F32) + b_ref[...].astype(F32)
    gates = gates_ref[...]
    dgate = both[:, D:] + pltpu.roll(both[:, D:], 64, 1)
    dsel = gates * (dgate - jnp.sum(gates * dgate, axis=1, keepdims=True))
    dlog = dsel.astype(BF16)
    dlog_ref[...] = dlog
    dh2 = both[:, :D] + dot_nt(dlog, wr_ref[...])
    r = r_ref[...]
    inverse = lax.rsqrt(jnp.mean(r * r, axis=1, keepdims=True) + EPSILON)
    unit = r * inverse
    gain_ref[...] = (dh2 * unit).astype(BF16)
    e2 = dh2 * g_ref[...]
    dr = dy_ref[...].astype(F32) + inverse * (e2 - unit * jnp.mean(e2 * unit, axis=1, keepdims=True))
    dr_ref[...] = dr
    da = dr.astype(BF16)
    da_ref[...] = da
    do = dot_nt(da, wo_ref[...]).astype(BF16)
    dop_ref[:, :HW] = do
    stats = []
    both = do.astype(F32) * o_ref[...]
    for h in range(HEADS):
        stats += list(split3(-jnp.sum(both[:, h * 128 : (h + 1) * 128], axis=1, keepdims=True)))
    dop_ref[:, HW:] = per_token(stats)


def middle(a, b, r, dy, h2p, gates, gain, wr, wo, o):
    return pl.pallas_call(
        middle_kernel,
        out_shape=(
            jax.ShapeDtypeStruct((T, D), F32),
            jax.ShapeDtypeStruct((T, D), BF16),
            jax.ShapeDtypeStruct((T, HW + EXTRA), BF16),
            jax.ShapeDtypeStruct((T, EXTRA), BF16),
            jax.ShapeDtypeStruct((T, D), BF16),
        ),
        in_specs=[VMEM] * 10,
        out_specs=(VMEM,) * 5,
        compiler_params=params(24),
        cost_estimate=cost(2 * T * D * (HW + 128), 5e6),
        name="middle",
    )(a, b, r, dy, h2p, gates, gain, wr, wo, o)


def attend_back_kernel(
    at_ref, qp_ref, kv_ref, dop_ref, kv_hbm, q_hbm, do_hbm, qbias_ref, kbias_ref, cos_ref, sin_ref, wq_ref, wk_ref, wv_ref,
    dqkv_ref, part_ref, kvs, qs, dos, sems,
):
    keys_at = pl.multiple_of(at_ref[0], 128)
    queries_at = pl.multiple_of(at_ref[1], 128)
    copies = [
        pltpu.make_async_copy(kv_hbm.at[pl.ds(keys_at, KEYS), :], kvs, sems.at[0]),
        pltpu.make_async_copy(q_hbm.at[pl.ds(queries_at, KEYS), :], qs, sems.at[1]),
        pltpu.make_async_copy(do_hbm.at[pl.ds(queries_at, KEYS), :], dos, sems.at[2]),
    ]
    for copy in copies:
        copy.start()
    for copy in copies:
        copy.wait()
    lane = lanes((T, EXTRA))
    q_extra = qp_ref[:, HW:].astype(F32)
    do_extra = dop_ref[:, HW:].astype(F32)
    dqs, dks, dvs = [], [], []
    for h in range(HEADS):
        cut = slice(h * 128, (h + 1) * 128)
        vcut = slice(HW + h * 128, HW + (h + 1) * 128)
        mine = (lane >= 3 * h) & (lane < 3 * h + 3)
        less = jnp.sum(jnp.where(mine, q_extra, 0.0), axis=1, keepdims=True)
        less_dot = jnp.sum(jnp.where(mine, do_extra, 0.0), axis=1, keepdims=True)
        p = jnp.exp((dot_nt(qp_ref[:, cut], kvs[:, cut]) + less) * SCALE + qbias_ref[...])
        dp = dot_nt(dop_ref[:, cut], kvs[:, vcut]) + less_dot
        ds = (p * dp * SCALE).astype(BF16)
        dqs.append(dot(ds, kvs[:, cut]))
        ones = mine.astype(BF16)
        k_wide = jnp.concatenate([kv_ref[:, cut], ones], axis=1)
        v_wide = jnp.concatenate([kv_ref[:, vcut], ones], axis=1)
        q_wide = jnp.concatenate([qs[:, cut], qs[:, HW:]], axis=1)
        do_wide = jnp.concatenate([dos[:, cut], dos[:, HW:]], axis=1)
        pt = jnp.exp(dot_nt(k_wide, q_wide) * SCALE + kbias_ref[...])
        dst = (pt * dot_nt(v_wide, do_wide) * SCALE).astype(BF16)
        dks.append(dot(dst, qs[:, cut]))
        dvs.append(dot(pt.astype(BF16), dos[:, cut]))
    cosine, sine = cos_ref[...], -sin_ref[...]
    dq = turn(jnp.concatenate(dqs, axis=1), cosine, sine).astype(BF16)
    dk = turn(jnp.concatenate(dks, axis=1), cosine, sine).astype(BF16)
    dv = jnp.concatenate(dvs, axis=1).astype(BF16)
    dqkv_ref[:, :HW] = dq
    dqkv_ref[:, HW : 2 * HW] = dk
    dqkv_ref[:, 2 * HW :] = dv
    part_ref[...] = (dot_nt(dq, wq_ref[...]) + dot_nt(dk, wk_ref[...]) + dot_nt(dv, wv_ref[...])).astype(BF16)


def attend_back(at, qp, kv, dop, kv_all, q_all, do_all, qbias, kbias, cosine, sine, wq, wk, wv):
    return pl.pallas_call(
        attend_back_kernel,
        out_shape=(jax.ShapeDtypeStruct((T, 3 * HW), BF16), jax.ShapeDtypeStruct((T, D), BF16)),
        in_specs=[SMEM, VMEM, VMEM, VMEM, ANY, ANY, ANY] + [VMEM] * 7,
        out_specs=(VMEM,) * 2,
        scratch_shapes=[
            pltpu.VMEM((KEYS, 2 * HW), BF16),
            pltpu.VMEM((KEYS, HW + EXTRA), BF16),
            pltpu.VMEM((KEYS, HW + EXTRA), BF16),
            pltpu.SemaphoreType.DMA((3,)),
        ],
        compiler_params=params(48),
        cost_estimate=cost(16 * T * KEYS * HW + 6 * T * HW * D, 2e7),
        name="attend_back",
    )(at, qp, kv, dop, kv_all, q_all, do_all, qbias, kbias, cosine, sine, wq, wk, wv)


def ep_perm(dyl, dz, dc):
    at = lambda yl, z, c: (yl * 4 + z) * 2 + c
    return [
        (at(yl, z, c), at(yl ^ dyl, (z + dz) % 4, c ^ dc)) for yl in range(2) for z in range(4) for c in range(2)
    ]


Z_UP, Z_DOWN, ACROSS, CORE = ep_perm(0, 1, 0), ep_perm(0, 3, 0), ep_perm(1, 0, 0), ep_perm(0, 0, 1)


def send(value, perm):
    return lax.ppermute(value, EP, perm)


def swap(value, axis):
    return lax.ppermute(value, axis, [(0, 1), (1, 0)])


def scatter_sum(own, oth):
    n, width = own.shape[1], own.shape[2]
    a, b = n * 3 // 8, n * 6 // 8
    wide = lambda v: v.astype(F32)
    none = lambda m: jnp.zeros((m, width), F32)
    t = wide(own) + wide(send(oth, CORE))
    far = t[7].astype(BF16)
    t1, t2, t3 = send(far[:a], ACROSS), send(far[a:b], Z_DOWN), send(far[b:], Z_UP)
    s3 = (t[3] + jnp.concatenate([wide(t1), none(n - a)], 0)).astype(BF16)
    s5 = (t[5] + jnp.concatenate([none(a), wide(t2), none(n - b)], 0)).astype(BF16)
    s6 = (t[6] + jnp.concatenate([none(b), wide(t3)], 0)).astype(BF16)
    u1, u2, u3 = send(s3, Z_DOWN), send(s6, Z_UP), send(s5, ACROSS)
    s1 = (t[1] + wide(u1) + wide(u3)).astype(BF16)
    s4 = (t[4] + wide(u2)).astype(BF16)
    v1, v2, v4 = send(s1, Z_DOWN), send(t[2].astype(BF16), Z_UP), send(s4, ACROSS)
    return t[0] + wide(v1) + wide(v2) + wide(v4)


def dense_sum(left, right, core):
    half = right.shape[1] // 2
    order = jnp.arange(D, dtype=jnp.int32).reshape(4, 2, 4, 40).transpose(2, 0, 1, 3).reshape(D)
    place = (jnp.arange(D, dtype=jnp.int32)[:, None] == order[None, :]).astype(BF16)
    left = jnp.dot(left, place, preferred_element_type=F32).astype(BF16)
    mine = jnp.where(core == 0, right[:, :half], right[:, half:])
    theirs = jnp.where(core == 0, right[:, half:], right[:, :half])
    out = lambda r: dot_tn(left, r).astype(BF16)
    both = (out(mine).astype(F32) + swap(out(theirs), "c").astype(F32)).astype(BF16)
    part = lax.psum_scatter(both, "z", scatter_dimension=0, tiled=True)
    parts = lax.all_to_all(part.reshape(8, 40, half), ("x", "yl"), split_axis=0, concat_axis=0, tiled=True)
    total = jnp.sum(parts.astype(F32), axis=0)
    first, second = total[:20], total[20:]
    keep = jnp.where(core == 0, first, second)
    got = swap(jnp.where(core == 0, second, first), "c")
    return jnp.concatenate([jnp.where(core == 0, keep, got), jnp.where(core == 0, got, keep)], axis=1)


def rotation(positions):
    half = HEAD_DIM // 2
    frequency = BASE ** (-(jnp.arange(half, dtype=F32) * 2.0) / HEAD_DIM)
    angles = positions.astype(F32)[:, None] * frequency[None, :]
    cosine, sine = jnp.cos(angles), jnp.sin(angles)
    return jnp.concatenate([cosine, cosine], axis=1), jnp.concatenate([-sine, sine], axis=1)


def mask_bias(query_pos, key_pos, query_doc, key_doc, starts, ends):
    visible = key_pos <= query_pos
    for j in range(starts.shape[0]):
        visible |= (query_pos >= starts[j]) & (query_pos < ends[j]) & (key_pos >= starts[j]) & (key_pos < ends[j])
    return jnp.where(visible & (query_doc == key_doc), 0.0, NEG_FILL).astype(F32)


def local(
    tokens, grad_out, doc_ids, piece_starts, piece_ends, routes, norm1_gain, norm2_gain, query_weight, key_weight, value_weight,
    output_weight, router_weight, shared_gate, shared_up, shared_down, expert_gate, expert_up, expert_down,
):
    core = lax.axis_index("c")
    rank = lax.axis_index(EP).astype(jnp.int32)
    group = lambda v: lax.all_gather(v, EP, axis=0, tiled=True)
    gain1, gain2 = norm1_gain[None, :], norm2_gain[None, :]
    wr = jnp.pad(router_weight, ((0, 0), (0, EXTRA - router_weight.shape[1])))
    own_pos = rank * T + jnp.arange(T, dtype=jnp.int32)
    cosine, sine = rotation(own_pos)
    keys_at = jnp.where(rank < 10, 0, 768).astype(jnp.int32)
    queries_at = jnp.where(rank < 6, 0, 768).astype(jnp.int32)
    at = jnp.stack([keys_at, queries_at])
    docs, starts, ends = doc_ids[0], piece_starts[0], piece_ends[0]
    own_doc = lax.dynamic_slice_in_dim(docs, rank * T, T)
    key_pos = keys_at + jnp.arange(KEYS, dtype=jnp.int32)
    query_pos = queries_at + jnp.arange(KEYS, dtype=jnp.int32)
    key_doc = lax.dynamic_slice_in_dim(docs, keys_at, KEYS)
    query_doc = lax.dynamic_slice_in_dim(docs, queries_at, KEYS)
    qbias = mask_bias(own_pos[:, None], key_pos[None, :], own_doc[:, None], key_doc[None, :], starts, ends)
    kbias = mask_bias(query_pos[None, :], own_pos[:, None], query_doc[None, :], own_doc[:, None], starts, ends)

    h1, q, kv, dyp, hot = project(
        tokens, gain1, query_weight, key_weight, value_weight, cosine, sine, routes, grad_out
    )
    kv_all = group(kv)
    dy_all = group(dyp)
    o, part, qp = attend(at, q, kv_all, qbias, output_weight)
    r, h2p, gates = gate(tokens, part, swap(part, "yh"), gain2, wr, hot)
    h2_all = group(h2p)
    q_all = group(qp)
    shared_out, shared_dh, sh, dsg, dsu = shared(h2p, grad_out, shared_gate, shared_up, shared_down)
    xb, dyg, eh, dgu, own, oth, yown, yoth = experts(
        rank[None], h2_all, dy_all, expert_gate, expert_up, expert_down
    )
    back = scatter_sum(own, oth)
    gu, down = expert_grads(xb, dyg, eh, dgu)
    gu = lax.psum_scatter(gu, "x", scatter_dimension=0, tiled=True)
    down = lax.psum_scatter(down, "x", scatter_dimension=0, tiled=True)
    back = jnp.concatenate([back[:, :D] + shared_dh, back[:, D:]], axis=1).astype(BF16)
    dr, da, dop, dlog, gain2_terms = middle(
        back, swap(back, "yh"), r, grad_out, h2p, gates, gain2, wr, output_weight, o
    )
    do_all = group(dop)
    mixed = (scatter_sum(yown, yoth) + shared_out).astype(BF16)
    output = (r + (mixed.astype(F32) + swap(mixed, "yh").astype(F32))).astype(BF16)

    put = lambda v, before, width: jnp.pad(v, ((0, 0), (before, width - before - v.shape[1])))
    one = jnp.ones((T, 1), BF16)
    left = jnp.concatenate([da, h2p[:, :D], grad_out, gain2_terms], axis=0)
    width = HW + 3 * FF + 64
    right = jnp.concatenate(
        [
            put(o.astype(BF16), 0, width),
            put(jnp.concatenate([dsg, dsu, jnp.zeros((T, FF), BF16), dlog[:, :63]], axis=1), HW, width),
            put(sh, HW + 2 * FF, width),
            put(one, width - 1, width),
        ],
        axis=0,
    )
    first = dense_sum(left, right, core)

    dqkv, dh1_part = attend_back(
        at, qp, kv, dop, kv_all, q_all, do_all, qbias, kbias, cosine, sine, query_weight, key_weight, value_weight
    )
    dh1 = dh1_part.astype(F32) + swap(dh1_part, "yh").astype(F32)
    x = tokens.astype(F32)
    inverse = lax.rsqrt(jnp.mean(x * x, axis=1, keepdims=True) + EPSILON)
    unit = x * inverse
    e1 = dh1 * gain1
    grad_tokens = dr + inverse * (e1 - unit * jnp.mean(e1 * unit, axis=1, keepdims=True))
    left = jnp.concatenate([h1, (dh1 * unit).astype(BF16)], axis=0)
    width = 3 * HW + 128
    right = jnp.concatenate([put(dqkv, 0, width), put(one, 3 * HW, width)], axis=0)
    second = dense_sum(left, right, core)

    o_at, s_at = 0, HW
    gu = gu.reshape(D // 4, E, 2, FF).astype(F32)
    return (
        output,
        grad_tokens,
        second[:, 3 * HW],
        first[:, HW + 3 * FF + 63],
        second[:, :HW],
        second[:, HW : 2 * HW],
        second[:, 2 * HW : 3 * HW],
        first[:, o_at : o_at + HW].T,
        first[:, HW + 3 * FF : HW + 3 * FF + 63],
        first[:, s_at : s_at + FF],
        first[:, s_at + FF : s_at + 2 * FF],
        first[:, s_at + 2 * FF : s_at + 3 * FF].T,
        gu[:, :, 0].transpose(1, 0, 2),
        gu[:, :, 1].transpose(1, 0, 2),
        down.reshape(D // 4, E, FF).astype(F32).transpose(1, 2, 0),
    )


def solution(mesh):
    fine = Mesh(mesh.devices.reshape(4, 2, 4, 2, 2), ("x", "yl", "z", "c", "yh"))
    rows64 = ("x", "yl", "z", "c")
    in_specs = (
        P(rows64, None),
        P(rows64, None),
        P("x", None),
        P("x", None),
        P("x", None),
        P(rows64, None),
        P(),
        P(),
        P(None, "yh"),
        P(None, "yh"),
        P(None, "yh"),
        P("yh", None),
        P(),
        P(None, "yh"),
        P(None, "yh"),
        P("yh", None),
        P(EP, None, "yh"),
        P(EP, None, "yh"),
        P(EP, "yh", None),
    )
    out_specs = (
        P(rows64, None),
        P(rows64, None),
        P(rows64),
        P(rows64),
        P(rows64, "yh"),
        P(rows64, "yh"),
        P(rows64, "yh"),
        P("yh", rows64),
        P(rows64, None),
        P(rows64, "yh"),
        P(rows64, "yh"),
        P("yh", rows64),
        P(EP, "x", "yh"),
        P(EP, "x", "yh"),
        P(EP, "yh", "x"),
    )
    return jax.shard_map(local, mesh=fine, in_specs=in_specs, out_specs=out_specs, check_vma=False)
```

```python
import jax
import jax.numpy as jnp
from jax import lax
from jax.experimental import pallas as pl
from jax.experimental.pallas import tpu as pltpu
from jax.sharding import Mesh, PartitionSpec as P

F32 = jnp.float32
BF16 = jnp.bfloat16
HEAD_DIM = 128
TOPK = 7
EPSILON = 1e-06
NEG_FILL = -1e30
BASE = 10000.0
SCALE = HEAD_DIM ** (-0.5)

T = 128
D = 1280
HEADS = 5
HW = HEADS * HEAD_DIM
FF = 448
E = 4
CAP = 16
BLOCKS = 16
KEYS = 1280
COUNT = BLOCKS * E * CAP
EXTRA = 128

EP = ("yl", "z", "c")
VMEM = pl.BlockSpec(memory_space=pltpu.VMEM)
SMEM = pl.BlockSpec(memory_space=pltpu.SMEM)
ANY = pl.BlockSpec(memory_space=pl.ANY)


def params(mib, **more):
    return pltpu.CompilerParams(vmem_limit_bytes=mib << 20, **more)


def cost(flops, moved):
    return pl.CostEstimate(flops=int(flops), bytes_accessed=int(moved), transcendentals=0)


def dot(a, b):
    return lax.dot_general(a, b, (((1,), (0,)), ((), ())), preferred_element_type=F32)


def dot_nt(a, b):
    return lax.dot_general(a, b, (((1,), (1,)), ((), ())), preferred_element_type=F32)


def dot_tn(a, b):
    return lax.dot_general(a, b, (((0,), (0,)), ((), ())), preferred_element_type=F32)


def split3(v):
    first = v.astype(BF16)
    rest = v - first.astype(F32)
    second = rest.astype(BF16)
    return first, second, (rest - second.astype(F32)).astype(BF16)


def lanes(shape):
    return lax.broadcasted_iota(jnp.int32, shape, 1)


def rows(shape):
    return lax.broadcasted_iota(jnp.int32, shape, 0)


def turn(values, cosine, sine):
    parts = []
    for h in range(HEADS):
        z = values[:, h * 128 : (h + 1) * 128]
        parts.append(z * cosine + pltpu.roll(z, 64, 1) * sine)
    return jnp.concatenate(parts, axis=1)


def per_token(columns):
    lane = lanes((T, EXTRA))
    out = jnp.zeros((T, EXTRA), F32)
    for j, column in enumerate(columns):
        if column is not None:
            out = jnp.where(lane == j, column.astype(F32), out)
    return out.astype(BF16)


def project_kernel(x_ref, g_ref, wq_hbm, wk_hbm, wv_hbm, cos_ref, sin_ref, h1_ref, kv_ref, q_ref, wq, wk, wv, sems):
    copies = [pltpu.make_async_copy(a, b, sems.at[i]) for i, (a, b) in enumerate(((wk_hbm, wk), (wv_hbm, wv), (wq_hbm, wq)))]
    for copy in copies:
        copy.start()
    x = x_ref[...].astype(F32)
    inverse = lax.rsqrt(jnp.mean(x * x, axis=1, keepdims=True) + EPSILON)
    h1 = (x * inverse * g_ref[...][None, :]).astype(BF16)
    h1_ref[...] = h1
    cosine, sine = cos_ref[...], sin_ref[...]
    copies[0].wait()
    kv_ref[:, :HW] = turn(dot(h1, wk[...]), cosine, sine).astype(BF16)
    copies[1].wait()
    kv_ref[:, HW:] = dot(h1, wv[...]).astype(BF16)
    copies[2].wait()
    q_ref[...] = turn(dot(h1, wq[...]), cosine, sine).astype(BF16)


def project(x, gain, wq, wk, wv, cosine, sine):
    weight = pltpu.VMEM((D, HW), BF16)
    return pl.pallas_call(
        project_kernel,
        out_shape=(
            jax.ShapeDtypeStruct((T, D), BF16),
            jax.ShapeDtypeStruct((T, 2 * HW), BF16),
            jax.ShapeDtypeStruct((T, HW), BF16),
        ),
        in_specs=[VMEM, VMEM, ANY, ANY, ANY, VMEM, VMEM],
        out_specs=(VMEM,) * 3,
        scratch_shapes=[weight, weight, weight, pltpu.SemaphoreType.DMA((3,))],
        compiler_params=params(60),
        cost_estimate=cost(2 * T * D * 3 * HW, 6e6),
        name="project",
    )(x, gain, wq, wk, wv, cosine, sine)


def slots_kernel(routes_ref, dy_ref, dyp_ref, hot_ref, place_ref):
    expert = rows((EXTRA, T))
    routes = routes_ref[...]
    hot = jnp.zeros((EXTRA, T), F32)
    for j in range(TOPK):
        hot = jnp.where(expert == routes[j : j + 1, :], 1.0, hot)
    hot = hot.astype(BF16)
    same = (rows((T, T)) == lanes((T, T))).astype(BF16)
    hot = dot_tn(hot, same)
    hot_ref[...] = hot
    before = (lanes((T, T)) < rows((T, T))).astype(BF16)
    slot = dot(before, hot.astype(BF16))
    slot = jnp.where(hot > 0.5, slot, -1.0).astype(BF16)
    dyp_ref[:, :D] = dy_ref[...]
    dyp_ref[:, D:] = slot
    at = lanes((EXTRA, COUNT))
    spread = (rows((EXTRA, COUNT)) == (at >> 4)).astype(BF16)
    place = dot(slot, spread) == (lanes((T, COUNT)) & (CAP - 1)).astype(F32)
    place_ref[...] = jnp.where(place, 1.0, 0.0).astype(BF16)


def slots(routes, dy):
    return pl.pallas_call(
        slots_kernel,
        out_shape=(
            jax.ShapeDtypeStruct((T, D + EXTRA), BF16),
            jax.ShapeDtypeStruct((T, EXTRA), F32),
            jax.ShapeDtypeStruct((T, COUNT), BF16),
        ),
        in_specs=[VMEM] * 2,
        out_specs=(VMEM,) * 3,
        compiler_params=params(12),
        cost_estimate=cost(2 * T * T * COUNT, 1e6),
        name="slots",
    )(routes, dy)


def masks_kernel(info_ref, docs_ref, qbias_ref, kbias_ref):
    chip, core = info_ref[0], info_ref[1]
    border = jnp.sum(jnp.where(docs_ref[...] == 0, 1.0, 0.0), axis=1, keepdims=True).astype(jnp.int32)
    lane = lanes((1, KEYS))
    own = chip * 2 * T + core * T + rows((T, 1))

    def bias(query, key, there):
        seen = key <= query
        for j in range(2):
            first, last = info_ref[3 + j], info_ref[5 + j]
            seen |= (query >= first) & (query < last) & (key >= first) & (key < last)
        same = (query >= border) == (key >= border)
        return jnp.where(seen & same & there, 0.0, NEG_FILL).astype(F32)

    qbias_ref[...] = bias(own, info_ref[2] + lane, lane >= 0)
    other = (lane >= KEYS // 2).astype(jnp.int32)
    step = (lane - other * (KEYS // 2)) >> 7
    query = (chip + step) * 2 * T + (core ^ other) * T + (lane & (T - 1))
    kbias_ref[...] = bias(query, own, query < BLOCKS * T)


def masks(info, docs):
    bias = jax.ShapeDtypeStruct((T, KEYS), F32)
    return pl.pallas_call(
        masks_kernel,
        out_shape=(bias, bias),
        in_specs=[SMEM, VMEM],
        out_specs=(VMEM,) * 2,
        compiler_params=params(12),
        cost_estimate=cost(40 * T * KEYS, 2e6),
        name="masks",
    )(info, docs)


WINDOW = 10


def attend_kernel(at_ref, q_ref, kv_hbm, bias_ref, wo_ref, o_ref, part_ref, stats_ref, kvs, sems):
    start = pl.multiple_of(at_ref[0], T)
    copies = []
    for i in range(2):
        cut = pl.ds(i * HW, HW)
        copies.append(pltpu.make_async_copy(kv_hbm.at[pl.ds(start, KEYS), cut], kvs.at[:, cut], sems.at[i]))
        copies[i].start()
    copies[0].wait()
    copies[1].wait()
    stats, outs = [], []
    for h in range(HEADS):
        cut = slice(h * 128, (h + 1) * 128)
        vcut = slice(HW + h * 128, HW + (h + 1) * 128)
        q = q_ref[:, cut]
        s = dot_nt(q, kvs[:, cut]) * SCALE + bias_ref[...]
        high = jnp.max(s, axis=1, keepdims=True)
        e = jnp.exp(s - high)
        total = jnp.sum(e, axis=1, keepdims=True)
        p = (e * (1.0 / total)).astype(BF16)
        outs.append(dot(p, kvs[:, vcut]))
        stats += list(split3((high + jnp.log(total)) * (-1.0 / SCALE)))
    o = jnp.concatenate(outs, axis=1)
    o_ref[...] = o
    part_ref[...] = dot(o.astype(BF16), wo_ref[...]).astype(BF16)
    stats_ref[...] = per_token([None] * (3 * HEADS) + stats)


def attend(at, q, kv_all, bias, wo):
    return pl.pallas_call(
        attend_kernel,
        out_shape=(
            jax.ShapeDtypeStruct((T, HW), F32),
            jax.ShapeDtypeStruct((T, D), BF16),
            jax.ShapeDtypeStruct((T, EXTRA), BF16),
        ),
        in_specs=[SMEM, VMEM, ANY, VMEM, VMEM],
        out_specs=(VMEM,) * 3,
        scratch_shapes=[pltpu.VMEM((KEYS, 2 * HW), BF16), pltpu.SemaphoreType.DMA((2,))],
        compiler_params=params(60),
        cost_estimate=cost(4 * T * KEYS * HW + 2 * T * HW * D, 6e6),
        name="attend",
    )(at, q, kv_all, bias, wo)


def gate_kernel(x_ref, a_ref, b_ref, g_ref, wr_ref, hot_ref, r_ref, h2p_ref, gates_ref):
    r = x_ref[...].astype(F32) + (a_ref[...].astype(F32) + b_ref[...].astype(F32))
    r_ref[...] = r
    inverse = lax.rsqrt(jnp.mean(r * r, axis=1, keepdims=True) + EPSILON)
    h2 = (r * inverse * g_ref[...]).astype(BF16)
    hot = hot_ref[...] > 0.5
    logits = jnp.where(hot, dot_nt(h2, wr_ref[...]), NEG_FILL)
    e = jnp.where(hot, jnp.exp(logits - jnp.max(logits, axis=1, keepdims=True)), 0.0)
    gates = e / jnp.sum(e, axis=1, keepdims=True)
    gates_ref[...] = gates
    first = gates.astype(BF16).astype(F32)
    h2p_ref[:, :D] = h2
    h2p_ref[:, D:] = (first + pltpu.roll(gates - first, 64, 1)).astype(BF16)


def gate(x, a, b, gain, wr, hot):
    return pl.pallas_call(
        gate_kernel,
        out_shape=(
            jax.ShapeDtypeStruct((T, D), F32),
            jax.ShapeDtypeStruct((T, D + EXTRA), BF16),
            jax.ShapeDtypeStruct((T, EXTRA), F32),
        ),
        in_specs=[VMEM] * 6,
        out_specs=(VMEM,) * 3,
        compiler_params=params(24),
        cost_estimate=cost(2 * T * D * 128, 2e6),
        name="gate",
    )(x, a, b, gain, wr, hot)


def silu_parts(gate_pre):
    sigmoid = 1.0 / (1.0 + jnp.exp(-gate_pre))
    return gate_pre * sigmoid, sigmoid * (1.0 + gate_pre * (1.0 - sigmoid))


def shared_kernel(h2p_ref, dy_ref, wg_ref, wu_ref, wd_ref, out_ref, dh_ref, sh_ref, dsg_ref, dsu_ref):
    h2 = h2p_ref[:, :D]
    sg = dot_nt(h2, wg_ref[...])
    su = dot_nt(h2, wu_ref[...])
    act, slope = silu_parts(sg)
    sh = (act * su).astype(BF16)
    sh_ref[...] = sh
    out_ref[...] = dot(sh, wd_ref[...])
    dsh = dot_nt(dy_ref[...], wd_ref[...])
    dsg = (dsh * su * slope).astype(BF16)
    dsu = (dsh * act).astype(BF16)
    dsg_ref[...] = dsg
    dsu_ref[...] = dsu
    dh_ref[...] = dot(dsg, wg_ref[...]) + dot(dsu, wu_ref[...])


def shared(h2p, dy, wg, wu, wd):
    hidden = jax.ShapeDtypeStruct((T, FF), BF16)
    return pl.pallas_call(
        shared_kernel,
        out_shape=(jax.ShapeDtypeStruct((T, D), F32), jax.ShapeDtypeStruct((T, D), F32), hidden, hidden, hidden),
        in_specs=[VMEM] * 5,
        out_specs=(VMEM,) * 5,
        compiler_params=params(24),
        cost_estimate=cost(1e6, 1e5),
        name="shared",
    )(h2p, dy, wg, wu, wd)


PAIR = 2 * E * CAP


def dispatch_kernel(rank_ref, dy_ref, hot_ref, out_ref):
    rank = rank_ref[0]
    spread = (rows((EXTRA, PAIR)) == rank * E + ((lanes((EXTRA, PAIR)) & (E * CAP - 1)) >> 4)).astype(BF16)
    place = (lanes((2 * T, PAIR)) & (CAP - 1)).astype(F32)
    own = (lanes((2 * T, PAIR)) >= E * CAP) == (rows((2 * T, PAIR)) >= T)
    for k in range(2):
        at = slice(k * 2 * T, (k + 1) * 2 * T)
        hot = jnp.where(own & (dot(dy_ref[at, D:], spread) == place), 1.0, 0.0).astype(BF16)
        hot_ref[at, :] = hot
        dy = dot_tn(hot, dy_ref[at, :D]).astype(BF16)
        for j in range(2):
            to = slice((k * 2 + j) * CAP, (k * 2 + j + 1) * CAP)
            for i in range(E):
                out_ref[i, to, :] = dy[(j * E + i) * CAP : (j * E + i + 1) * CAP]


def dispatch(rank, dy_all):
    return pl.pallas_call(
        dispatch_kernel,
        out_shape=(
            jax.ShapeDtypeStruct((BLOCKS * T, PAIR), BF16),
            jax.ShapeDtypeStruct((E, BLOCKS * CAP, D), BF16),
        ),
        grid=(BLOCKS // 4,),
        in_specs=[SMEM, pl.BlockSpec((4 * T, D + EXTRA), lambda k: (k, 0))],
        out_specs=(pl.BlockSpec((4 * T, PAIR), lambda k: (k, 0)), pl.BlockSpec((E, 4 * CAP, D), lambda k: (0, k, 0))),
        compiler_params=params(60, dimension_semantics=("arbitrary",)),
        cost_estimate=cost(2 * BLOCKS * T * PAIR * D, 1e7),
        name="dispatch",
    )(rank, dy_all)


def experts_kernel(rank_ref, hot_ref, dy_ref, h2_hbm, wg_ref, wu_ref, wd_ref, out_ref, grads_hbm, h2s, xs, dys, gs, ehs, stage, sems, outs):
    e = pl.program_id(0)
    rank = rank_ref[0]
    slot = e & 1

    def result(slot, group):
        to = pl.ds(pl.multiple_of(group * 2 * FF, 128), 2 * FF)
        return pltpu.make_async_copy(stage.at[slot], grads_hbm.at[:, to], outs.at[slot])

    @pl.when(e == 0)
    def _():
        copies = []
        for k in range(0, BLOCKS, 2):
            at = pl.ds(k * T, 2 * T)
            copies.append(pltpu.make_async_copy(h2_hbm.at[at, :], h2s.at[at, :], sems.at[k // 2]))
        for copy in copies:
            copy.start()
        named = rank * E + ((rows((PAIR, EXTRA)) & (E * CAP - 1)) >> 4)
        column = lanes((PAIR, EXTRA))
        mine = (column == named) | (column == named + 64)
        for k in range(0, BLOCKS, 2):
            at = slice(k * T, (k + 2) * T)
            copies[k // 2].wait()
            x = dot_tn(hot_ref[at, :], h2s[at, :])
            g = jnp.sum(jnp.where(mine, x[:, D:], 0.0), axis=1, keepdims=True)
            g = jnp.broadcast_to(g, (PAIR, 128))
            x = x[:, :D].astype(BF16)
            for j in range(2):
                to = slice((k + j) * CAP, (k + j + 1) * CAP)
                for i in range(E):
                    cut = slice((j * E + i) * CAP, (j * E + i + 1) * CAP)
                    xs[i, to, :] = x[cut]
                    gs[i, to, :] = g[cut]

    x = xs[e]
    g = gs[e][:, :1]
    eg = dot_nt(x, wg_ref[0])
    eu = dot_nt(x, wu_ref[0])
    act, slope = silu_parts(eg)
    eh = (act * eu).astype(BF16)
    y = dot(eh, wd_ref[0]).astype(BF16).astype(F32)
    dyg = (g * dy_ref[0].astype(F32)).astype(BF16)
    deh = dot_nt(dy_ref[0], wd_ref[0])
    dgate = jnp.sum(eh.astype(F32) * deh, axis=1, keepdims=True)
    deh = g * deh
    deg = (deh * eu * slope).astype(BF16)
    deu = (deh * act).astype(BF16)
    db = (dot(deg, wg_ref[0]) + dot(deu, wu_ref[0])).astype(BF16)
    column = lanes((BLOCKS * CAP, EXTRA))
    expert = rank * E + e
    first = dgate.astype(BF16).astype(F32)
    placed = jnp.where(column == expert, first, jnp.where(column == expert + 64, dgate - first, 0.0)).astype(BF16)
    gy = (g * y).astype(BF16)
    at = pl.ds(pl.multiple_of(e * CAP, CAP), CAP)
    for k in range(BLOCKS):
        cut = slice(k * CAP, (k + 1) * CAP)
        out_ref[k, at, :D] = db[cut]
        out_ref[k, at, D : D + EXTRA] = placed[cut]
        out_ref[k, at, D + EXTRA :] = gy[cut]

    @pl.when(e >= 2)
    def _():
        result(slot, e - 2).wait()

    dgu = jnp.concatenate([deg, deu], axis=1)
    for r in range(0, D, 256):
        stage[slot, r : r + 256, :] = dot_tn(x[:, r : r + 256], dgu).astype(BF16)
    result(slot, e).start()
    none = jnp.zeros((BLOCKS * CAP, FF), BF16)

    @pl.when(slot == 0)
    def _():
        dys[...] = dyg
        ehs[...] = jnp.concatenate([eh, none], axis=1)

    @pl.when(slot == 1)
    def _():
        wide = jnp.concatenate([none, eh], axis=1)

        @pl.when(e == E - 1)
        def _():
            result(2, E).wait()

        for r in range(0, D, 256):
            both = dot_tn(dys[:, r : r + 256], ehs[...]) + dot_tn(dyg[:, r : r + 256], wide)
            stage[2, r : r + 256, :] = both.astype(BF16)
        result(2, E + (e >> 1)).start()

    @pl.when(e == E - 1)
    def _():
        result(0, E - 2).wait()
        result(1, E - 1).wait()
        result(2, E + 1).wait()


GRADS = 6
BACK = D + EXTRA + D


def experts(rank, hot, dy, h2_all, wg, wu, wd):
    n = BLOCKS * CAP
    per = lambda shape: pl.BlockSpec((1, *shape), lambda e: (e, 0, 0))
    held = lambda shape: pl.BlockSpec(shape, lambda e: (0,) * len(shape), pipeline_mode=pl.Buffered(1))
    return pl.pallas_call(
        experts_kernel,
        out_shape=(
            jax.ShapeDtypeStruct((BLOCKS, E * CAP, BACK), BF16),
            jax.ShapeDtypeStruct((D, GRADS * 2 * FF), BF16),
        ),
        grid=(E,),
        in_specs=[SMEM, held((BLOCKS * T, PAIR)), per((n, D)), ANY, per((FF, D)), per((FF, D)), per((FF, D))],
        out_specs=(held((BLOCKS, E * CAP, BACK)), ANY),
        scratch_shapes=[
            pltpu.VMEM((BLOCKS * T, D + EXTRA), BF16),
            pltpu.VMEM((E, n, D), BF16),
            pltpu.VMEM((n, D), BF16),
            pltpu.VMEM((E, n, 128), F32),
            pltpu.VMEM((n, 2 * FF), BF16),
            pltpu.VMEM((3, D, 2 * FF), BF16),
            pltpu.SemaphoreType.DMA((BLOCKS // 2,)),
            pltpu.SemaphoreType.DMA((3,)),
        ],
        compiler_params=params(58, dimension_semantics=("arbitrary",)),
        cost_estimate=cost(2 * E * n * D * FF * 9, 5e7),
        name="experts",
    )(rank, hot, dy, h2_all, wg, wu, wd)


def combine_kernel(place_ref, back_ref, dh_ref, out_ref, back_out_ref, mixed_ref):
    total = dot(place_ref[...], back_ref[...])
    back_out_ref[:, :D] = (total[:, :D] + dh_ref[...]).astype(BF16)
    back_out_ref[:, D:] = total[:, D : D + EXTRA].astype(BF16)
    mixed_ref[...] = (total[:, D + EXTRA :] + out_ref[...]).astype(BF16)


def combine(place, back, dh, out):
    return pl.pallas_call(
        combine_kernel,
        out_shape=(jax.ShapeDtypeStruct((T, D + EXTRA), BF16), jax.ShapeDtypeStruct((T, D), BF16)),
        in_specs=[VMEM] * 4,
        out_specs=(VMEM,) * 2,
        compiler_params=params(24),
        cost_estimate=cost(2 * T * COUNT * BACK, 7e6),
        name="combine",
    )(place, back.reshape(COUNT, BACK), dh, out)


def unpack_kernel(gu_ref, down_ref, gate_ref, up_ref, out_ref):
    gu = gu_ref[...].astype(F32)
    gate_ref[0] = gu[:, :FF]
    up_ref[0] = gu[:, FF:]
    down = down_ref[...].astype(F32)
    out_ref[0] = jnp.where((pl.program_id(0) & 1) == 1, down[:, FF:], down[:, :FF])


def unpack(grads):
    part = jax.ShapeDtypeStruct((E, D // 4, FF), F32)
    out = pl.BlockSpec((1, D // 4, FF), lambda e: (e, 0, 0))
    block = lambda at: pl.BlockSpec((D // 4, 2 * FF), at)
    return pl.pallas_call(
        unpack_kernel,
        out_shape=(part, part, part),
        grid=(E,),
        in_specs=[block(lambda e: (0, e)), block(lambda e: (0, E + e // 2))],
        out_specs=(out, out, out),
        compiler_params=params(60, dimension_semantics=("arbitrary",)),
        cost_estimate=cost(1e6, 1.2e7),
        name="unpack",
    )(grads, grads)


def middle_kernel(a_ref, b_ref, r_ref, dy_ref, h2p_ref, gates_ref, g_ref, wr_ref, wo_ref, o_ref, stats_ref, dr_ref, da_ref, dop_ref, dlog_ref, gain_ref):
    both = a_ref[...].astype(F32) + b_ref[...].astype(F32)
    gates = gates_ref[...]
    dgate = both[:, D:] + pltpu.roll(both[:, D:], 64, 1)
    dsel = gates * (dgate - jnp.sum(gates * dgate, axis=1, keepdims=True))
    dlog = dsel.astype(BF16)
    dlog_ref[...] = dlog
    dh2 = both[:, :D] + dot(dlog, wr_ref[...])
    r = r_ref[...]
    inverse = lax.rsqrt(jnp.mean(r * r, axis=1, keepdims=True) + EPSILON)
    unit = r * inverse
    gain_ref[...] = (dh2 * unit).astype(BF16)
    e2 = dh2 * g_ref[...]
    dr = dy_ref[...].astype(F32) + inverse * (e2 - unit * jnp.mean(e2 * unit, axis=1, keepdims=True))
    dr_ref[...] = dr
    da = dr.astype(BF16)
    da_ref[...] = da
    do = dot_nt(da, wo_ref[...]).astype(BF16)
    dop_ref[:, :HW] = do
    stats = []
    both = do.astype(F32) * o_ref[...]
    for h in range(HEADS):
        stats += list(split3(-jnp.sum(both[:, h * 128 : (h + 1) * 128], axis=1, keepdims=True)))
    dop_ref[:, HW:] = per_token(stats) + stats_ref[...]


def middle(a, b, r, dy, h2p, gates, gain, wr, wo, o, stats):
    return pl.pallas_call(
        middle_kernel,
        out_shape=(
            jax.ShapeDtypeStruct((T, D), F32),
            jax.ShapeDtypeStruct((T, D), BF16),
            jax.ShapeDtypeStruct((T, HW + EXTRA), BF16),
            jax.ShapeDtypeStruct((T, EXTRA), BF16),
            jax.ShapeDtypeStruct((T, D), BF16),
        ),
        in_specs=[VMEM] * 11,
        out_specs=(VMEM,) * 5,
        compiler_params=params(24),
        cost_estimate=cost(2 * T * D * (HW + 128), 5e6),
        name="middle",
    )(a, b, r, dy, h2p, gates, gain, wr, wo, o, stats)


HALF = 3 * HW // 2
PADDED = 1024


def attend_back_kernel(*refs):
    at_ref, kv_hbm, do_hbm, refs = refs[0], refs[1], refs[2 : 2 + WINDOW], refs[2 + WINDOW :]
    q_hbm, refs = refs[:WINDOW], refs[WINDOW:]
    w_hbm, refs = refs[:3], refs[3:]
    kv_ref, qbias_ref, kbias_ref, cos_ref, sin_ref, dqkv_ref, part_ref, kvs, qs, dos, ws, sems = refs
    keys_at = pl.ds(pl.multiple_of(at_ref[0], T), KEYS)
    copies = [pltpu.make_async_copy(v, dos.at[i], sems.at[i]) for i, v in enumerate(do_hbm)]
    copies += [pltpu.make_async_copy(v, qs.at[i], sems.at[WINDOW + i]) for i, v in enumerate(q_hbm)]
    copies += [pltpu.make_async_copy(v, ws.at[i], sems.at[2 * WINDOW + i]) for i, v in enumerate(w_hbm)]
    copies.append(pltpu.make_async_copy(kv_hbm.at[keys_at, :], kvs, sems.at[2 * WINDOW + 3]))
    early = [2 * WINDOW + 3, 0, WINDOW]
    late = [i for i in range(2 * WINDOW) if i not in early]
    weights = [2 * WINDOW, 2 * WINDOW + 1, 2 * WINDOW + 2]
    for i in early + late + weights:
        copies[i].start()
    for i in early:
        copies[i].wait()
    lane = lanes((T, EXTRA))
    extra = dos[0, :, HW:]
    stats = extra.astype(F32)
    side = lambda parts: jnp.concatenate(parts, axis=1)
    block = lambda v, i: v[:, i * T : (i + 1) * T]
    every = range(WINDOW)
    heads = [(slice(h * 128, (h + 1) * 128), slice(HW + h * 128, HW + (h + 1) * 128)) for h in range(HEADS)]
    its = lambda first: (lane >= first) & (lane < first + 3)
    dqs, dks, dvs = [], [], []
    for h, (cut, vcut) in enumerate(heads):
        less_dot = jnp.sum(jnp.where(its(3 * h), stats, 0.0), axis=1, keepdims=True)
        less = jnp.sum(jnp.where(its(3 * (HEADS + h)), stats, 0.0), axis=1, keepdims=True)
        q, do = qs[0, :, cut], dos[0, :, cut]
        p = jnp.exp((dot_nt(q, kvs[:, cut]) + less) * SCALE + qbias_ref[...])
        dp = dot_nt(do, kvs[:, vcut]) + less_dot
        ds = (p * dp * SCALE).astype(BF16)
        dqs.append(dot(ds, kvs[:, cut]))
    for i in late:
        copies[i].wait()
    for h, (cut, vcut) in enumerate(heads):
        k_wide = side([kv_ref[:, cut], its(3 * (HEADS + h)).astype(BF16)])
        v_wide = side([kv_ref[:, vcut], its(3 * h).astype(BF16)])
        pt = side([dot_nt(k_wide, side([qs[i, :, cut], dos[i, :, HW:]])) for i in every])
        pt = jnp.exp(pt * SCALE + kbias_ref[...])
        dpt = side([dot_nt(v_wide, side([dos[i, :, cut], dos[i, :, HW:]])) for i in every])
        dst = (pt * dpt * SCALE).astype(BF16)
        pt = pt.astype(BF16)
        dks.append(sum(dot(block(dst, i), qs[i, :, cut]) for i in every))
        dvs.append(sum(dot(block(pt, i), dos[i, :, cut]) for i in every))
    cosine, sine = cos_ref[...], -sin_ref[...]
    dq = turn(side(dqs), cosine, sine).astype(BF16)
    dk = turn(side(dks), cosine, sine).astype(BF16)
    dv = side(dvs).astype(BF16)
    dqkv = side([dq, dk, dv])
    none = jnp.zeros((T, PADDED - HALF), BF16)
    dqkv_ref[...] = side([dqkv[:, :HALF], none, dqkv[:, HALF:], none])
    for i in weights:
        copies[i].wait()
    part = dot_nt(dq, ws[0]) + dot_nt(dk, ws[1]) + dot_nt(dv, ws[2])
    part_ref[...] = part.astype(BF16)


def attend_back(at, qs, kv_all, dos, kv, qbias, kbias, cosine, sine, wq, wk, wv):
    return pl.pallas_call(
        attend_back_kernel,
        out_shape=(
            jax.ShapeDtypeStruct((T, 2 * PADDED), BF16),
            jax.ShapeDtypeStruct((T, D), BF16),
        ),
        in_specs=[SMEM] + [ANY] * (4 + 2 * WINDOW) + [VMEM] * 5,
        out_specs=(VMEM,) * 2,
        scratch_shapes=[
            pltpu.VMEM((KEYS, 2 * HW), BF16),
            pltpu.VMEM((WINDOW, T, HW), BF16),
            pltpu.VMEM((WINDOW, T, HW + EXTRA), BF16),
            pltpu.VMEM((3, D, HW), BF16),
            pltpu.SemaphoreType.DMA((2 * WINDOW + 4,)),
        ],
        compiler_params=params(56),
        cost_estimate=cost(16 * T * KEYS * HW + 6 * T * HW * D, 2e7),
        name="attend_back",
    )(at, kv_all, *dos, *qs, wq, wk, wv, kv, qbias, kbias, cosine, sine)


WIDE = 384


def chunks_kernel(h1_ref, out_ref):
    at = lanes((1, WIDE))
    part = jnp.zeros((1, WIDE), jnp.int32)
    for j in range(1, 8):
        part += (at >= 40 * j).astype(jnp.int32)
    for z in range(4):
        source = part * 160 + z * 40 + (at - part * 40)
        place = ((rows((D, WIDE)) == source) & (at < 320)).astype(BF16)
        out_ref[z] = dot(h1_ref[...], place).astype(BF16)


def chunks(h1):
    return pl.pallas_call(
        chunks_kernel,
        out_shape=jax.ShapeDtypeStruct((4, h1.shape[0], WIDE), BF16),
        in_specs=[VMEM],
        out_specs=VMEM,
        compiler_params=params(16),
        cost_estimate=cost(2 * h1.shape[0] * D * 4 * WIDE, 2e6),
        name="chunks",
    )(h1)


def projection_grads_kernel(left_ref, *refs):
    parts, out_ref = refs[:-1], refs[-1]
    right = jnp.concatenate([v[...] for v in parts], axis=0)
    out_ref[...] = dot_tn(left_ref[...], right)[:320].astype(BF16)


def projection_grads(left, parts):
    return pl.pallas_call(
        projection_grads_kernel,
        out_shape=jax.ShapeDtypeStruct((320, PADDED), BF16),
        in_specs=[VMEM] * (1 + len(parts)),
        out_specs=VMEM,
        compiler_params=params(24),
        cost_estimate=cost(2 * 8 * T * WIDE * PADDED, 4e6),
        name="projection_grads",
    )(left.reshape(8 * T, WIDE), *parts)


def ep_perm(dyl, dz, dc):
    at = lambda yl, z, c: (yl * 4 + z) * 2 + c
    return [
        (at(yl, z, c), at(yl ^ dyl, (z + dz) % 4, c ^ dc)) for yl in range(2) for z in range(4) for c in range(2)
    ]


CORE = ep_perm(0, 0, 1)


def send(value, perm):
    return lax.ppermute(value, EP, perm)


def swap(value, axis):
    return lax.ppermute(value, axis, [(0, 1), (1, 0)])


def to_owners(value):
    return lax.all_to_all(value, EP, split_axis=0, concat_axis=0, tiled=True)


def window_perm(step, back):
    pairs = [(i, i + step) for i in range(8 - step) if i + step < 5 or i >= 3]
    pairs = [(j, i) if back else (i, j) for i, j in pairs]
    return [(2 * i + c, 2 * j + c) for i, j in pairs for c in range(2)]


def window(value, back):
    own = [value] + [send(value, window_perm(step, back)) for step in range(1, 5)]
    return own


def with_other_core(own):
    return list(own) + [send(v, CORE) for v in own]


def both_cores(left):
    return jnp.concatenate([left, swap(left, "c")], axis=0)


def dense_right(right, core):
    half = right.shape[1] // 2
    mine = jnp.where(core == 0, right[:, :half], right[:, half:])
    theirs = jnp.where(core == 0, right[:, half:], right[:, :half])
    return both_cores_of(mine, theirs)


def both_cores_of(mine, theirs):
    return jnp.concatenate([mine, swap(theirs, "c")], axis=0)


def products(left, right):
    return dot_tn(left, right).astype(BF16).reshape(8, 4, 40, right.shape[1])


NEAR = [(0, 1), (1, 0), (2, 3), (3, 2)]
WRAP = [(0, 3), (3, 0), (1, 2), (2, 1)]


def z_sum_near(a, b, z):
    chunk = lambda v, i: lax.dynamic_slice_in_dim(v, i, 1, 1)
    near, wrap = z ^ 1, 3 - z
    far = 3 - near
    a1 = lax.ppermute(jnp.concatenate([chunk(a, near), chunk(a, far)], axis=1), "z", NEAR)
    b1 = lax.ppermute(jnp.concatenate([chunk(b, wrap), chunk(b, far)], axis=1), "z", WRAP)
    return a1, b1


def z_sum_far(a, b, a1, b1, z):
    wide = lambda v: v.astype(F32)
    low = lambda v: v.astype(BF16)
    chunk = lambda v, i: lax.dynamic_slice_in_dim(v, i, 1, 1)
    near, wrap = z ^ 1, 3 - z
    a2 = lax.ppermute(low(wide(chunk(a, wrap)) + wide(a1[:, 1:])), "z", WRAP)
    b2 = lax.ppermute(low(wide(chunk(b, near)) + wide(b1[:, 1:])), "z", NEAR)
    return (
        low(wide(chunk(a, z)) + wide(a1[:, :1]) + wide(a2)),
        low(wide(chunk(b, z)) + wide(b1[:, :1]) + wide(b2)),
    )


UP = [(0, 1), (1, 2), (2, 3), (3, 0)]
DOWN = [(1, 0), (2, 1), (3, 2), (0, 3)]


def z_gather_far(below, above):
    half = below.shape[0] // 2
    return lax.ppermute(below[:half], "z", UP), lax.ppermute(above[half:], "z", DOWN)


def xy_sum(part):
    parts = lax.all_to_all(part, ("x", "yl"), split_axis=0, concat_axis=0, tiled=True)
    return jnp.sum(parts.astype(F32), axis=0)


def core_rows(total, core):
    first, second = total[:20], total[20:]
    keep = jnp.where(core == 0, first, second)
    got = swap(jnp.where(core == 0, second, first), "c")
    return jnp.where(core == 0, keep, got), jnp.where(core == 0, got, keep)


def rotation(positions):
    half = HEAD_DIM // 2
    frequency = BASE ** (-(jnp.arange(half, dtype=F32) * 2.0) / HEAD_DIM)
    angles = positions.astype(F32)[:, None] * frequency[None, :]
    cosine, sine = jnp.cos(angles), jnp.sin(angles)
    return jnp.concatenate([cosine, cosine], axis=1), jnp.concatenate([-sine, sine], axis=1)


def after(values, ready):
    return lax.optimization_barrier((values, ready))


def local(
    tokens, grad_out, doc_ids, piece_starts, piece_ends, routes, norm1_gain, norm2_gain, query_weight, key_weight, value_weight,
    output_weight, router_weight, shared_gate, shared_up, shared_down, expert_gate, expert_up, expert_down,
):
    core, z = lax.axis_index("c"), lax.axis_index("z")
    rank = lax.axis_index(EP).astype(jnp.int32)
    gain1, gain2 = norm1_gain[None, :], norm2_gain[None, :]
    wr = jnp.pad(router_weight.T, ((0, EXTRA - router_weight.shape[1]), (0, 0)))
    cosine, sine = rotation(rank * T + jnp.arange(T, dtype=jnp.int32))
    keys_at = jnp.where(rank < 10, 0, 768).astype(jnp.int32)
    info = jnp.concatenate([jnp.stack([rank // 2, rank % 2, keys_at]), piece_starts[0], piece_ends[0]]).astype(jnp.int32)
    group = lambda v: lax.all_gather(v, EP, axis=0, tiled=True)

    h1, kv, q = project(tokens, norm1_gain, query_weight, key_weight, value_weight, cosine, sine)
    kv_all = group(kv)
    h1_left = lax.all_to_all(chunks(h1), "z", split_axis=0, concat_axis=0, tiled=True)
    h1_left = jnp.stack([h1_left, swap(h1_left, "c")], axis=1)
    pick = lambda i: lax.dynamic_slice_in_dim(h1_left, i % 4, 1, 0)
    h1_left = jnp.concatenate([pick(z), pick(z + 3), pick(z + 1), pick(z + 2)], axis=0)
    dyp, hot, place = slots(routes.T, grad_out)
    qbias, kbias = masks(info, doc_ids)
    (dyp, q, h1_left, qbias, kbias), kv_all = after((dyp, q, h1_left, qbias, kbias), kv_all)
    dy_all = group(dyp)
    o, part, stats = attend(keys_at[None], q, kv_all, qbias, output_weight)
    r, h2p, gates = gate(tokens, part, swap(part, "yh"), gain2, wr, hot)
    h2_all = group(h2p)
    shared_out, shared_dh, sh, dsg, dsu = shared(h2p, grad_out, shared_gate.T, shared_up.T, shared_down)
    places, dys = dispatch(rank[None], dy_all)

    put = lambda v, before, width: jnp.pad(v, ((0, 0), (before, width - before - v.shape[1])))
    both = 3 * FF // 2
    halves = lambda v, used, padded: jnp.concatenate([put(v[:, :used], 0, padded), put(v[:, used:], 0, padded)], axis=1)
    right = jnp.concatenate([put(jnp.concatenate([dsg, dsu], axis=1), 0, 3 * FF), put(sh, 2 * FF, 3 * FF)], axis=0)
    sums_a = products(
        both_cores(jnp.concatenate([h2p[:, :D], grad_out], axis=0)), dense_right(halves(right, both, 768), core)
    ).transpose(1, 0, 2, 3).reshape(D, 768)
    late_q, part = after(q, part)
    qs = window(late_q, True)
    (places, dys, qs, sums_a), h2_all = after((places, dys, qs, sums_a), h2_all)
    qs = with_other_core(qs)
    sums_a = lax.psum_scatter(sums_a, "z", scatter_dimension=0, tiled=True)
    back, grads = experts(
        rank[None], places, dys, h2_all, expert_gate.transpose(0, 2, 1), expert_up.transpose(0, 2, 1), expert_down
    )
    grads, sums_a = after(grads, sums_a)
    grads = lax.psum_scatter(grads, "x", scatter_dimension=0, tiled=True)
    back, mixed = combine(place, to_owners(back), shared_dh, shared_out)
    dr, da, dop, dlog, gain2_terms = middle(
        back, swap(back, "yh"), r, grad_out, h2p, gates, gain2, wr, output_weight, o, stats
    )
    dos = with_other_core(window(dop, True))

    one = jnp.ones((T, 1), BF16)
    width = HW + 64
    other = jnp.concatenate(
        [put(o.astype(BF16), 0, width), put(dlog[:, :63], HW, width), put(one, width - 1, width)], axis=0
    )
    sums_b = products(
        both_cores(jnp.concatenate([da, h2p[:, :D], gain2_terms], axis=0)),
        dense_right(halves(other, width // 2, 384), core),
    )
    b_near, b_wrap = sums_b[..., :256], sums_b[..., 256:]
    steps = z_sum_near(b_near, b_wrap, z)
    dos, steps = after(dos, steps)
    sums_b = z_sum_far(b_near, b_wrap, *steps, z)

    dqkv, dh1_part = attend_back(
        keys_at[None], qs, kv_all, dos, kv, qbias, kbias, cosine, sine, query_weight, key_weight, value_weight
    )
    right = dense_right(dqkv, core)
    below, above = lax.ppermute(right, "z", UP), lax.ppermute(right, "z", DOWN)
    (dh1_part, mixed, sums_a, sums_b), (below, above) = after((dh1_part, mixed, sums_a, sums_b), (below, above))
    rights = [right, below, above, *z_gather_far(below, above)]
    total = xy_sum(jnp.concatenate([sums_b[0][:, 0], sums_b[1][:, 0], sums_a.reshape(8, 40, 768)], axis=2))
    (grads, total), rights = after((grads, total), rights)
    unpacked = unpack(grads)
    output = (r + (mixed.astype(F32) + swap(mixed, "yh").astype(F32))).astype(BF16)
    first, second = core_rows(total, core)
    columns = lambda at, n: jnp.concatenate([first[:, at : at + n], second[:, at : at + n]], axis=1)
    other_grads, shared_grads = columns(0, width // 2), columns(384, both)
    total = xy_sum(projection_grads(h1_left, rights).reshape(8, 40, PADDED))
    total, unpacked = after(total, unpacked)
    gate_grads, up_grads, down_grads = unpacked
    at = lax.axis_index("x") * 320 + lax.axis_index("yl") * 160 + z * 40 + core * 20
    here = lambda v: lax.dynamic_slice_in_dim(v, at, 20, 0)
    weight = jnp.concatenate([here(query_weight), here(key_weight), here(value_weight)], axis=1).astype(F32)
    weight = weight / here(norm1_gain)[:, None]
    first, second = core_rows(total, core)
    qkv_grads = jnp.concatenate([first[:, :HALF], second[:, :HALF]], axis=1)
    gain = jnp.sum(qkv_grads * weight, axis=1, keepdims=True)
    gain = gain + swap(gain, "yh")

    dh1 = dh1_part.astype(F32) + swap(dh1_part, "yh").astype(F32)
    x = tokens.astype(F32)
    inverse = lax.rsqrt(jnp.mean(x * x, axis=1, keepdims=True) + EPSILON)
    unit = x * inverse
    e1 = dh1 * gain1
    grad_tokens = dr + inverse * (e1 - unit * jnp.mean(e1 * unit, axis=1, keepdims=True))

    return (
        output,
        grad_tokens,
        gain[:, 0],
        other_grads[:, width - 1],
        qkv_grads[:, :HW],
        qkv_grads[:, HW : 2 * HW],
        qkv_grads[:, 2 * HW :],
        other_grads[:, :HW].T,
        other_grads[:, HW : width - 1],
        shared_grads[:, :FF],
        shared_grads[:, FF : 2 * FF],
        shared_grads[:, 2 * FF :].T,
        gate_grads,
        up_grads,
        down_grads.transpose(0, 2, 1),
    )


def solution(mesh):
    fine = Mesh(mesh.devices.reshape(4, 2, 4, 2, 2), ("x", "yl", "z", "c", "yh"))
    rows64 = ("x", "yl", "z", "c")
    in_specs = (
        P(rows64, None),
        P(rows64, None),
        P("x", None),
        P("x", None),
        P("x", None),
        P(rows64, None),
        P(),
        P(),
        P(None, "yh"),
        P(None, "yh"),
        P(None, "yh"),
        P("yh", None),
        P(),
        P(None, "yh"),
        P(None, "yh"),
        P("yh", None),
        P(EP, None, "yh"),
        P(EP, None, "yh"),
        P(EP, "yh", None),
    )
    out_specs = (
        P(rows64, None),
        P(rows64, None),
        P(rows64),
        P(rows64),
        P(rows64, "yh"),
        P(rows64, "yh"),
        P(rows64, "yh"),
        P("yh", rows64),
        P(rows64, None),
        P(rows64, "yh"),
        P(rows64, "yh"),
        P("yh", rows64),
        P(EP, "x", "yh"),
        P(EP, "x", "yh"),
        P(EP, "yh", "x"),
    )
    return jax.shard_map(local, mesh=fine, in_specs=in_specs, out_specs=out_specs, check_vma=False)
```

```python
import jax
import jax.numpy as jnp
from jax import lax
from jax.experimental import pallas as pl
from jax.experimental.pallas import tpu as pltpu
from jax.sharding import Mesh, PartitionSpec as P

F32 = jnp.float32
BF16 = jnp.bfloat16
HEAD_DIM = 128
TOPK = 7
EPSILON = 1e-06
NEG_FILL = -1e30
BASE = 10000.0
SCALE = HEAD_DIM ** (-0.5)

T = 128
D = 1280
HEADS = 5
HW = HEADS * HEAD_DIM
FF = 448
E = 4
CAP = 16
BLOCKS = 16
KEYS = 1280
COUNT = BLOCKS * E * CAP
EXTRA = 128

EP = ("yl", "z", "c")
VMEM = pl.BlockSpec(memory_space=pltpu.VMEM)
SMEM = pl.BlockSpec(memory_space=pltpu.SMEM)
ANY = pl.BlockSpec(memory_space=pl.ANY)


def params(mib, **more):
    return pltpu.CompilerParams(vmem_limit_bytes=mib << 20, **more)


def cost(flops, moved):
    return pl.CostEstimate(flops=int(flops), bytes_accessed=int(moved), transcendentals=0)


def dot(a, b):
    return lax.dot_general(a, b, (((1,), (0,)), ((), ())), preferred_element_type=F32)


def dot_nt(a, b):
    return lax.dot_general(a, b, (((1,), (1,)), ((), ())), preferred_element_type=F32)


def dot_tn(a, b):
    return lax.dot_general(a, b, (((0,), (0,)), ((), ())), preferred_element_type=F32)


def split3(v):
    first = v.astype(BF16)
    rest = v - first.astype(F32)
    second = rest.astype(BF16)
    return first, second, (rest - second.astype(F32)).astype(BF16)


def lanes(shape):
    return lax.broadcasted_iota(jnp.int32, shape, 1)


def rows(shape):
    return lax.broadcasted_iota(jnp.int32, shape, 0)


def turn(values, cosine, sine):
    parts = []
    for h in range(HEADS):
        z = values[:, h * 128 : (h + 1) * 128]
        parts.append(z * cosine + pltpu.roll(z, 64, 1) * sine)
    return jnp.concatenate(parts, axis=1)


def per_token(columns):
    lane = lanes((T, EXTRA))
    out = jnp.zeros((T, EXTRA), F32)
    for j, column in enumerate(columns):
        if column is not None:
            out = jnp.where(lane == j, column.astype(F32), out)
    return out.astype(BF16)


def project_kernel(x_ref, g_ref, wq_hbm, wk_hbm, wv_hbm, cos_ref, sin_ref, h1_ref, kv_ref, q_ref, wq, wk, wv, sems):
    copies = [pltpu.make_async_copy(a, b, sems.at[i]) for i, (a, b) in enumerate(((wk_hbm, wk), (wv_hbm, wv), (wq_hbm, wq)))]
    for copy in copies:
        copy.start()
    x = x_ref[...].astype(F32)
    inverse = lax.rsqrt(jnp.mean(x * x, axis=1, keepdims=True) + EPSILON)
    h1 = (x * inverse * g_ref[...][None, :]).astype(BF16)
    h1_ref[...] = h1
    cosine, sine = cos_ref[...], sin_ref[...]
    copies[0].wait()
    kv_ref[:, :HW] = turn(dot(h1, wk[...]), cosine, sine).astype(BF16)
    copies[1].wait()
    kv_ref[:, HW:] = dot(h1, wv[...]).astype(BF16)
    copies[2].wait()
    q_ref[...] = turn(dot(h1, wq[...]), cosine, sine).astype(BF16)


def project(x, gain, wq, wk, wv, cosine, sine):
    weight = pltpu.VMEM((D, HW), BF16)
    return pl.pallas_call(
        project_kernel,
        out_shape=(
            jax.ShapeDtypeStruct((T, D), BF16),
            jax.ShapeDtypeStruct((T, 2 * HW), BF16),
            jax.ShapeDtypeStruct((T, HW), BF16),
        ),
        in_specs=[VMEM, VMEM, ANY, ANY, ANY, VMEM, VMEM],
        out_specs=(VMEM,) * 3,
        scratch_shapes=[weight, weight, weight, pltpu.SemaphoreType.DMA((3,))],
        compiler_params=params(60),
        cost_estimate=cost(2 * T * D * 3 * HW, 6e6),
        name="project",
    )(x, gain, wq, wk, wv, cosine, sine)


def slots_kernel(routes_ref, dy_ref, dyp_ref, hot_ref, place_ref):
    expert = rows((EXTRA, T))
    routes = routes_ref[...]
    hot = jnp.zeros((EXTRA, T), F32)
    for j in range(TOPK):
        hot = jnp.where(expert == routes[j : j + 1, :], 1.0, hot)
    hot = hot.astype(BF16)
    same = (rows((T, T)) == lanes((T, T))).astype(BF16)
    hot = dot_tn(hot, same)
    hot_ref[...] = hot
    before = (lanes((T, T)) < rows((T, T))).astype(BF16)
    slot = dot(before, hot.astype(BF16))
    slot = jnp.where(hot > 0.5, slot, -1.0).astype(BF16)
    dyp_ref[:, :D] = dy_ref[...]
    dyp_ref[:, D:] = slot
    at = lanes((EXTRA, COUNT))
    spread = (rows((EXTRA, COUNT)) == (at >> 4)).astype(BF16)
    place = dot(slot, spread) == (lanes((T, COUNT)) & (CAP - 1)).astype(F32)
    place_ref[...] = jnp.where(place, 1.0, 0.0).astype(BF16)


def slots(routes, dy):
    return pl.pallas_call(
        slots_kernel,
        out_shape=(
            jax.ShapeDtypeStruct((T, D + EXTRA), BF16),
            jax.ShapeDtypeStruct((T, EXTRA), F32),
            jax.ShapeDtypeStruct((T, COUNT), BF16),
        ),
        in_specs=[VMEM] * 2,
        out_specs=(VMEM,) * 3,
        compiler_params=params(12),
        cost_estimate=cost(2 * T * T * COUNT, 1e6),
        name="slots",
    )(routes, dy)


def masks_kernel(info_ref, docs_ref, qbias_ref, kbias_ref):
    chip, core = info_ref[0], info_ref[1]
    border = jnp.sum(jnp.where(docs_ref[...] == 0, 1.0, 0.0), axis=1, keepdims=True).astype(jnp.int32)
    lane = lanes((1, KEYS))
    own = chip * 2 * T + core * T + rows((T, 1))

    def bias(query, key, there):
        seen = key <= query
        for j in range(2):
            first, last = info_ref[3 + j], info_ref[5 + j]
            seen |= (query >= first) & (query < last) & (key >= first) & (key < last)
        same = (query >= border) == (key >= border)
        return jnp.where(seen & same & there, 0.0, NEG_FILL).astype(F32)

    qbias_ref[...] = bias(own, info_ref[2] + lane, lane >= 0)
    other = (lane >= KEYS // 2).astype(jnp.int32)
    step = (lane - other * (KEYS // 2)) >> 7
    query = (chip + step) * 2 * T + (core ^ other) * T + (lane & (T - 1))
    kbias_ref[...] = bias(query, own, query < BLOCKS * T)


def masks(info, docs):
    bias = jax.ShapeDtypeStruct((T, KEYS), F32)
    return pl.pallas_call(
        masks_kernel,
        out_shape=(bias, bias),
        in_specs=[SMEM, VMEM],
        out_specs=(VMEM,) * 2,
        compiler_params=params(12),
        cost_estimate=cost(40 * T * KEYS, 2e6),
        name="masks",
    )(info, docs)


WINDOW = 10


def attend_kernel(at_ref, q_ref, kv_hbm, bias_ref, wo_ref, o_ref, part_ref, stats_ref, kvs, sems):
    start = pl.multiple_of(at_ref[0], T)
    copies = []
    for i in range(2):
        cut = pl.ds(i * HW, HW)
        copies.append(pltpu.make_async_copy(kv_hbm.at[pl.ds(start, KEYS), cut], kvs.at[:, cut], sems.at[i]))
        copies[i].start()
    copies[0].wait()
    copies[1].wait()
    stats, outs = [], []
    for h in range(HEADS):
        cut = slice(h * 128, (h + 1) * 128)
        vcut = slice(HW + h * 128, HW + (h + 1) * 128)
        q = q_ref[:, cut]
        s = dot_nt(q, kvs[:, cut]) * SCALE + bias_ref[...]
        high = jnp.max(s, axis=1, keepdims=True)
        e = jnp.exp(s - high)
        total = jnp.sum(e, axis=1, keepdims=True)
        p = (e * (1.0 / total)).astype(BF16)
        outs.append(dot(p, kvs[:, vcut]))
        stats += list(split3((high + jnp.log(total)) * (-1.0 / SCALE)))
    o = jnp.concatenate(outs, axis=1)
    o_ref[...] = o
    part_ref[...] = dot(o.astype(BF16), wo_ref[...]).astype(BF16)
    stats_ref[...] = per_token([None] * (3 * HEADS) + stats)


def attend(at, q, kv_all, bias, wo):
    return pl.pallas_call(
        attend_kernel,
        out_shape=(
            jax.ShapeDtypeStruct((T, HW), F32),
            jax.ShapeDtypeStruct((T, D), BF16),
            jax.ShapeDtypeStruct((T, EXTRA), BF16),
        ),
        in_specs=[SMEM, VMEM, ANY, VMEM, VMEM],
        out_specs=(VMEM,) * 3,
        scratch_shapes=[pltpu.VMEM((KEYS, 2 * HW), BF16), pltpu.SemaphoreType.DMA((2,))],
        compiler_params=params(60),
        cost_estimate=cost(4 * T * KEYS * HW + 2 * T * HW * D, 6e6),
        name="attend",
    )(at, q, kv_all, bias, wo)


def gate_kernel(x_ref, a_ref, b_ref, g_ref, wr_ref, hot_ref, r_ref, h2p_ref, gates_ref):
    r = x_ref[...].astype(F32) + (a_ref[...].astype(F32) + b_ref[...].astype(F32))
    r_ref[...] = r
    inverse = lax.rsqrt(jnp.mean(r * r, axis=1, keepdims=True) + EPSILON)
    h2 = (r * inverse * g_ref[...]).astype(BF16)
    hot = hot_ref[...] > 0.5
    logits = jnp.where(hot, dot_nt(h2, wr_ref[...]), NEG_FILL)
    e = jnp.where(hot, jnp.exp(logits - jnp.max(logits, axis=1, keepdims=True)), 0.0)
    gates = e / jnp.sum(e, axis=1, keepdims=True)
    gates_ref[...] = gates
    first = gates.astype(BF16).astype(F32)
    h2p_ref[:, :D] = h2
    h2p_ref[:, D:] = (first + pltpu.roll(gates - first, 64, 1)).astype(BF16)


def gate(x, a, b, gain, wr, hot):
    return pl.pallas_call(
        gate_kernel,
        out_shape=(
            jax.ShapeDtypeStruct((T, D), F32),
            jax.ShapeDtypeStruct((T, D + EXTRA), BF16),
            jax.ShapeDtypeStruct((T, EXTRA), F32),
        ),
        in_specs=[VMEM] * 6,
        out_specs=(VMEM,) * 3,
        compiler_params=params(24),
        cost_estimate=cost(2 * T * D * 128, 2e6),
        name="gate",
    )(x, a, b, gain, wr, hot)


def silu_parts(gate_pre):
    sigmoid = 1.0 / (1.0 + jnp.exp(-gate_pre))
    return gate_pre * sigmoid, sigmoid * (1.0 + gate_pre * (1.0 - sigmoid))


def shared_kernel(h2p_ref, dy_ref, wg_ref, wu_ref, wd_ref, out_ref, dh_ref, sh_ref, dsg_ref, dsu_ref):
    h2 = h2p_ref[:, :D]
    sg = dot_nt(h2, wg_ref[...])
    su = dot_nt(h2, wu_ref[...])
    act, slope = silu_parts(sg)
    sh = (act * su).astype(BF16)
    sh_ref[...] = sh
    out_ref[...] = dot(sh, wd_ref[...])
    dsh = dot_nt(dy_ref[...], wd_ref[...])
    dsg = (dsh * su * slope).astype(BF16)
    dsu = (dsh * act).astype(BF16)
    dsg_ref[...] = dsg
    dsu_ref[...] = dsu
    dh_ref[...] = dot(dsg, wg_ref[...]) + dot(dsu, wu_ref[...])


def shared(h2p, dy, wg, wu, wd):
    hidden = jax.ShapeDtypeStruct((T, FF), BF16)
    return pl.pallas_call(
        shared_kernel,
        out_shape=(jax.ShapeDtypeStruct((T, D), F32), jax.ShapeDtypeStruct((T, D), F32), hidden, hidden, hidden),
        in_specs=[VMEM] * 5,
        out_specs=(VMEM,) * 5,
        compiler_params=params(24),
        cost_estimate=cost(1e6, 1e5),
        name="shared",
    )(h2p, dy, wg, wu, wd)


PAIR = 2 * E * CAP


def dispatch_kernel(rank_ref, dy_ref, hot_ref, out_ref):
    rank = rank_ref[0]
    spread = (rows((EXTRA, PAIR)) == rank * E + ((lanes((EXTRA, PAIR)) & (E * CAP - 1)) >> 4)).astype(BF16)
    place = (lanes((2 * T, PAIR)) & (CAP - 1)).astype(F32)
    own = (lanes((2 * T, PAIR)) >= E * CAP) == (rows((2 * T, PAIR)) >= T)
    for k in range(2):
        at = slice(k * 2 * T, (k + 1) * 2 * T)
        hot = jnp.where(own & (dot(dy_ref[at, D:], spread) == place), 1.0, 0.0).astype(BF16)
        hot_ref[at, :] = hot
        dy = dot_tn(hot, dy_ref[at, :D]).astype(BF16)
        for j in range(2):
            to = slice((k * 2 + j) * CAP, (k * 2 + j + 1) * CAP)
            for i in range(E):
                out_ref[i, to, :] = dy[(j * E + i) * CAP : (j * E + i + 1) * CAP]


def dispatch(rank, dy_all):
    return pl.pallas_call(
        dispatch_kernel,
        out_shape=(
            jax.ShapeDtypeStruct((BLOCKS * T, PAIR), BF16),
            jax.ShapeDtypeStruct((E, BLOCKS * CAP, D), BF16),
        ),
        grid=(BLOCKS // 4,),
        in_specs=[SMEM, pl.BlockSpec((4 * T, D + EXTRA), lambda k: (k, 0))],
        out_specs=(pl.BlockSpec((4 * T, PAIR), lambda k: (k, 0)), pl.BlockSpec((E, 4 * CAP, D), lambda k: (0, k, 0))),
        compiler_params=params(60, dimension_semantics=("arbitrary",)),
        cost_estimate=cost(2 * BLOCKS * T * PAIR * D, 1e7),
        name="dispatch",
    )(rank, dy_all)


def experts_kernel(rank_ref, hot_ref, dy_ref, h2_hbm, wg_ref, wu_ref, wd_ref, out_ref, grads_hbm, h2s, xs, gs, stage, sems, outs):
    e = pl.program_id(0)
    rank = rank_ref[0]
    slot = e & 1

    def result(slot, group):
        to = pl.ds(pl.multiple_of(group * 2 * FF, 128), 2 * FF)
        return pltpu.make_async_copy(stage.at[slot], grads_hbm.at[:, to], outs.at[slot])

    @pl.when(e == 0)
    def _():
        copies = []
        for k in range(0, BLOCKS, 2):
            at = pl.ds(k * T, 2 * T)
            copies.append(pltpu.make_async_copy(h2_hbm.at[at, :], h2s.at[at, :], sems.at[k // 2]))
        for copy in copies:
            copy.start()
        named = rank * E + ((rows((PAIR, EXTRA)) & (E * CAP - 1)) >> 4)
        column = lanes((PAIR, EXTRA))
        mine = (column == named) | (column == named + 64)
        for k in range(0, BLOCKS, 2):
            at = slice(k * T, (k + 2) * T)
            copies[k // 2].wait()
            x = dot_tn(hot_ref[at, :], h2s[at, :])
            g = jnp.sum(jnp.where(mine, x[:, D:], 0.0), axis=1, keepdims=True)
            g = jnp.broadcast_to(g, (PAIR, 128))
            x = x[:, :D].astype(BF16)
            for j in range(2):
                to = slice((k + j) * CAP, (k + j + 1) * CAP)
                for i in range(E):
                    cut = slice((j * E + i) * CAP, (j * E + i + 1) * CAP)
                    xs[i, to, :] = x[cut]
                    gs[i, to, :] = g[cut]

    x = xs[e]
    g = gs[e][:, :1]
    eg = dot_nt(x, wg_ref[0])
    eu = dot_nt(x, wu_ref[0])
    act, slope = silu_parts(eg)
    eh = act * eu
    geh = (g * eh).astype(BF16)
    eh = eh.astype(BF16)
    dy = dy_ref[0]
    deh = dot_nt(dy, wd_ref[0])
    dgate = jnp.sum(eh.astype(F32) * deh, axis=1, keepdims=True)
    deh = g * deh
    deg = (deh * eu * slope).astype(BF16)
    deu = (deh * act).astype(BF16)
    shape = (BLOCKS, CAP, -1)
    out_ref[:, 0, :, D + EXTRA :] = (g * dot(eh, wd_ref[0])).astype(BF16).reshape(shape)
    out_ref[:, 0, :, :D] = (dot(deg, wg_ref[0]) + dot(deu, wu_ref[0])).astype(BF16).reshape(shape)
    column = lanes((BLOCKS * CAP, EXTRA))
    expert = rank * E + e
    first = dgate.astype(BF16).astype(F32)
    placed = jnp.where(column == expert, first, jnp.where(column == expert + 64, dgate - first, 0.0))
    out_ref[:, 0, :, D : D + EXTRA] = placed.astype(BF16).reshape(shape)

    @pl.when(e >= 2)
    def _():
        result(slot, e - 2).wait()

    dgu = jnp.concatenate([deg, deu], axis=1)
    for r in range(0, D, 256):
        stage[slot, r : r + 256, :] = dot_tn(x[:, r : r + 256], dgu).astype(BF16)
    result(slot, e).start()

    @pl.when(slot == 0)
    def _():
        @pl.when(e == 2)
        def _():
            result(2, E).wait()

        for r in range(0, D, 256):
            stage[2, r : r + 256, :FF] = dot_tn(dy[:, r : r + 256], geh).astype(BF16)

    @pl.when(slot == 1)
    def _():
        for r in range(0, D, 256):
            stage[2, r : r + 256, FF:] = dot_tn(dy[:, r : r + 256], geh).astype(BF16)
        result(2, E + (e >> 1)).start()

    @pl.when(e == E - 1)
    def _():
        result(0, E - 2).wait()
        result(1, E - 1).wait()
        result(2, E + 1).wait()


GRADS = 6
BACK = D + EXTRA + D


def experts(rank, hot, dy, h2_all, wg, wu, wd):
    n = BLOCKS * CAP
    per = lambda shape: pl.BlockSpec((1, *shape), lambda e: (e, 0, 0))
    held = lambda shape: pl.BlockSpec(shape, lambda e: (0,) * len(shape), pipeline_mode=pl.Buffered(1))
    return pl.pallas_call(
        experts_kernel,
        out_shape=(
            jax.ShapeDtypeStruct((BLOCKS, E, CAP, BACK), BF16),
            jax.ShapeDtypeStruct((D, GRADS * 2 * FF), BF16),
        ),
        grid=(E,),
        in_specs=[SMEM, held((BLOCKS * T, PAIR)), per((n, D)), ANY, per((FF, D)), per((FF, D)), per((FF, D))],
        out_specs=(pl.BlockSpec((BLOCKS, 1, CAP, BACK), lambda e: (0, e, 0, 0)), ANY),
        scratch_shapes=[
            pltpu.VMEM((BLOCKS * T, D + EXTRA), BF16),
            pltpu.VMEM((E, n, D), BF16),
            pltpu.VMEM((E, n, 128), F32),
            pltpu.VMEM((3, D, 2 * FF), BF16),
            pltpu.SemaphoreType.DMA((BLOCKS // 2,)),
            pltpu.SemaphoreType.DMA((3,)),
        ],
        compiler_params=params(58, dimension_semantics=("arbitrary",)),
        cost_estimate=cost(2 * E * n * D * FF * 9, 5e7),
        name="experts",
    )(rank, hot, dy, h2_all, wg, wu, wd)


def combine_kernel(place_ref, back_ref, dh_ref, out_ref, back_out_ref, mixed_ref):
    total = dot(place_ref[...], back_ref[...])
    back_out_ref[:, :D] = (total[:, :D] + dh_ref[...]).astype(BF16)
    back_out_ref[:, D:] = total[:, D : D + EXTRA].astype(BF16)
    mixed_ref[...] = (total[:, D + EXTRA :] + out_ref[...]).astype(BF16)


def combine(place, back, dh, out):
    return pl.pallas_call(
        combine_kernel,
        out_shape=(jax.ShapeDtypeStruct((T, D + EXTRA), BF16), jax.ShapeDtypeStruct((T, D), BF16)),
        in_specs=[VMEM] * 4,
        out_specs=(VMEM,) * 2,
        compiler_params=params(24),
        cost_estimate=cost(2 * T * COUNT * BACK, 7e6),
        name="combine",
    )(place, back.reshape(COUNT, BACK), dh, out)


def middle_kernel(a_ref, b_ref, r_ref, dy_ref, h2p_ref, gates_ref, g_ref, wr_ref, wo_ref, o_ref, stats_ref, dr_ref, da_ref, dop_ref, dlog_ref, gain_ref):
    both = a_ref[...].astype(F32) + b_ref[...].astype(F32)
    gates = gates_ref[...]
    dgate = both[:, D:] + pltpu.roll(both[:, D:], 64, 1)
    dsel = gates * (dgate - jnp.sum(gates * dgate, axis=1, keepdims=True))
    dlog = dsel.astype(BF16)
    dlog_ref[...] = dlog
    dh2 = both[:, :D] + dot(dlog, wr_ref[...])
    r = r_ref[...]
    inverse = lax.rsqrt(jnp.mean(r * r, axis=1, keepdims=True) + EPSILON)
    unit = r * inverse
    gain_ref[...] = (dh2 * unit).astype(BF16)
    e2 = dh2 * g_ref[...]
    dr = dy_ref[...].astype(F32) + inverse * (e2 - unit * jnp.mean(e2 * unit, axis=1, keepdims=True))
    dr_ref[...] = dr
    da = dr.astype(BF16)
    da_ref[...] = da
    do = dot_nt(da, wo_ref[...]).astype(BF16)
    dop_ref[:, :HW] = do
    stats = []
    both = do.astype(F32) * o_ref[...]
    for h in range(HEADS):
        stats += list(split3(-jnp.sum(both[:, h * 128 : (h + 1) * 128], axis=1, keepdims=True)))
    dop_ref[:, HW:] = per_token(stats) + stats_ref[...]


def middle(a, b, r, dy, h2p, gates, gain, wr, wo, o, stats):
    return pl.pallas_call(
        middle_kernel,
        out_shape=(
            jax.ShapeDtypeStruct((T, D), F32),
            jax.ShapeDtypeStruct((T, D), BF16),
            jax.ShapeDtypeStruct((T, HW + EXTRA), BF16),
            jax.ShapeDtypeStruct((T, EXTRA), BF16),
            jax.ShapeDtypeStruct((T, D), BF16),
        ),
        in_specs=[VMEM] * 11,
        out_specs=(VMEM,) * 5,
        compiler_params=params(24),
        cost_estimate=cost(2 * T * D * (HW + 128), 5e6),
        name="middle",
    )(a, b, r, dy, h2p, gates, gain, wr, wo, o, stats)


HALF = 3 * HW // 2
PADDED = 1024


def attend_back_kernel(*refs):
    at_ref, q_hbm, kv_hbm, do_hbm, refs = refs[0], refs[1], refs[2], refs[3 : 3 + WINDOW], refs[3 + WINDOW :]
    w_hbm, refs = refs[:3], refs[3:]
    kv_ref, qbias_ref, kbias_ref, cos_ref, sin_ref, dqkv_ref, part_ref, kvs, qs, dos, ws, sems = refs
    keys_at = pl.ds(pl.multiple_of(at_ref[WINDOW], T), KEYS)
    copies = [pltpu.make_async_copy(v, dos.at[i], sems.at[i]) for i, v in enumerate(do_hbm)]
    for i in range(WINDOW):
        source = q_hbm.at[pl.ds(pl.multiple_of(at_ref[i], T), T), :]
        copies.append(pltpu.make_async_copy(source, qs.at[i], sems.at[WINDOW + i]))
    copies += [pltpu.make_async_copy(v, ws.at[i], sems.at[2 * WINDOW + i]) for i, v in enumerate(w_hbm)]
    copies.append(pltpu.make_async_copy(kv_hbm.at[keys_at, :], kvs, sems.at[2 * WINDOW + 3]))
    early = [2 * WINDOW + 3, 0, WINDOW]
    late = [i for i in range(2 * WINDOW) if i not in early]
    weights = [2 * WINDOW, 2 * WINDOW + 1, 2 * WINDOW + 2]
    for i in early + late + weights:
        copies[i].start()
    for i in early:
        copies[i].wait()
    lane = lanes((T, EXTRA))
    extra = dos[0, :, HW:]
    stats = extra.astype(F32)
    side = lambda parts: jnp.concatenate(parts, axis=1)
    block = lambda v, i: v[:, i * T : (i + 1) * T]
    every = range(WINDOW)
    heads = [(slice(h * 128, (h + 1) * 128), slice(HW + h * 128, HW + (h + 1) * 128)) for h in range(HEADS)]
    its = lambda first: (lane >= first) & (lane < first + 3)
    dqs, dks, dvs = [], [], []
    for h, (cut, vcut) in enumerate(heads):
        less_dot = jnp.sum(jnp.where(its(3 * h), stats, 0.0), axis=1, keepdims=True)
        less = jnp.sum(jnp.where(its(3 * (HEADS + h)), stats, 0.0), axis=1, keepdims=True)
        q, do = qs[0, :, cut], dos[0, :, cut]
        p = jnp.exp((dot_nt(q, kvs[:, cut]) + less) * SCALE + qbias_ref[...])
        dp = dot_nt(do, kvs[:, vcut]) + less_dot
        ds = (p * dp * SCALE).astype(BF16)
        dqs.append(dot(ds, kvs[:, cut]))
    for i in late:
        copies[i].wait()
    for h, (cut, vcut) in enumerate(heads):
        k_wide = side([kv_ref[:, cut], its(3 * (HEADS + h)).astype(BF16)])
        v_wide = side([kv_ref[:, vcut], its(3 * h).astype(BF16)])
        pt = side([dot_nt(k_wide, side([qs[i, :, cut], dos[i, :, HW:]])) for i in every])
        pt = jnp.exp(pt * SCALE + kbias_ref[...])
        dpt = side([dot_nt(v_wide, side([dos[i, :, cut], dos[i, :, HW:]])) for i in every])
        dst = (pt * dpt * SCALE).astype(BF16)
        pt = pt.astype(BF16)
        dks.append(sum(dot(block(dst, i), qs[i, :, cut]) for i in every))
        dvs.append(sum(dot(block(pt, i), dos[i, :, cut]) for i in every))
    cosine, sine = cos_ref[...], -sin_ref[...]
    dq = turn(side(dqs), cosine, sine).astype(BF16)
    dk = turn(side(dks), cosine, sine).astype(BF16)
    dv = side(dvs).astype(BF16)
    dqkv = side([dq, dk, dv])
    none = jnp.zeros((T, PADDED - HALF), BF16)
    dqkv_ref[...] = side([dqkv[:, :HALF], none, dqkv[:, HALF:], none])
    for i in weights:
        copies[i].wait()
    part = dot_nt(dq, ws[0]) + dot_nt(dk, ws[1]) + dot_nt(dv, ws[2])
    part_ref[...] = part.astype(BF16)


def attend_back(at, q_all, kv_all, dos, kv, qbias, kbias, cosine, sine, wq, wk, wv):
    return pl.pallas_call(
        attend_back_kernel,
        out_shape=(
            jax.ShapeDtypeStruct((T, 2 * PADDED), BF16),
            jax.ShapeDtypeStruct((T, D), BF16),
        ),
        in_specs=[SMEM] + [ANY] * (5 + WINDOW) + [VMEM] * 5,
        out_specs=(VMEM,) * 2,
        scratch_shapes=[
            pltpu.VMEM((KEYS, 2 * HW), BF16),
            pltpu.VMEM((WINDOW, T, HW), BF16),
            pltpu.VMEM((WINDOW, T, HW + EXTRA), BF16),
            pltpu.VMEM((3, D, HW), BF16),
            pltpu.SemaphoreType.DMA((2 * WINDOW + 4,)),
        ],
        compiler_params=params(56),
        cost_estimate=cost(16 * T * KEYS * HW + 6 * T * HW * D, 2e7),
        name="attend_back",
    )(at, q_all, kv_all, *dos, wq, wk, wv, kv, qbias, kbias, cosine, sine)


WIDE = 384


def chunks_kernel(h1_ref, out_ref):
    at = lanes((1, WIDE))
    part = jnp.zeros((1, WIDE), jnp.int32)
    for j in range(1, 8):
        part += (at >= 40 * j).astype(jnp.int32)
    for z in range(4):
        source = part * 160 + z * 40 + (at - part * 40)
        place = ((rows((D, WIDE)) == source) & (at < 320)).astype(BF16)
        out_ref[z] = dot(h1_ref[...], place).astype(BF16)


def chunks(h1):
    return pl.pallas_call(
        chunks_kernel,
        out_shape=jax.ShapeDtypeStruct((4, h1.shape[0], WIDE), BF16),
        in_specs=[VMEM],
        out_specs=VMEM,
        compiler_params=params(16),
        cost_estimate=cost(2 * h1.shape[0] * D * 4 * WIDE, 2e6),
        name="chunks",
    )(h1)


SUM_B, SUM_A = 384, 768
GRADS_WIDTH = GRADS * 2 * FF


def projection_grads_kernel(*refs):
    left_hbm, parts, grads_hbm = refs[0], refs[1:6], refs[6]
    out_ref, expert_outs, (left, right, grads, ready, sems, out_sems) = refs[7], refs[8:11], refs[11:]
    copies = [pltpu.make_async_copy(grads_hbm, grads, sems.at[6])]
    copies.append(pltpu.make_async_copy(left_hbm, left, sems.at[0]))
    at = 0
    for i, part in enumerate(parts):
        n = part.shape[0]
        copies.append(pltpu.make_async_copy(part, right.at[pl.ds(at, n), :], sems.at[1 + i]))
        at += n
    for copy in copies:
        copy.start()
    copies[0].wait()
    writes = []
    for e in range(E):
        gate_up = grads[:, e * 2 * FF : (e + 1) * 2 * FF].astype(F32)
        start = (2 * E + e) * FF
        if e % 2 == 0:
            down = grads[:, start : start + 2 * FF].astype(F32)
        ready[e % 2, 0] = gate_up[:, :FF]
        ready[e % 2, 1] = gate_up[:, FF:]
        ready[e % 2, 2] = down[:, (e % 2) * FF : (e % 2 + 1) * FF]
        for i, out in enumerate(expert_outs):
            writes.append(pltpu.make_async_copy(ready.at[e % 2, i], out.at[e], out_sems.at[e % 2, i]))
            writes[-1].start()
        if e in (1, 2):
            for write in writes[3 * (e - 1) : 3 * e]:
                write.wait()
    for copy in copies[1:]:
        copy.wait()
    out_ref[...] = dot_tn(left[...], right[...])[:320].astype(BF16)
    for write in writes[6:]:
        write.wait()


def projection_grads(left, parts, grads):
    expert = jax.ShapeDtypeStruct((E, D // 4, FF), F32)
    return pl.pallas_call(
        projection_grads_kernel,
        out_shape=(jax.ShapeDtypeStruct((320, PADDED), BF16), expert, expert, expert),
        in_specs=[ANY] * 7,
        out_specs=(VMEM, ANY, ANY, ANY),
        scratch_shapes=[
            pltpu.VMEM((8 * T, WIDE), BF16),
            pltpu.VMEM((8 * T, PADDED), BF16),
            pltpu.VMEM((320, GRADS_WIDTH), BF16),
            pltpu.VMEM((2, 3, 320, FF), F32),
            pltpu.SemaphoreType.DMA((7,)),
            pltpu.SemaphoreType.DMA((2, 3)),
        ],
        compiler_params=params(56),
        cost_estimate=cost(2 * 8 * T * WIDE * PADDED, 2e7),
        name="projection_grads",
    )(left, *parts, grads)


def other_sums_kernel(left_ref, right_ref, sums_ref, out_ref):
    out_ref[:, SUM_B:] = sums_ref[...]
    out_ref[:, :SUM_B] = dot_tn(left_ref[...], right_ref[...]).astype(BF16)


def other_sums(left, right, sums):
    return pl.pallas_call(
        other_sums_kernel,
        out_shape=jax.ShapeDtypeStruct((D, SUM_B + SUM_A), BF16),
        in_specs=[VMEM] * 3,
        out_specs=VMEM,
        compiler_params=params(24),
        cost_estimate=cost(2 * left.shape[0] * D * SUM_B, 8e6),
        name="other_sums",
    )(left, right, sums)


DENSE = PADDED + SUM_B + SUM_A


def add_up_kernel(core_ref, parts_ref, others_ref, weight_ref, keep_ref, give_ref, gain_ref):
    first = core_ref[0] == 0
    at = 0
    for ref in (parts_ref, others_ref):
        total = ref[0].astype(F32)
        for i in range(1, 8):
            total += ref[i].astype(F32)
        cut = slice(at, at + ref.shape[2])
        at += ref.shape[2]
        keep_ref[:, cut] = jnp.where(first, total[:20], total[20:])
        give_ref[:, cut] = jnp.where(first, total[20:], total[:20])
        if ref is parts_ref:
            gain_ref[...] = jnp.broadcast_to(jnp.sum(total * weight_ref[...], axis=1, keepdims=True), (40, 128))


def add_up(core, parts, others, weight):
    return pl.pallas_call(
        add_up_kernel,
        out_shape=(
            jax.ShapeDtypeStruct((20, DENSE), F32),
            jax.ShapeDtypeStruct((20, DENSE), F32),
            jax.ShapeDtypeStruct((40, 128), F32),
        ),
        in_specs=[SMEM, VMEM, VMEM, VMEM],
        out_specs=(VMEM,) * 3,
        compiler_params=params(24),
        cost_estimate=cost(1e6, 2e6),
        name="add_up",
    )(core, parts, others, weight)


def dense_outputs_kernel(core_ref, keep_ref, got_ref, g0, g1, g2, g3, q_ref, k_ref, v_ref, o_ref, router_ref, gate_ref, up_ref, down_ref, gains_ref):
    first = core_ref[0] == 0
    keep, got = keep_ref[...], got_ref[...]
    low, high = jnp.where(first, keep, got), jnp.where(first, got, keep)
    columns = lambda at, n: jnp.concatenate([low[:, at : at + n], high[:, at : at + n]], axis=1)
    qkv = columns(0, HALF)
    q_ref[...] = qkv[:, :HW]
    k_ref[...] = qkv[:, HW : 2 * HW]
    v_ref[...] = qkv[:, 2 * HW :]
    other = columns(PADDED, (HW + 64) // 2)
    o_ref[...] = other[:, :HW]
    router_ref[...] = other[:, HW : HW + 63]
    expert = columns(PADDED + SUM_B, 3 * FF // 2)
    gate_ref[...] = expert[:, :FF]
    up_ref[...] = expert[:, FF : 2 * FF]
    down_ref[...] = expert[:, 2 * FF :]
    gain = g0[...] + g1[...] + g2[...] + g3[...]
    gain = jnp.where(first, gain[:20], gain[20:])
    lane = lanes((20, 128))
    both = jnp.where(lane == 0, gain, 0.0) + jnp.where(lane == 1, other[:, HW + 63 :], 0.0)
    same = (rows((20, 20)) == lanes((20, 20))).astype(F32)
    gains_ref[...] = lax.dot_general(both, same, (((0,), (0,)), ((), ())), precision=lax.Precision.HIGHEST, preferred_element_type=F32)


def dense_outputs(core, keep, got, gains):
    out = lambda n: jax.ShapeDtypeStruct((20, n), F32)
    return pl.pallas_call(
        dense_outputs_kernel,
        out_shape=(out(HW), out(HW), out(HW), out(HW), out(63), out(FF), out(FF), out(FF), jax.ShapeDtypeStruct((128, 20), F32)),
        in_specs=[SMEM] + [VMEM] * 6,
        out_specs=(VMEM,) * 9,
        compiler_params=params(16),
        cost_estimate=cost(1e6, 1e6),
        name="dense_outputs",
    )(core, keep, got, *gains)


def ep_perm(dyl, dz, dc):
    at = lambda yl, z, c: (yl * 4 + z) * 2 + c
    return [
        (at(yl, z, c), at(yl ^ dyl, (z + dz) % 4, c ^ dc)) for yl in range(2) for z in range(4) for c in range(2)
    ]


CORE = ep_perm(0, 0, 1)


def send(value, perm):
    return lax.ppermute(value, EP, perm)


def swap(value, axis):
    return lax.ppermute(value, axis, [(0, 1), (1, 0)])


def to_owners(value):
    return lax.all_to_all(value, EP, split_axis=0, concat_axis=0, tiled=True)


def window_perm(step, back):
    pairs = [(i, i + step) for i in range(8 - step) if i + step < 5 or i >= 3]
    pairs = [(j, i) if back else (i, j) for i, j in pairs]
    return [(2 * i + c, 2 * j + c) for i, j in pairs for c in range(2)]


def window(value, back):
    own = [value] + [send(value, window_perm(step, back)) for step in range(1, 5)]
    return own


def with_other_core(own):
    return list(own) + [send(v, CORE) for v in own]


def both_cores(left):
    return jnp.concatenate([left, swap(left, "c")], axis=0)


def dense_right(right, core):
    half = right.shape[1] // 2
    mine = jnp.where(core == 0, right[:, :half], right[:, half:])
    theirs = jnp.where(core == 0, right[:, half:], right[:, :half])
    return both_cores_of(mine, theirs)


def both_cores_of(mine, theirs):
    return jnp.concatenate([mine, swap(theirs, "c")], axis=0)


def products(left, right):
    return dot_tn(left, right).astype(BF16)


UP = [(0, 1), (1, 2), (2, 3), (3, 0)]
DOWN = [(1, 0), (2, 1), (3, 2), (0, 3)]


def z_gather_far(below, above):
    half = below.shape[0] // 2
    return lax.ppermute(below[:half], "z", UP), lax.ppermute(above[half:], "z", DOWN)


def xy_sum(part):
    parts = lax.all_to_all(part, ("x", "yl"), split_axis=0, concat_axis=0, tiled=True)
    return jnp.sum(parts.astype(F32), axis=0)


def rotation(positions):
    half = HEAD_DIM // 2
    frequency = BASE ** (-(jnp.arange(half, dtype=F32) * 2.0) / HEAD_DIM)
    angles = positions.astype(F32)[:, None] * frequency[None, :]
    cosine, sine = jnp.cos(angles), jnp.sin(angles)
    return jnp.concatenate([cosine, cosine], axis=1), jnp.concatenate([-sine, sine], axis=1)


def after(values, ready):
    return lax.optimization_barrier((values, ready))


def local(
    tokens, grad_out, doc_ids, piece_starts, piece_ends, routes, norm1_gain, norm2_gain, query_weight, key_weight, value_weight,
    output_weight, router_weight, shared_gate, shared_up, shared_down, expert_gate, expert_up, expert_down,
):
    core, z = lax.axis_index("c"), lax.axis_index("z")
    rank = lax.axis_index(EP).astype(jnp.int32)
    gain1, gain2 = norm1_gain[None, :], norm2_gain[None, :]
    wr = jnp.pad(router_weight.T, ((0, EXTRA - router_weight.shape[1]), (0, 0)))
    cosine, sine = rotation(rank * T + jnp.arange(T, dtype=jnp.int32))
    keys_at = jnp.where(rank < 10, 0, 768).astype(jnp.int32)
    info = jnp.concatenate([jnp.stack([rank // 2, rank % 2, keys_at]), piece_starts[0], piece_ends[0]]).astype(jnp.int32)
    entry = jnp.arange(WINDOW, dtype=jnp.int32)
    seen_from = jnp.minimum(rank // 2 + entry % 5, 7) * 2 + (rank % 2) ^ (entry // 5)
    group = lambda v: lax.all_gather(v, EP, axis=0, tiled=True)

    h1, kv, q = project(tokens, norm1_gain, query_weight, key_weight, value_weight, cosine, sine)
    kv_all = group(kv)
    h1_left = lax.all_to_all(chunks(h1), "z", split_axis=0, concat_axis=0, tiled=True)
    h1_left = jnp.stack([h1_left, swap(h1_left, "c")], axis=1)
    pick = lambda i: lax.dynamic_slice_in_dim(h1_left, i % 4, 1, 0)
    h1_left = jnp.concatenate([pick(z), pick(z + 3), pick(z + 1), pick(z + 2)], axis=0)
    dyp, hot, place = slots(routes.T, grad_out)
    qbias, kbias = masks(info, doc_ids)
    at = lax.axis_index("x") * 320 + lax.axis_index("yl") * 160 + z * 40
    here = lambda v: lax.dynamic_slice_in_dim(v, at, 40, 0)
    weight = jnp.concatenate([here(query_weight), here(key_weight), here(value_weight)], axis=1).astype(F32)
    weight = jnp.where(core == 0, weight[:, :HALF], weight[:, HALF:]) / here(norm1_gain)[:, None]
    weight = jnp.pad(weight, ((0, 0), (0, PADDED - HALF)))
    (dyp, q, h1_left, qbias, kbias, weight), kv_all = after((dyp, q, h1_left, qbias, kbias, weight), kv_all)
    dy_all = group(dyp)
    o, part, stats = attend(keys_at[None], q, kv_all, qbias, output_weight)
    r, h2p, gates = gate(tokens, part, swap(part, "yh"), gain2, wr, hot)
    h2_all = group(h2p)
    shared_out, shared_dh, sh, dsg, dsu = shared(h2p, grad_out, shared_gate.T, shared_up.T, shared_down)
    places, dys = dispatch(rank[None], dy_all)

    put = lambda v, before, width: jnp.pad(v, ((0, 0), (before, width - before - v.shape[1])))
    both = 3 * FF // 2
    halves = lambda v, used, padded: jnp.concatenate([put(v[:, :used], 0, padded), put(v[:, used:], 0, padded)], axis=1)
    right = jnp.concatenate([put(jnp.concatenate([dsg, dsu], axis=1), 0, 3 * FF), put(sh, 2 * FF, 3 * FF)], axis=0)
    sums_a = products(
        both_cores(jnp.concatenate([h2p[:, :D], grad_out], axis=0)), dense_right(halves(right, both, 768), core)
    )
    (places, dys, sums_a, late_q), h2_all = after((places, dys, sums_a, q), h2_all)
    q_all = group(late_q)
    back, grads = experts(
        rank[None], places, dys, h2_all, expert_gate.transpose(0, 2, 1), expert_up.transpose(0, 2, 1), expert_down
    )
    grads = lax.psum_scatter(grads, "x", scatter_dimension=0, tiled=True)
    back, mixed = combine(place, to_owners(back.reshape(BLOCKS, E * CAP, BACK)), shared_dh, shared_out)
    dr, da, dop, dlog, gain2_terms = middle(
        back, swap(back, "yh"), r, grad_out, h2p, gates, gain2, wr, output_weight, o, stats
    )
    dos = with_other_core(window(dop, True))

    one = jnp.ones((T, 1), BF16)
    width = HW + 64
    other = jnp.concatenate(
        [put(o.astype(BF16), 0, width), put(dlog[:, :63], HW, width), put(one, width - 1, width)], axis=0
    )
    sums_ab = other_sums(
        both_cores(jnp.concatenate([da, h2p[:, :D], gain2_terms], axis=0)),
        dense_right(halves(other, width // 2, SUM_B), core),
        sums_a,
    )
    (dos, h1_left), sums_ab = after((dos, h1_left.reshape(8 * T, WIDE)), sums_ab)
    sums_ab = sums_ab.reshape(8, 4, 40, SUM_B + SUM_A).transpose(1, 0, 2, 3).reshape(D, SUM_B + SUM_A)
    sums_ab = lax.psum_scatter(sums_ab, "z", scatter_dimension=0, tiled=True)

    dqkv, dh1_part = attend_back(
        jnp.concatenate([seen_from * T, keys_at[None]]), q_all, kv_all, dos, kv, qbias, kbias, cosine, sine, query_weight, key_weight, value_weight
    )
    right = dense_right(dqkv, core)
    (dh1_part, mixed), right = after((dh1_part, mixed), right)
    output = (r + (mixed.astype(F32) + swap(mixed, "yh").astype(F32))).astype(BF16)
    below, above = lax.ppermute(right, "z", UP), lax.ppermute(right, "z", DOWN)
    rights = [right, below, above, *z_gather_far(below, above)]
    sums_c, gate_grads, up_grads, down_grads = projection_grads(h1_left, rights, grads)
    spread_out = lambda v: lax.all_to_all(v.reshape(8, 40, -1), ("x", "yl"), split_axis=0, concat_axis=0, tiled=True)
    parts = spread_out(sums_c)
    others, parts = after(sums_ab, parts)
    others = spread_out(others)
    keep, give, gain = add_up(core.astype(jnp.int32)[None], parts, others, weight)
    across = lax.ppermute(gain, ("c", "yh"), [(0, 3), (1, 2), (2, 1), (3, 0)])
    gains = gain, swap(gain, "yh"), swap(gain, "c"), across
    dense = dense_outputs(core.astype(jnp.int32)[None], keep, swap(give, "c"), gains)

    dh1 = dh1_part.astype(F32) + swap(dh1_part, "yh").astype(F32)
    x = tokens.astype(F32)
    inverse = lax.rsqrt(jnp.mean(x * x, axis=1, keepdims=True) + EPSILON)
    unit = x * inverse
    e1 = dh1 * gain1
    grad_tokens = dr + inverse * (e1 - unit * jnp.mean(e1 * unit, axis=1, keepdims=True))

    return (
        output,
        grad_tokens,
        dense[8][0],
        dense[8][1],
        dense[0],
        dense[1],
        dense[2],
        dense[3].T,
        dense[4],
        dense[5],
        dense[6],
        dense[7].T,
        gate_grads,
        up_grads,
        down_grads.transpose(0, 2, 1),
    )


def solution(mesh):
    fine = Mesh(mesh.devices.reshape(4, 2, 4, 2, 2), ("x", "yl", "z", "c", "yh"))
    rows64 = ("x", "yl", "z", "c")
    in_specs = (
        P(rows64, None),
        P(rows64, None),
        P("x", None),
        P("x", None),
        P("x", None),
        P(rows64, None),
        P(),
        P(),
        P(None, "yh"),
        P(None, "yh"),
        P(None, "yh"),
        P("yh", None),
        P(),
        P(None, "yh"),
        P(None, "yh"),
        P("yh", None),
        P(EP, None, "yh"),
        P(EP, None, "yh"),
        P(EP, "yh", None),
    )
    out_specs = (
        P(rows64, None),
        P(rows64, None),
        P(rows64),
        P(rows64),
        P(rows64, "yh"),
        P(rows64, "yh"),
        P(rows64, "yh"),
        P("yh", rows64),
        P(rows64, None),
        P(rows64, "yh"),
        P(rows64, "yh"),
        P("yh", rows64),
        P(EP, "x", "yh"),
        P(EP, "x", "yh"),
        P(EP, "yh", "x"),
    )
    return jax.shard_map(local, mesh=fine, in_specs=in_specs, out_specs=out_specs, check_vma=False)
```

```python
import jax
import jax.numpy as jnp
from jax import lax
from jax.experimental import pallas as pl
from jax.experimental.pallas import tpu as pltpu
from jax.sharding import Mesh, PartitionSpec as P

F32 = jnp.float32
BF16 = jnp.bfloat16
HEAD_DIM = 128
TOPK = 7
EPSILON = 1e-06
NEG_FILL = -1e30
BASE = 10000.0
SCALE = HEAD_DIM ** (-0.5)

T = 128
D = 1280
HEADS = 5
HW = HEADS * HEAD_DIM
FF = 448
E = 4
CAP = 16
BLOCKS = 16
KEYS = 1280
COUNT = BLOCKS * E * CAP
EXTRA = 128

EP = ("yl", "z", "c")
VMEM = pl.BlockSpec(memory_space=pltpu.VMEM)
SMEM = pl.BlockSpec(memory_space=pltpu.SMEM)
ANY = pl.BlockSpec(memory_space=pl.ANY)


def params(mib, **more):
    return pltpu.CompilerParams(vmem_limit_bytes=mib << 20, **more)


def cost(flops, moved):
    return pl.CostEstimate(flops=int(flops), bytes_accessed=int(moved), transcendentals=0)


def dot(a, b):
    return lax.dot_general(a, b, (((1,), (0,)), ((), ())), preferred_element_type=F32)


def dot_nt(a, b):
    return lax.dot_general(a, b, (((1,), (1,)), ((), ())), preferred_element_type=F32)


def dot_tn(a, b):
    return lax.dot_general(a, b, (((0,), (0,)), ((), ())), preferred_element_type=F32)


def split3(v):
    first = v.astype(BF16)
    rest = v - first.astype(F32)
    second = rest.astype(BF16)
    return first, second, (rest - second.astype(F32)).astype(BF16)


def lanes(shape):
    return lax.broadcasted_iota(jnp.int32, shape, 1)


def rows(shape):
    return lax.broadcasted_iota(jnp.int32, shape, 0)


def turn(values, cosine, sine):
    parts = []
    for h in range(HEADS):
        z = values[:, h * 128 : (h + 1) * 128]
        parts.append(z * cosine + pltpu.roll(z, 64, 1) * sine)
    return jnp.concatenate(parts, axis=1)


def per_token(columns):
    lane = lanes((T, EXTRA))
    out = jnp.zeros((T, EXTRA), F32)
    for j, column in enumerate(columns):
        if column is not None:
            out = jnp.where(lane == j, column.astype(F32), out)
    return out.astype(BF16)


def project_kernel(x_ref, g_ref, wk_hbm, wv_hbm, cos_ref, sin_ref, h1_ref, kv_ref, wk, wv, sems):
    copies = [pltpu.make_async_copy(a, b, sems.at[i]) for i, (a, b) in enumerate(((wk_hbm, wk), (wv_hbm, wv)))]
    for copy in copies:
        copy.start()
    x = x_ref[...].astype(F32)
    inverse = lax.rsqrt(jnp.mean(x * x, axis=1, keepdims=True) + EPSILON)
    h1 = (x * inverse * g_ref[...][None, :]).astype(BF16)
    h1_ref[...] = h1
    cosine, sine = cos_ref[...], sin_ref[...]
    copies[0].wait()
    kv_ref[:, :HW] = turn(dot(h1, wk[...]), cosine, sine).astype(BF16)
    copies[1].wait()
    kv_ref[:, HW:] = dot(h1, wv[...]).astype(BF16)


def project(x, gain, wk, wv, cosine, sine):
    weight = pltpu.VMEM((D, HW), BF16)
    return pl.pallas_call(
        project_kernel,
        out_shape=(
            jax.ShapeDtypeStruct((T, D), BF16),
            jax.ShapeDtypeStruct((T, 2 * HW), BF16),
        ),
        in_specs=[VMEM, VMEM, ANY, ANY, VMEM, VMEM],
        out_specs=(VMEM,) * 2,
        scratch_shapes=[weight, weight, pltpu.SemaphoreType.DMA((2,))],
        compiler_params=params(60),
        cost_estimate=cost(2 * T * D * 2 * HW, 4e6),
        name="project",
    )(x, gain, wk, wv, cosine, sine)


def project_q_kernel(h1_ref, wq_ref, cos_ref, sin_ref, q_ref):
    q_ref[...] = turn(dot(h1_ref[...], wq_ref[...]), cos_ref[...], sin_ref[...]).astype(BF16)


def project_q(h1, wq, cosine, sine):
    return pl.pallas_call(
        project_q_kernel,
        out_shape=jax.ShapeDtypeStruct((T, HW), BF16),
        in_specs=[VMEM] * 4,
        out_specs=VMEM,
        compiler_params=params(16),
        cost_estimate=cost(2 * T * D * HW, 3e6),
        name="project_q",
    )(h1, wq, cosine, sine)


def slots_kernel(routes_ref, dy_ref, dyp_ref, hot_ref, place_ref):
    expert = rows((EXTRA, T))
    routes = routes_ref[...]
    hot = jnp.zeros((EXTRA, T), F32)
    for j in range(TOPK):
        hot = jnp.where(expert == routes[j : j + 1, :], 1.0, hot)
    hot = hot.astype(BF16)
    same = (rows((T, T)) == lanes((T, T))).astype(BF16)
    hot = dot_tn(hot, same)
    hot_ref[...] = hot
    before = (lanes((T, T)) < rows((T, T))).astype(BF16)
    slot = dot(before, hot.astype(BF16))
    slot = jnp.where(hot > 0.5, slot, -1.0).astype(BF16)
    dyp_ref[:, :D] = dy_ref[...]
    dyp_ref[:, D:] = slot
    at = lanes((EXTRA, COUNT))
    spread = (rows((EXTRA, COUNT)) == (at >> 4)).astype(BF16)
    place = dot(slot, spread) == (lanes((T, COUNT)) & (CAP - 1)).astype(F32)
    place_ref[...] = jnp.where(place, 1.0, 0.0).astype(BF16)


def slots(routes, dy):
    return pl.pallas_call(
        slots_kernel,
        out_shape=(
            jax.ShapeDtypeStruct((T, D + EXTRA), BF16),
            jax.ShapeDtypeStruct((T, EXTRA), F32),
            jax.ShapeDtypeStruct((T, COUNT), BF16),
        ),
        in_specs=[VMEM] * 2,
        out_specs=(VMEM,) * 3,
        compiler_params=params(12),
        cost_estimate=cost(2 * T * T * COUNT, 1e6),
        name="slots",
    )(routes, dy)


def masks_kernel(info_ref, docs_ref, qbias_ref, kbias_ref):
    chip, core = info_ref[0], info_ref[1]
    border = jnp.sum(jnp.where(docs_ref[...] == 0, 1.0, 0.0), axis=1, keepdims=True).astype(jnp.int32)
    lane = lanes((1, KEYS))
    own = chip * 2 * T + core * T + rows((T, 1))

    def bias(query, key, there):
        seen = key <= query
        for j in range(2):
            first, last = info_ref[3 + j], info_ref[5 + j]
            seen |= (query >= first) & (query < last) & (key >= first) & (key < last)
        same = (query >= border) == (key >= border)
        return jnp.where(seen & same & there, 0.0, NEG_FILL).astype(F32)

    qbias_ref[...] = bias(own, info_ref[2] + lane, lane >= 0)
    other = (lane >= KEYS // 2).astype(jnp.int32)
    step = (lane - other * (KEYS // 2)) >> 7
    query = (chip + step) * 2 * T + (core ^ other) * T + (lane & (T - 1))
    kbias_ref[...] = bias(query, own, query < BLOCKS * T)


def masks(info, docs):
    bias = jax.ShapeDtypeStruct((T, KEYS), F32)
    return pl.pallas_call(
        masks_kernel,
        out_shape=(bias, bias),
        in_specs=[SMEM, VMEM],
        out_specs=(VMEM,) * 2,
        compiler_params=params(12),
        cost_estimate=cost(40 * T * KEYS, 2e6),
        name="masks",
    )(info, docs)


WINDOW = 10


def attend_kernel(at_ref, q_ref, kv_hbm, bias_ref, wo_ref, o_ref, part_ref, stats_ref, kvs, sems):
    start = pl.multiple_of(at_ref[0], T)
    copies = []
    for i in range(2):
        cut = pl.ds(i * HW, HW)
        copies.append(pltpu.make_async_copy(kv_hbm.at[pl.ds(start, KEYS), cut], kvs.at[:, cut], sems.at[i]))
        copies[i].start()
    copies[0].wait()
    stats, outs = [], []
    for h in range(HEADS):
        cut = slice(h * 128, (h + 1) * 128)
        vcut = slice(HW + h * 128, HW + (h + 1) * 128)
        q = q_ref[:, cut]
        s = dot_nt(q, kvs[:, cut]) * SCALE + bias_ref[...]
        high = jnp.max(s, axis=1, keepdims=True)
        e = jnp.exp(s - high)
        total = jnp.sum(e, axis=1, keepdims=True)
        p = (e * (1.0 / total)).astype(BF16)
        if h == 0:
            copies[1].wait()
        outs.append(dot(p, kvs[:, vcut]))
        stats += list(split3((high + jnp.log(total)) * (-1.0 / SCALE)))
    o = jnp.concatenate(outs, axis=1)
    o_ref[...] = o
    part_ref[...] = dot(o.astype(BF16), wo_ref[...]).astype(BF16)
    stats_ref[...] = per_token([None] * (3 * HEADS) + stats)


def attend(at, q, kv_all, bias, wo):
    return pl.pallas_call(
        attend_kernel,
        out_shape=(
            jax.ShapeDtypeStruct((T, HW), F32),
            jax.ShapeDtypeStruct((T, D), BF16),
            jax.ShapeDtypeStruct((T, EXTRA), BF16),
        ),
        in_specs=[SMEM, VMEM, ANY, VMEM, VMEM],
        out_specs=(VMEM,) * 3,
        scratch_shapes=[pltpu.VMEM((KEYS, 2 * HW), BF16), pltpu.SemaphoreType.DMA((2,))],
        compiler_params=params(60),
        cost_estimate=cost(4 * T * KEYS * HW + 2 * T * HW * D, 6e6),
        name="attend",
    )(at, q, kv_all, bias, wo)


def gate_kernel(x_ref, a_ref, b_ref, g_ref, wr_ref, hot_ref, r_ref, h2p_ref, gates_ref):
    r = x_ref[...].astype(F32) + (a_ref[...].astype(F32) + b_ref[...].astype(F32))
    r_ref[...] = r
    inverse = lax.rsqrt(jnp.mean(r * r, axis=1, keepdims=True) + EPSILON)
    h2 = (r * inverse * g_ref[...]).astype(BF16)
    hot = hot_ref[...] > 0.5
    logits = jnp.where(hot, dot_nt(h2, wr_ref[...]), NEG_FILL)
    e = jnp.where(hot, jnp.exp(logits - jnp.max(logits, axis=1, keepdims=True)), 0.0)
    gates = e / jnp.sum(e, axis=1, keepdims=True)
    gates_ref[...] = gates
    first = gates.astype(BF16).astype(F32)
    h2p_ref[:, :D] = h2
    h2p_ref[:, D:] = (first + pltpu.roll(gates - first, 64, 1)).astype(BF16)


def gate(x, a, b, gain, wr, hot):
    return pl.pallas_call(
        gate_kernel,
        out_shape=(
            jax.ShapeDtypeStruct((T, D), F32),
            jax.ShapeDtypeStruct((T, D + EXTRA), BF16),
            jax.ShapeDtypeStruct((T, EXTRA), F32),
        ),
        in_specs=[VMEM] * 6,
        out_specs=(VMEM,) * 3,
        compiler_params=params(24),
        cost_estimate=cost(2 * T * D * 128, 2e6),
        name="gate",
    )(x, a, b, gain, wr, hot)


def silu_parts(gate_pre):
    sigmoid = 1.0 / (1.0 + jnp.exp(-gate_pre))
    return gate_pre * sigmoid, sigmoid * (1.0 + gate_pre * (1.0 - sigmoid))


def shared_kernel(h2p_ref, dy_ref, wg_ref, wu_ref, wd_ref, out_ref, dh_ref, sh_ref, dsg_ref, dsu_ref):
    h2 = h2p_ref[:, :D]
    sg = dot_nt(h2, wg_ref[...])
    su = dot_nt(h2, wu_ref[...])
    act, slope = silu_parts(sg)
    sh = (act * su).astype(BF16)
    sh_ref[...] = sh
    out_ref[...] = dot(sh, wd_ref[...])
    dsh = dot_nt(dy_ref[...], wd_ref[...])
    dsg = (dsh * su * slope).astype(BF16)
    dsu = (dsh * act).astype(BF16)
    dsg_ref[...] = dsg
    dsu_ref[...] = dsu
    dh_ref[...] = dot(dsg, wg_ref[...]) + dot(dsu, wu_ref[...])


def shared(h2p, dy, wg, wu, wd):
    hidden = jax.ShapeDtypeStruct((T, FF), BF16)
    return pl.pallas_call(
        shared_kernel,
        out_shape=(jax.ShapeDtypeStruct((T, D), F32), jax.ShapeDtypeStruct((T, D), F32), hidden, hidden, hidden),
        in_specs=[VMEM] * 5,
        out_specs=(VMEM,) * 5,
        compiler_params=params(24),
        cost_estimate=cost(1e6, 1e5),
        name="shared",
    )(h2p, dy, wg, wu, wd)


PAIR = 2 * E * CAP


def dispatch_kernel(rank_ref, dy_ref, hot_ref, out_ref):
    rank = rank_ref[0]
    spread = (rows((EXTRA, PAIR)) == rank * E + ((lanes((EXTRA, PAIR)) & (E * CAP - 1)) >> 4)).astype(BF16)
    place = (lanes((2 * T, PAIR)) & (CAP - 1)).astype(F32)
    own = (lanes((2 * T, PAIR)) >= E * CAP) == (rows((2 * T, PAIR)) >= T)
    for k in range(2):
        at = slice(k * 2 * T, (k + 1) * 2 * T)
        hot = jnp.where(own & (dot(dy_ref[at, D:], spread) == place), 1.0, 0.0).astype(BF16)
        hot_ref[at, :] = hot
        dy = dot_tn(hot, dy_ref[at, :D]).astype(BF16)
        for j in range(2):
            to = slice((k * 2 + j) * CAP, (k * 2 + j + 1) * CAP)
            for i in range(E):
                out_ref[i, to, :] = dy[(j * E + i) * CAP : (j * E + i + 1) * CAP]


def dispatch(rank, dy_all):
    return pl.pallas_call(
        dispatch_kernel,
        out_shape=(
            jax.ShapeDtypeStruct((BLOCKS * T, PAIR), BF16),
            jax.ShapeDtypeStruct((E, BLOCKS * CAP, D), BF16),
        ),
        grid=(BLOCKS // 4,),
        in_specs=[SMEM, pl.BlockSpec((4 * T, D + EXTRA), lambda k: (k, 0))],
        out_specs=(pl.BlockSpec((4 * T, PAIR), lambda k: (k, 0)), pl.BlockSpec((E, 4 * CAP, D), lambda k: (0, k, 0))),
        compiler_params=params(60, dimension_semantics=("arbitrary",)),
        cost_estimate=cost(2 * BLOCKS * T * PAIR * D, 1e7),
        name="dispatch",
    )(rank, dy_all)


def experts_kernel(rank_ref, hot_ref, dy_ref, h2_hbm, wg_ref, wu_ref, wd_ref, out_ref, grads_hbm, h2s, xs, gs, stage, sems, outs):
    e = pl.program_id(0)
    rank = rank_ref[0]
    slot = e & 1

    def result(slot, group):
        to = pl.ds(pl.multiple_of(group * 2 * FF, 128), 2 * FF)
        return pltpu.make_async_copy(stage.at[slot], grads_hbm.at[:, to], outs.at[slot])

    @pl.when(e == 0)
    def _():
        copies = []
        for k in range(0, BLOCKS, 2):
            at = pl.ds(k * T, 2 * T)
            copies.append(pltpu.make_async_copy(h2_hbm.at[at, :], h2s.at[at, :], sems.at[k // 2]))
        for copy in copies:
            copy.start()
        named = rank * E + ((rows((PAIR, EXTRA)) & (E * CAP - 1)) >> 4)
        column = lanes((PAIR, EXTRA))
        mine = (column == named) | (column == named + 64)
        for k in range(0, BLOCKS, 2):
            at = slice(k * T, (k + 2) * T)
            copies[k // 2].wait()
            x = dot_tn(hot_ref[at, :], h2s[at, :])
            g = jnp.sum(jnp.where(mine, x[:, D:], 0.0), axis=1, keepdims=True)
            g = jnp.broadcast_to(g, (PAIR, 128))
            x = x[:, :D].astype(BF16)
            for j in range(2):
                to = slice((k + j) * CAP, (k + j + 1) * CAP)
                for i in range(E):
                    cut = slice((j * E + i) * CAP, (j * E + i + 1) * CAP)
                    xs[i, to, :] = x[cut]
                    gs[i, to, :] = g[cut]

    x = xs[e]
    g = gs[e][:, :1]
    eg = dot_nt(x, wg_ref[0])
    eu = dot_nt(x, wu_ref[0])
    act, slope = silu_parts(eg)
    eh = act * eu
    geh = (g * eh).astype(BF16)
    eh = eh.astype(BF16)
    dy = dy_ref[0]
    deh = dot_nt(dy, wd_ref[0])
    dgate = jnp.sum(eh.astype(F32) * deh, axis=1, keepdims=True)
    deh = g * deh
    deg = (deh * eu * slope).astype(BF16)
    deu = (deh * act).astype(BF16)
    shape = (BLOCKS, CAP, -1)
    out_ref[:, 0, :, D + EXTRA :] = (g * dot(eh, wd_ref[0])).astype(BF16).reshape(shape)
    out_ref[:, 0, :, :D] = (dot(deg, wg_ref[0]) + dot(deu, wu_ref[0])).astype(BF16).reshape(shape)
    column = lanes((BLOCKS * CAP, EXTRA))
    expert = rank * E + e
    first = dgate.astype(BF16).astype(F32)
    placed = jnp.where(column == expert, first, jnp.where(column == expert + 64, dgate - first, 0.0))
    out_ref[:, 0, :, D : D + EXTRA] = placed.astype(BF16).reshape(shape)

    @pl.when(e >= 2)
    def _():
        result(slot, e - 2).wait()

    dgu = jnp.concatenate([deg, deu], axis=1)
    for r in range(0, D, 256):
        stage[slot, r : r + 256, :] = dot_tn(x[:, r : r + 256], dgu).astype(BF16)
    result(slot, e).start()

    @pl.when(slot == 0)
    def _():
        @pl.when(e == 2)
        def _():
            result(2, E).wait()

        for r in range(0, D, 256):
            stage[2, r : r + 256, :FF] = dot_tn(dy[:, r : r + 256], geh).astype(BF16)

    @pl.when(slot == 1)
    def _():
        for r in range(0, D, 256):
            stage[2, r : r + 256, FF:] = dot_tn(dy[:, r : r + 256], geh).astype(BF16)
        result(2, E + (e >> 1)).start()

    @pl.when(e == E - 1)
    def _():
        result(0, E - 2).wait()
        result(1, E - 1).wait()
        result(2, E + 1).wait()


GRADS = 6
BACK = D + EXTRA + D


def experts(rank, hot, dy, h2_all, wg, wu, wd):
    n = BLOCKS * CAP
    per = lambda shape: pl.BlockSpec((1, *shape), lambda e: (e, 0, 0))
    held = lambda shape: pl.BlockSpec(shape, lambda e: (0,) * len(shape), pipeline_mode=pl.Buffered(1))
    return pl.pallas_call(
        experts_kernel,
        out_shape=(
            jax.ShapeDtypeStruct((BLOCKS, E, CAP, BACK), BF16),
            jax.ShapeDtypeStruct((D, GRADS * 2 * FF), BF16),
        ),
        grid=(E,),
        in_specs=[SMEM, held((BLOCKS * T, PAIR)), per((n, D)), ANY, per((FF, D)), per((FF, D)), per((FF, D))],
        out_specs=(pl.BlockSpec((BLOCKS, 1, CAP, BACK), lambda e: (0, e, 0, 0)), ANY),
        scratch_shapes=[
            pltpu.VMEM((BLOCKS * T, D + EXTRA), BF16),
            pltpu.VMEM((E, n, D), BF16),
            pltpu.VMEM((E, n, 128), F32),
            pltpu.VMEM((3, D, 2 * FF), BF16),
            pltpu.SemaphoreType.DMA((BLOCKS // 2,)),
            pltpu.SemaphoreType.DMA((3,)),
        ],
        compiler_params=params(58, dimension_semantics=("arbitrary",)),
        cost_estimate=cost(2 * E * n * D * FF * 9, 5e7),
        name="experts",
    )(rank, hot, dy, h2_all, wg, wu, wd)


def combine_kernel(place_ref, back_ref, dh_ref, out_ref, back_out_ref, mixed_ref):
    total = dot(place_ref[...], back_ref[...])
    back_out_ref[:, :D] = (total[:, :D] + dh_ref[...]).astype(BF16)
    back_out_ref[:, D:] = total[:, D : D + EXTRA].astype(BF16)
    mixed_ref[...] = (total[:, D + EXTRA :] + out_ref[...]).astype(BF16)


def combine(place, back, dh, out):
    return pl.pallas_call(
        combine_kernel,
        out_shape=(jax.ShapeDtypeStruct((T, D + EXTRA), BF16), jax.ShapeDtypeStruct((T, D), BF16)),
        in_specs=[VMEM] * 4,
        out_specs=(VMEM,) * 2,
        compiler_params=params(24),
        cost_estimate=cost(2 * T * COUNT * BACK, 7e6),
        name="combine",
    )(place, back.reshape(COUNT, BACK), dh, out)


def middle_kernel(a_ref, b_ref, r_ref, dy_ref, h2p_ref, gates_ref, g_ref, wr_ref, wo_ref, o_ref, stats_ref, dr_ref, da_ref, dop_ref, dlog_ref, gain_ref):
    both = a_ref[...].astype(F32) + b_ref[...].astype(F32)
    gates = gates_ref[...]
    dgate = both[:, D:] + pltpu.roll(both[:, D:], 64, 1)
    dsel = gates * (dgate - jnp.sum(gates * dgate, axis=1, keepdims=True))
    dlog = dsel.astype(BF16)
    dlog_ref[...] = dlog
    dh2 = both[:, :D] + dot(dlog, wr_ref[...])
    r = r_ref[...]
    inverse = lax.rsqrt(jnp.mean(r * r, axis=1, keepdims=True) + EPSILON)
    unit = r * inverse
    gain_ref[...] = (dh2 * unit).astype(BF16)
    e2 = dh2 * g_ref[...]
    dr = dy_ref[...].astype(F32) + inverse * (e2 - unit * jnp.mean(e2 * unit, axis=1, keepdims=True))
    dr_ref[...] = dr
    da = dr.astype(BF16)
    da_ref[...] = da
    do = dot_nt(da, wo_ref[...]).astype(BF16)
    dop_ref[:, :HW] = do
    stats = []
    both = do.astype(F32) * o_ref[...]
    for h in range(HEADS):
        stats += list(split3(-jnp.sum(both[:, h * 128 : (h + 1) * 128], axis=1, keepdims=True)))
    dop_ref[:, HW:] = per_token(stats) + stats_ref[...]


def middle(a, b, r, dy, h2p, gates, gain, wr, wo, o, stats):
    return pl.pallas_call(
        middle_kernel,
        out_shape=(
            jax.ShapeDtypeStruct((T, D), F32),
            jax.ShapeDtypeStruct((T, D), BF16),
            jax.ShapeDtypeStruct((T, HW + EXTRA), BF16),
            jax.ShapeDtypeStruct((T, EXTRA), BF16),
            jax.ShapeDtypeStruct((T, D), BF16),
        ),
        in_specs=[VMEM] * 11,
        out_specs=(VMEM,) * 5,
        compiler_params=params(24),
        cost_estimate=cost(2 * T * D * (HW + 128), 5e6),
        name="middle",
    )(a, b, r, dy, h2p, gates, gain, wr, wo, o, stats)


HALF = 3 * HW // 2
PADDED = 1024


def attend_back_kernel(*refs):
    at_ref, q_hbm, kv_hbm, do_hbm, refs = refs[0], refs[1], refs[2], refs[3 : 3 + WINDOW], refs[3 + WINDOW :]
    w_hbm, refs = refs[:3], refs[3:]
    kv_ref, qbias_ref, kbias_ref, cos_ref, sin_ref, mine_ref, theirs_ref, part_ref, kvs, qs, dos, ws, sems = refs
    keys_at = pl.ds(pl.multiple_of(at_ref[WINDOW], T), KEYS)
    copies = [pltpu.make_async_copy(v, dos.at[i], sems.at[i]) for i, v in enumerate(do_hbm)]
    for i in range(WINDOW):
        source = q_hbm.at[pl.ds(pl.multiple_of(at_ref[i], T), T), :]
        copies.append(pltpu.make_async_copy(source, qs.at[i], sems.at[WINDOW + i]))
    copies += [pltpu.make_async_copy(v, ws.at[i], sems.at[2 * WINDOW + i]) for i, v in enumerate(w_hbm)]
    copies.append(pltpu.make_async_copy(kv_hbm.at[keys_at, :], kvs, sems.at[2 * WINDOW + 3]))
    early = [2 * WINDOW + 3, 0, WINDOW]
    late = [i for i in range(2 * WINDOW) if i not in early]
    weights = [2 * WINDOW, 2 * WINDOW + 1, 2 * WINDOW + 2]
    for i in early + late + weights:
        copies[i].start()
    for i in early:
        copies[i].wait()
    lane = lanes((T, EXTRA))
    extra = dos[0, :, HW:]
    stats = extra.astype(F32)
    side = lambda parts: jnp.concatenate(parts, axis=1)
    block = lambda v, i: v[:, i * T : (i + 1) * T]
    every = range(WINDOW)
    heads = [(slice(h * 128, (h + 1) * 128), slice(HW + h * 128, HW + (h + 1) * 128)) for h in range(HEADS)]
    its = lambda first: (lane >= first) & (lane < first + 3)
    dqs, dks, dvs = [], [], []
    for h, (cut, vcut) in enumerate(heads):
        less_dot = jnp.sum(jnp.where(its(3 * h), stats, 0.0), axis=1, keepdims=True)
        less = jnp.sum(jnp.where(its(3 * (HEADS + h)), stats, 0.0), axis=1, keepdims=True)
        q, do = qs[0, :, cut], dos[0, :, cut]
        p = jnp.exp((dot_nt(q, kvs[:, cut]) + less) * SCALE + qbias_ref[...])
        dp = dot_nt(do, kvs[:, vcut]) + less_dot
        ds = (p * dp * SCALE).astype(BF16)
        dqs.append(dot(ds, kvs[:, cut]))
    for i in late:
        copies[i].wait()
    for h, (cut, vcut) in enumerate(heads):
        k_wide = side([kv_ref[:, cut], its(3 * (HEADS + h)).astype(BF16)])
        v_wide = side([kv_ref[:, vcut], its(3 * h).astype(BF16)])
        pt = side([dot_nt(k_wide, side([qs[i, :, cut], dos[i, :, HW:]])) for i in every])
        pt = jnp.exp(pt * SCALE + kbias_ref[...])
        dpt = side([dot_nt(v_wide, side([dos[i, :, cut], dos[i, :, HW:]])) for i in every])
        dst = (pt * dpt * SCALE).astype(BF16)
        pt = pt.astype(BF16)
        dks.append(sum(dot(block(dst, i), qs[i, :, cut]) for i in every))
        dvs.append(sum(dot(block(pt, i), dos[i, :, cut]) for i in every))
    cosine, sine = cos_ref[...], -sin_ref[...]
    dq = turn(side(dqs), cosine, sine).astype(BF16)
    dk = turn(side(dks), cosine, sine).astype(BF16)
    dv = side(dvs).astype(BF16)
    dqkv = side([dq, dk, dv])
    none = jnp.zeros((T, PADDED - HALF), BF16)
    low, high = side([dqkv[:, :HALF], none]), side([dqkv[:, HALF:], none])
    first = at_ref[WINDOW + 1] == 0
    mine_ref[...] = jnp.where(first, low, high)
    theirs_ref[...] = jnp.where(first, high, low)
    for i in weights:
        copies[i].wait()
    part = dot_nt(dq, ws[0]) + dot_nt(dk, ws[1]) + dot_nt(dv, ws[2])
    part_ref[...] = part.astype(BF16)


def attend_back(at, q_all, kv_all, dos, kv, qbias, kbias, cosine, sine, wq, wk, wv):
    return pl.pallas_call(
        attend_back_kernel,
        out_shape=(
            jax.ShapeDtypeStruct((T, PADDED), BF16),
            jax.ShapeDtypeStruct((T, PADDED), BF16),
            jax.ShapeDtypeStruct((T, D), BF16),
        ),
        in_specs=[SMEM] + [ANY] * (5 + WINDOW) + [VMEM] * 5,
        out_specs=(VMEM,) * 3,
        scratch_shapes=[
            pltpu.VMEM((KEYS, 2 * HW), BF16),
            pltpu.VMEM((WINDOW, T, HW), BF16),
            pltpu.VMEM((WINDOW, T, HW + EXTRA), BF16),
            pltpu.VMEM((3, D, HW), BF16),
            pltpu.SemaphoreType.DMA((2 * WINDOW + 4,)),
        ],
        compiler_params=params(56),
        cost_estimate=cost(16 * T * KEYS * HW + 6 * T * HW * D, 2e7),
        name="attend_back",
    )(at, q_all, kv_all, *dos, wq, wk, wv, kv, qbias, kbias, cosine, sine)


WIDE = 384


def chunks_kernel(h1_ref, out_ref):
    at = lanes((1, WIDE))
    part = jnp.zeros((1, WIDE), jnp.int32)
    for j in range(1, 8):
        part += (at >= 40 * j).astype(jnp.int32)
    for z in range(4):
        source = part * 160 + z * 40 + (at - part * 40)
        place = ((rows((D, WIDE)) == source) & (at < 320)).astype(BF16)
        out_ref[z] = dot(h1_ref[...], place).astype(BF16)


def chunks(h1):
    return pl.pallas_call(
        chunks_kernel,
        out_shape=jax.ShapeDtypeStruct((4, h1.shape[0], WIDE), BF16),
        in_specs=[VMEM],
        out_specs=VMEM,
        compiler_params=params(16),
        cost_estimate=cost(2 * h1.shape[0] * D * 4 * WIDE, 2e6),
        name="chunks",
    )(h1)


SUM_B, SUM_A = 384, 768
USED_B, USED_A = (HW + 64) // 2, 3 * FF // 2
GRADS_WIDTH = GRADS * 2 * FF


def projection_grads_kernel(*refs):
    left_hbm, parts, grads_hbm = refs[0], refs[1:6], refs[6]
    out_ref, expert_outs, (left, right, grads, ready, sems, out_sems) = refs[7], refs[8:11], refs[11:]
    copies = [pltpu.make_async_copy(grads_hbm, grads, sems.at[6])]
    copies.append(pltpu.make_async_copy(left_hbm, left, sems.at[0]))
    at = 0
    for i, part in enumerate(parts):
        n = part.shape[0]
        copies.append(pltpu.make_async_copy(part, right.at[pl.ds(at, n), :], sems.at[1 + i]))
        at += n
    for copy in copies:
        copy.start()
    copies[0].wait()
    writes = []
    for e in range(E):
        gate_up = grads[:, e * 2 * FF : (e + 1) * 2 * FF].astype(F32)
        start = (2 * E + e) * FF
        if e % 2 == 0:
            down = grads[:, start : start + 2 * FF].astype(F32)
        ready[e % 2, 0] = gate_up[:, :FF]
        ready[e % 2, 1] = gate_up[:, FF:]
        ready[e % 2, 2] = down[:, (e % 2) * FF : (e % 2 + 1) * FF]
        for i, out in enumerate(expert_outs):
            writes.append(pltpu.make_async_copy(ready.at[e % 2, i], out.at[e], out_sems.at[e % 2, i]))
            writes[-1].start()
        if e in (1, 2):
            for write in writes[3 * (e - 1) : 3 * e]:
                write.wait()
    for copy in copies[1:]:
        copy.wait()
    out_ref[...] = dot_tn(left[...], right[...])[:320].astype(BF16)
    for write in writes[6:]:
        write.wait()


def projection_grads(left, parts, grads):
    expert = jax.ShapeDtypeStruct((E, D // 4, FF), F32)
    return pl.pallas_call(
        projection_grads_kernel,
        out_shape=(jax.ShapeDtypeStruct((320, PADDED), BF16), expert, expert, expert),
        in_specs=[ANY] * 7,
        out_specs=(VMEM, ANY, ANY, ANY),
        scratch_shapes=[
            pltpu.VMEM((8 * T, WIDE), BF16),
            pltpu.VMEM((8 * T, PADDED), BF16),
            pltpu.VMEM((320, GRADS_WIDTH), BF16),
            pltpu.VMEM((2, 3, 320, FF), F32),
            pltpu.SemaphoreType.DMA((7,)),
            pltpu.SemaphoreType.DMA((2, 3)),
        ],
        compiler_params=params(56),
        cost_estimate=cost(2 * 8 * T * WIDE * PADDED, 2e7),
        name="projection_grads",
    )(left, *parts, grads)


def other_sums_kernel(left_ref, right_ref, sums_ref, out_ref):
    out_ref[:, :USED_A] = sums_ref[:, :USED_A]
    out_ref[:, USED_A:] = dot_tn(left_ref[...], right_ref[...])[:, :USED_B].astype(BF16)


def other_sums(left, right, sums):
    return pl.pallas_call(
        other_sums_kernel,
        out_shape=jax.ShapeDtypeStruct((D, USED_A + USED_B), BF16),
        in_specs=[VMEM] * 3,
        out_specs=VMEM,
        compiler_params=params(24),
        cost_estimate=cost(2 * left.shape[0] * D * SUM_B, 8e6),
        name="other_sums",
    )(left, right, sums)


def own_and_others(core_ref, parts_ref, keep_ref, give_ref):
    total = parts_ref[0].astype(F32)
    for i in range(1, 8):
        total += parts_ref[i].astype(F32)
    first = core_ref[0] == 0
    keep_ref[...] = jnp.where(first, total[:20], total[20:])
    give_ref[...] = jnp.where(first, total[20:], total[:20])
    return total


def add_up_kernel(core_ref, parts_ref, keep_ref, give_ref):
    own_and_others(core_ref, parts_ref, keep_ref, give_ref)


def add_up_gain_kernel(core_ref, parts_ref, weight_ref, keep_ref, give_ref, gain_ref):
    total = own_and_others(core_ref, parts_ref, keep_ref, give_ref)
    gain_ref[...] = jnp.broadcast_to(jnp.sum(total * weight_ref[...], axis=1, keepdims=True), (40, 128))


def add_up(core, parts, *weight):
    half = jax.ShapeDtypeStruct((20, parts.shape[2]), F32)
    outs = (half, half) + (jax.ShapeDtypeStruct((40, 128), F32),) * len(weight)
    return pl.pallas_call(
        add_up_gain_kernel if weight else add_up_kernel,
        out_shape=outs,
        in_specs=[SMEM] + [VMEM] * (1 + len(weight)),
        out_specs=(VMEM,) * len(outs),
        compiler_params=params(24),
        cost_estimate=cost(1e6, 2e6),
        name="add_up",
    )(core, parts, *weight)


def dense_outputs_kernel(core_ref, keep_ref, got_ref, keep2_ref, got2_ref, g0, g1, g2, g3, q_ref, k_ref, v_ref, o_ref, router_ref, gate_ref, up_ref, down_ref, gains_ref):
    first = core_ref[0] == 0

    def halves(keep, got):
        low, high = jnp.where(first, keep, got), jnp.where(first, got, keep)
        return lambda at, n: jnp.concatenate([low[:, at : at + n], high[:, at : at + n]], axis=1)

    qkv = halves(keep_ref[...], got_ref[...])(0, HALF)
    q_ref[...] = qkv[:, :HW]
    k_ref[...] = qkv[:, HW : 2 * HW]
    v_ref[...] = qkv[:, 2 * HW :]
    columns = halves(keep2_ref[...], got2_ref[...])
    other = columns(USED_A, USED_B)
    o_ref[...] = other[:, :HW]
    router_ref[...] = other[:, HW : HW + 63]
    expert = columns(0, USED_A)
    gate_ref[...] = expert[:, :FF]
    up_ref[...] = expert[:, FF : 2 * FF]
    down_ref[...] = expert[:, 2 * FF :]
    gain = g0[...] + g1[...] + g2[...] + g3[...]
    gain = jnp.where(first, gain[:20], gain[20:])
    lane = lanes((20, 128))
    both = jnp.where(lane == 0, gain, 0.0) + jnp.where(lane == 1, other[:, HW + 63 :], 0.0)
    same = (rows((20, 20)) == lanes((20, 20))).astype(F32)
    gains_ref[...] = lax.dot_general(both, same, (((0,), (0,)), ((), ())), precision=lax.Precision.HIGHEST, preferred_element_type=F32)


def dense_outputs(core, qkv, others, gains):
    out = lambda n: jax.ShapeDtypeStruct((20, n), F32)
    return pl.pallas_call(
        dense_outputs_kernel,
        out_shape=(out(HW), out(HW), out(HW), out(HW), out(63), out(FF), out(FF), out(FF), jax.ShapeDtypeStruct((128, 20), F32)),
        in_specs=[SMEM] + [VMEM] * 8,
        out_specs=(VMEM,) * 9,
        compiler_params=params(16),
        cost_estimate=cost(1e6, 1e6),
        name="dense_outputs",
    )(core, *qkv, *others, *gains)


def ep_perm(dyl, dz, dc):
    at = lambda yl, z, c: (yl * 4 + z) * 2 + c
    return [
        (at(yl, z, c), at(yl ^ dyl, (z + dz) % 4, c ^ dc)) for yl in range(2) for z in range(4) for c in range(2)
    ]


CORE = ep_perm(0, 0, 1)


def send(value, perm):
    return lax.ppermute(value, EP, perm)


def swap(value, axis):
    return lax.ppermute(value, axis, [(0, 1), (1, 0)])


def to_owners(value):
    return lax.all_to_all(value, EP, split_axis=0, concat_axis=0, tiled=True)


def window_perm(step, back):
    pairs = [(i, i + step) for i in range(8 - step) if i + step < 5 or i >= 3]
    pairs = [(j, i) if back else (i, j) for i, j in pairs]
    return [(2 * i + c, 2 * j + c) for i, j in pairs for c in range(2)]


def window(value, back):
    own = [value] + [send(value, window_perm(step, back)) for step in range(1, 5)]
    return own


def with_other_core(own):
    return list(own) + [send(v, CORE) for v in own]


def both_cores(left):
    return jnp.concatenate([left, swap(left, "c")], axis=0)


def dense_right(right, core):
    half = right.shape[1] // 2
    mine = jnp.where(core == 0, right[:, :half], right[:, half:])
    theirs = jnp.where(core == 0, right[:, half:], right[:, :half])
    return both_cores_of(mine, theirs)


def both_cores_of(mine, theirs):
    return jnp.concatenate([mine, swap(theirs, "c")], axis=0)


def products(left, right):
    return dot_tn(left, right).astype(BF16)


UP = [(0, 1), (1, 2), (2, 3), (3, 0)]
DOWN = [(1, 0), (2, 1), (3, 2), (0, 3)]


def z_gather_far(below, above):
    half = below.shape[0] // 2
    return lax.ppermute(below[:half], "z", UP), lax.ppermute(above[half:], "z", DOWN)


def xy_sum(part):
    parts = lax.all_to_all(part, ("x", "yl"), split_axis=0, concat_axis=0, tiled=True)
    return jnp.sum(parts.astype(F32), axis=0)


def rotation(positions):
    half = HEAD_DIM // 2
    frequency = BASE ** (-(jnp.arange(half, dtype=F32) * 2.0) / HEAD_DIM)
    angles = positions.astype(F32)[:, None] * frequency[None, :]
    cosine, sine = jnp.cos(angles), jnp.sin(angles)
    return jnp.concatenate([cosine, cosine], axis=1), jnp.concatenate([-sine, sine], axis=1)


def after(values, ready):
    return lax.optimization_barrier((values, ready))


def local(
    tokens, grad_out, doc_ids, piece_starts, piece_ends, routes, norm1_gain, norm2_gain, query_weight, key_weight, value_weight,
    output_weight, router_weight, shared_gate, shared_up, shared_down, expert_gate, expert_up, expert_down,
):
    core, z = lax.axis_index("c"), lax.axis_index("z")
    rank = lax.axis_index(EP).astype(jnp.int32)
    gain1, gain2 = norm1_gain[None, :], norm2_gain[None, :]
    wr = jnp.pad(router_weight.T, ((0, EXTRA - router_weight.shape[1]), (0, 0)))
    cosine, sine = rotation(rank * T + jnp.arange(T, dtype=jnp.int32))
    keys_at = jnp.where(rank < 10, 0, 768).astype(jnp.int32)
    info = jnp.concatenate([jnp.stack([rank // 2, rank % 2, keys_at]), piece_starts[0], piece_ends[0]]).astype(jnp.int32)
    entry = jnp.arange(WINDOW, dtype=jnp.int32)
    seen_from = jnp.minimum(rank // 2 + entry % 5, 7) * 2 + (rank % 2) ^ (entry // 5)
    group = lambda v: lax.all_gather(v, EP, axis=0, tiled=True)

    h1, kv = project(tokens, norm1_gain, key_weight, value_weight, cosine, sine)
    kv_all = group(kv)
    q = project_q(h1, query_weight, cosine, sine)
    h1_left = lax.all_to_all(chunks(h1), "z", split_axis=0, concat_axis=0, tiled=True)
    h1_left = jnp.stack([h1_left, swap(h1_left, "c")], axis=1)
    pick = lambda i: lax.dynamic_slice_in_dim(h1_left, i % 4, 1, 0)
    h1_left = jnp.concatenate([pick(z), pick(z + 3), pick(z + 1), pick(z + 2)], axis=0)
    dyp, hot, place = slots(routes.T, grad_out)
    qbias, kbias = masks(info, doc_ids)
    at = lax.axis_index("x") * 320 + lax.axis_index("yl") * 160 + z * 40
    here = lambda v: lax.dynamic_slice_in_dim(v, at, 40, 0)
    weight = jnp.concatenate([here(query_weight), here(key_weight), here(value_weight)], axis=1).astype(F32)
    weight = jnp.where(core == 0, weight[:, :HALF], weight[:, HALF:]) / here(norm1_gain)[:, None]
    weight = jnp.pad(weight, ((0, 0), (0, PADDED - HALF)))
    (dyp, q, h1_left, qbias, kbias, weight), kv_all = after((dyp, q, h1_left, qbias, kbias, weight), kv_all)
    dy_all = group(dyp)
    o, part, stats = attend(keys_at[None], q, kv_all, qbias, output_weight)
    r, h2p, gates = gate(tokens, part, swap(part, "yh"), gain2, wr, hot)
    h2_all = group(h2p)
    shared_out, shared_dh, sh, dsg, dsu = shared(h2p, grad_out, shared_gate.T, shared_up.T, shared_down)
    places, dys = dispatch(rank[None], dy_all)

    put = lambda v, before, width: jnp.pad(v, ((0, 0), (before, width - before - v.shape[1])))
    both = 3 * FF // 2
    halves = lambda v, used, padded: jnp.concatenate([put(v[:, :used], 0, padded), put(v[:, used:], 0, padded)], axis=1)
    right = jnp.concatenate([put(jnp.concatenate([dsg, dsu], axis=1), 0, 3 * FF), put(sh, 2 * FF, 3 * FF)], axis=0)
    sums_a = products(
        both_cores(jnp.concatenate([h2p[:, :D], grad_out], axis=0)), dense_right(halves(right, both, 768), core)
    )
    (places, dys, sums_a, late_q), h2_all = after((places, dys, sums_a, q), h2_all)
    q_all = group(late_q)
    back, grads = experts(
        rank[None], places, dys, h2_all, expert_gate.transpose(0, 2, 1), expert_up.transpose(0, 2, 1), expert_down
    )
    grads = lax.psum_scatter(grads, "x", scatter_dimension=0, tiled=True)
    back, mixed = combine(place, to_owners(back.reshape(BLOCKS, E * CAP, BACK)), shared_dh, shared_out)
    dr, da, dop, dlog, gain2_terms = middle(
        back, swap(back, "yh"), r, grad_out, h2p, gates, gain2, wr, output_weight, o, stats
    )
    dos = with_other_core(window(dop, True))

    one = jnp.ones((T, 1), BF16)
    width = HW + 64
    other = jnp.concatenate(
        [put(o.astype(BF16), 0, width), put(dlog[:, :63], HW, width), put(one, width - 1, width)], axis=0
    )
    sums_ab = other_sums(
        both_cores(jnp.concatenate([da, h2p[:, :D], gain2_terms], axis=0)),
        dense_right(halves(other, width // 2, SUM_B), core),
        sums_a,
    )
    (dos, h1_left), sums_ab = after((dos, h1_left.reshape(8 * T, WIDE)), sums_ab)
    sums_ab = sums_ab.reshape(8, 4, 40, USED_A + USED_B).transpose(1, 0, 2, 3).reshape(D, USED_A + USED_B)
    sums_ab = lax.psum_scatter(sums_ab, "z", scatter_dimension=0, tiled=True)

    mine, theirs, dh1_part = attend_back(
        jnp.concatenate([seen_from * T, keys_at[None], core.astype(jnp.int32)[None]]), q_all, kv_all, dos, kv, qbias, kbias, cosine, sine, query_weight, key_weight, value_weight
    )
    right = both_cores_of(mine, theirs)
    (dh1_part, mixed), right = after((dh1_part, mixed), right)
    output = (r + (mixed.astype(F32) + swap(mixed, "yh").astype(F32))).astype(BF16)
    below, above = lax.ppermute(right, "z", UP), lax.ppermute(right, "z", DOWN)
    rights = [right, below, above, *z_gather_far(below, above)]
    sums_c, gate_grads, up_grads, down_grads = projection_grads(h1_left, rights, grads)
    spread_out = lambda v: lax.all_to_all(v.reshape(8, 40, -1), ("x", "yl"), split_axis=0, concat_axis=0, tiled=True)
    parts = spread_out(sums_c)
    dh1 = dh1_part.astype(F32) + swap(dh1_part, "yh").astype(F32)
    x = tokens.astype(F32)
    inverse = lax.rsqrt(jnp.mean(x * x, axis=1, keepdims=True) + EPSILON)
    unit = x * inverse
    e1 = dh1 * gain1
    grad_tokens = dr + inverse * (e1 - unit * jnp.mean(e1 * unit, axis=1, keepdims=True))
    others, (parts, output, grad_tokens) = after(sums_ab, (parts, output, grad_tokens))
    others = spread_out(others)
    which = core.astype(jnp.int32)[None]
    keep, give, gain = add_up(which, parts, weight)
    across = lax.ppermute(gain, ("c", "yh"), [(0, 3), (1, 2), (2, 1), (3, 0)])
    gains = gain, swap(gain, "yh"), swap(gain, "c"), across
    qkv = keep, swap(give, "c")
    (keep, give), gains = after(add_up(which, others), gains)
    dense = dense_outputs(which, qkv, (keep, swap(give, "c")), gains)

    return (
        output,
        grad_tokens,
        dense[8][0],
        dense[8][1],
        dense[0],
        dense[1],
        dense[2],
        dense[3].T,
        dense[4],
        dense[5],
        dense[6],
        dense[7].T,
        gate_grads,
        up_grads,
        down_grads.transpose(0, 2, 1),
    )


def solution(mesh):
    fine = Mesh(mesh.devices.reshape(4, 2, 4, 2, 2), ("x", "yl", "z", "c", "yh"))
    rows64 = ("x", "yl", "z", "c")
    in_specs = (
        P(rows64, None),
        P(rows64, None),
        P("x", None),
        P("x", None),
        P("x", None),
        P(rows64, None),
        P(),
        P(),
        P(None, "yh"),
        P(None, "yh"),
        P(None, "yh"),
        P("yh", None),
        P(),
        P(None, "yh"),
        P(None, "yh"),
        P("yh", None),
        P(EP, None, "yh"),
        P(EP, None, "yh"),
        P(EP, "yh", None),
    )
    out_specs = (
        P(rows64, None),
        P(rows64, None),
        P(rows64),
        P(rows64),
        P(rows64, "yh"),
        P(rows64, "yh"),
        P(rows64, "yh"),
        P("yh", rows64),
        P(rows64, None),
        P(rows64, "yh"),
        P(rows64, "yh"),
        P("yh", rows64),
        P(EP, "x", "yh"),
        P(EP, "x", "yh"),
        P(EP, "yh", "x"),
    )
    return jax.shard_map(local, mesh=fine, in_specs=in_specs, out_specs=out_specs, check_vma=False)
```

```python
import jax
import jax.numpy as jnp
from jax import lax
from jax.experimental import pallas as pl
from jax.experimental.pallas import tpu as pltpu
from jax.sharding import Mesh, PartitionSpec as P

F32 = jnp.float32
BF16 = jnp.bfloat16
HEAD_DIM = 128
TOPK = 7
EPSILON = 1e-06
NEG_FILL = -1e30
BASE = 10000.0
SCALE = HEAD_DIM ** (-0.5)

T = 128
D = 1280
HEADS = 5
HW = HEADS * HEAD_DIM
FF = 448
E = 4
CAP = 16
BLOCKS = 16
KEYS = 1280
COUNT = BLOCKS * E * CAP
EXTRA = 128

EP = ("yl", "z", "c")
VMEM = pl.BlockSpec(memory_space=pltpu.VMEM)
SMEM = pl.BlockSpec(memory_space=pltpu.SMEM)
ANY = pl.BlockSpec(memory_space=pl.ANY)


def params(mib, **more):
    return pltpu.CompilerParams(vmem_limit_bytes=mib << 20, **more)


def cost(flops, moved):
    return pl.CostEstimate(flops=int(flops), bytes_accessed=int(moved), transcendentals=0)


def dot(a, b):
    return lax.dot_general(a, b, (((1,), (0,)), ((), ())), preferred_element_type=F32)


def dot_nt(a, b):
    return lax.dot_general(a, b, (((1,), (1,)), ((), ())), preferred_element_type=F32)


def dot_tn(a, b):
    return lax.dot_general(a, b, (((0,), (0,)), ((), ())), preferred_element_type=F32)


def split3(v):
    first = v.astype(BF16)
    rest = v - first.astype(F32)
    second = rest.astype(BF16)
    return first, second, (rest - second.astype(F32)).astype(BF16)


def lanes(shape):
    return lax.broadcasted_iota(jnp.int32, shape, 1)


def rows(shape):
    return lax.broadcasted_iota(jnp.int32, shape, 0)


def turn(values, cosine, sine):
    parts = []
    for h in range(HEADS):
        z = values[:, h * 128 : (h + 1) * 128]
        parts.append(z * cosine + pltpu.roll(z, 64, 1) * sine)
    return jnp.concatenate(parts, axis=1)


def per_token(columns):
    lane = lanes((T, EXTRA))
    out = jnp.zeros((T, EXTRA), F32)
    for j, column in enumerate(columns):
        if column is not None:
            out = jnp.where(lane == j, column.astype(F32), out)
    return out.astype(BF16)


def project_kernel(x_ref, g_ref, wk_hbm, wv_hbm, cos_ref, sin_ref, h1_ref, kv_ref, wk, wv, sems):
    copies = [pltpu.make_async_copy(a, b, sems.at[i]) for i, (a, b) in enumerate(((wk_hbm, wk), (wv_hbm, wv)))]
    for copy in copies:
        copy.start()
    x = x_ref[...].astype(F32)
    inverse = lax.rsqrt(jnp.mean(x * x, axis=1, keepdims=True) + EPSILON)
    h1 = (x * inverse * g_ref[...][None, :]).astype(BF16)
    h1_ref[...] = h1
    cosine, sine = cos_ref[...], sin_ref[...]
    copies[0].wait()
    kv_ref[:, :HW] = turn(dot(h1, wk[...]), cosine, sine).astype(BF16)
    copies[1].wait()
    kv_ref[:, HW:] = dot(h1, wv[...]).astype(BF16)


def project(x, gain, wk, wv, cosine, sine):
    weight = pltpu.VMEM((D, HW), BF16)
    return pl.pallas_call(
        project_kernel,
        out_shape=(
            jax.ShapeDtypeStruct((T, D), BF16),
            jax.ShapeDtypeStruct((T, 2 * HW), BF16),
        ),
        in_specs=[VMEM, VMEM, ANY, ANY, VMEM, VMEM],
        out_specs=(VMEM,) * 2,
        scratch_shapes=[weight, weight, pltpu.SemaphoreType.DMA((2,))],
        compiler_params=params(60),
        cost_estimate=cost(2 * T * D * 2 * HW, 4e6),
        name="project",
    )(x, gain, wk, wv, cosine, sine)


def project_q_kernel(h1_ref, wq_ref, cos_ref, sin_ref, q_ref):
    q_ref[...] = turn(dot(h1_ref[...], wq_ref[...]), cos_ref[...], sin_ref[...]).astype(BF16)


def project_q(h1, wq, cosine, sine):
    return pl.pallas_call(
        project_q_kernel,
        out_shape=jax.ShapeDtypeStruct((T, HW), BF16),
        in_specs=[VMEM] * 4,
        out_specs=VMEM,
        compiler_params=params(16),
        cost_estimate=cost(2 * T * D * HW, 3e6),
        name="project_q",
    )(h1, wq, cosine, sine)


def slots_kernel(routes_ref, dy_ref, dyp_ref, hot_ref, place_ref):
    expert = rows((EXTRA, T))
    routes = routes_ref[...]
    hot = jnp.zeros((EXTRA, T), F32)
    for j in range(TOPK):
        hot = jnp.where(expert == routes[j : j + 1, :], 1.0, hot)
    hot = hot.astype(BF16)
    same = (rows((T, T)) == lanes((T, T))).astype(BF16)
    hot = dot_tn(hot, same)
    hot_ref[...] = hot
    before = (lanes((T, T)) < rows((T, T))).astype(BF16)
    slot = dot(before, hot.astype(BF16))
    slot = jnp.where(hot > 0.5, slot, -1.0).astype(BF16)
    dyp_ref[:, :D] = dy_ref[...]
    dyp_ref[:, D:] = slot
    at = lanes((EXTRA, COUNT))
    spread = (rows((EXTRA, COUNT)) == (at >> 4)).astype(BF16)
    place = dot(slot, spread) == (lanes((T, COUNT)) & (CAP - 1)).astype(F32)
    place_ref[...] = jnp.where(place, 1.0, 0.0).astype(BF16)


def slots(routes, dy):
    return pl.pallas_call(
        slots_kernel,
        out_shape=(
            jax.ShapeDtypeStruct((T, D + EXTRA), BF16),
            jax.ShapeDtypeStruct((T, EXTRA), F32),
            jax.ShapeDtypeStruct((T, COUNT), BF16),
        ),
        in_specs=[VMEM] * 2,
        out_specs=(VMEM,) * 3,
        compiler_params=params(12),
        cost_estimate=cost(2 * T * T * COUNT, 1e6),
        name="slots",
    )(routes, dy)


def masks_kernel(info_ref, docs_ref, qbias_ref, kbias_ref):
    chip, core = info_ref[0], info_ref[1]
    border = jnp.sum(jnp.where(docs_ref[...] == 0, 1.0, 0.0), axis=1, keepdims=True).astype(jnp.int32)
    lane = lanes((1, KEYS))
    own = chip * 2 * T + core * T + rows((T, 1))

    def bias(query, key, there):
        seen = key <= query
        for j in range(2):
            first, last = info_ref[3 + j], info_ref[5 + j]
            seen |= (query >= first) & (query < last) & (key >= first) & (key < last)
        same = (query >= border) == (key >= border)
        return jnp.where(seen & same & there, 0.0, NEG_FILL).astype(F32)

    qbias_ref[...] = bias(own, info_ref[2] + lane, lane >= 0)
    other = (lane >= KEYS // 2).astype(jnp.int32)
    step = (lane - other * (KEYS // 2)) >> 7
    query = (chip + step) * 2 * T + (core ^ other) * T + (lane & (T - 1))
    kbias_ref[...] = bias(query, own, query < BLOCKS * T)


def masks(info, docs):
    bias = jax.ShapeDtypeStruct((T, KEYS), F32)
    return pl.pallas_call(
        masks_kernel,
        out_shape=(bias, bias),
        in_specs=[SMEM, VMEM],
        out_specs=(VMEM,) * 2,
        compiler_params=params(12),
        cost_estimate=cost(40 * T * KEYS, 2e6),
        name="masks",
    )(info, docs)


WINDOW = 10


def attend_kernel(at_ref, q_ref, kv_hbm, bias_ref, wo_ref, o_ref, part_ref, stats_ref, kvs, sems):
    start = pl.multiple_of(at_ref[0], T)
    copies = []
    for i in range(2):
        cut = pl.ds(i * HW, HW)
        copies.append(pltpu.make_async_copy(kv_hbm.at[pl.ds(start, KEYS), cut], kvs.at[:, cut], sems.at[i]))
        copies[i].start()
    copies[0].wait()
    stats, outs = [], []
    for h in range(HEADS):
        cut = slice(h * 128, (h + 1) * 128)
        vcut = slice(HW + h * 128, HW + (h + 1) * 128)
        q = q_ref[:, cut]
        s = dot_nt(q, kvs[:, cut]) * SCALE + bias_ref[...]
        high = jnp.max(s, axis=1, keepdims=True)
        e = jnp.exp(s - high)
        total = jnp.sum(e, axis=1, keepdims=True)
        p = (e * (1.0 / total)).astype(BF16)
        if h == 0:
            copies[1].wait()
        outs.append(dot(p, kvs[:, vcut]))
        stats += list(split3((high + jnp.log(total)) * (-1.0 / SCALE)))
    o = jnp.concatenate(outs, axis=1)
    o_ref[...] = o
    part_ref[...] = dot(o.astype(BF16), wo_ref[...]).astype(BF16)
    stats_ref[...] = per_token([None] * (3 * HEADS) + stats)


def attend(at, q, kv_all, bias, wo):
    return pl.pallas_call(
        attend_kernel,
        out_shape=(
            jax.ShapeDtypeStruct((T, HW), F32),
            jax.ShapeDtypeStruct((T, D), BF16),
            jax.ShapeDtypeStruct((T, EXTRA), BF16),
        ),
        in_specs=[SMEM, VMEM, ANY, VMEM, VMEM],
        out_specs=(VMEM,) * 3,
        scratch_shapes=[pltpu.VMEM((KEYS, 2 * HW), BF16), pltpu.SemaphoreType.DMA((2,))],
        compiler_params=params(60),
        cost_estimate=cost(4 * T * KEYS * HW + 2 * T * HW * D, 6e6),
        name="attend",
    )(at, q, kv_all, bias, wo)


def gate_kernel(x_ref, a_ref, b_ref, g_ref, wr_ref, hot_ref, r_ref, h2p_ref, gates_ref):
    r = x_ref[...].astype(F32) + (a_ref[...].astype(F32) + b_ref[...].astype(F32))
    r_ref[...] = r
    inverse = lax.rsqrt(jnp.mean(r * r, axis=1, keepdims=True) + EPSILON)
    h2 = (r * inverse * g_ref[...]).astype(BF16)
    hot = hot_ref[...] > 0.5
    logits = jnp.where(hot, dot_nt(h2, wr_ref[...]), NEG_FILL)
    e = jnp.where(hot, jnp.exp(logits - jnp.max(logits, axis=1, keepdims=True)), 0.0)
    gates = e / jnp.sum(e, axis=1, keepdims=True)
    gates_ref[...] = gates
    first = gates.astype(BF16).astype(F32)
    h2p_ref[:, :D] = h2
    h2p_ref[:, D:] = (first + pltpu.roll(gates - first, 64, 1)).astype(BF16)


def gate(x, a, b, gain, wr, hot):
    return pl.pallas_call(
        gate_kernel,
        out_shape=(
            jax.ShapeDtypeStruct((T, D), F32),
            jax.ShapeDtypeStruct((T, D + EXTRA), BF16),
            jax.ShapeDtypeStruct((T, EXTRA), F32),
        ),
        in_specs=[VMEM] * 6,
        out_specs=(VMEM,) * 3,
        compiler_params=params(24),
        cost_estimate=cost(2 * T * D * 128, 2e6),
        name="gate",
    )(x, a, b, gain, wr, hot)


def silu_parts(gate_pre):
    sigmoid = 1.0 / (1.0 + jnp.exp(-gate_pre))
    return gate_pre * sigmoid, sigmoid * (1.0 + gate_pre * (1.0 - sigmoid))


def shared_kernel(h2p_ref, dy_ref, wg_ref, wu_ref, wd_ref, out_ref, dh_ref, sh_ref, dsg_ref, dsu_ref):
    h2 = h2p_ref[:, :D]
    sg = dot_nt(h2, wg_ref[...])
    su = dot_nt(h2, wu_ref[...])
    act, slope = silu_parts(sg)
    sh = (act * su).astype(BF16)
    sh_ref[...] = sh
    out_ref[...] = dot(sh, wd_ref[...])
    dsh = dot_nt(dy_ref[...], wd_ref[...])
    dsg = (dsh * su * slope).astype(BF16)
    dsu = (dsh * act).astype(BF16)
    dsg_ref[...] = dsg
    dsu_ref[...] = dsu
    dh_ref[...] = dot(dsg, wg_ref[...]) + dot(dsu, wu_ref[...])


def shared(h2p, dy, wg, wu, wd):
    hidden = jax.ShapeDtypeStruct((T, FF), BF16)
    return pl.pallas_call(
        shared_kernel,
        out_shape=(jax.ShapeDtypeStruct((T, D), F32), jax.ShapeDtypeStruct((T, D), F32), hidden, hidden, hidden),
        in_specs=[VMEM] * 5,
        out_specs=(VMEM,) * 5,
        compiler_params=params(24),
        cost_estimate=cost(1e6, 1e5),
        name="shared",
    )(h2p, dy, wg, wu, wd)


PAIR = 2 * E * CAP


def dispatch_kernel(rank_ref, dy_ref, hot_ref, out_ref):
    rank = rank_ref[0]
    spread = (rows((EXTRA, PAIR)) == rank * E + ((lanes((EXTRA, PAIR)) & (E * CAP - 1)) >> 4)).astype(BF16)
    place = (lanes((2 * T, PAIR)) & (CAP - 1)).astype(F32)
    own = (lanes((2 * T, PAIR)) >= E * CAP) == (rows((2 * T, PAIR)) >= T)
    for k in range(2):
        at = slice(k * 2 * T, (k + 1) * 2 * T)
        hot = jnp.where(own & (dot(dy_ref[at, D:], spread) == place), 1.0, 0.0).astype(BF16)
        hot_ref[at, :] = hot
        dy = dot_tn(hot, dy_ref[at, :D]).astype(BF16)
        for j in range(2):
            to = slice((k * 2 + j) * CAP, (k * 2 + j + 1) * CAP)
            for i in range(E):
                out_ref[i, to, :] = dy[(j * E + i) * CAP : (j * E + i + 1) * CAP]


def dispatch(rank, dy_all):
    return pl.pallas_call(
        dispatch_kernel,
        out_shape=(
            jax.ShapeDtypeStruct((BLOCKS * T, PAIR), BF16),
            jax.ShapeDtypeStruct((E, BLOCKS * CAP, D), BF16),
        ),
        grid=(BLOCKS // 4,),
        in_specs=[SMEM, pl.BlockSpec((4 * T, D + EXTRA), lambda k: (k, 0))],
        out_specs=(pl.BlockSpec((4 * T, PAIR), lambda k: (k, 0)), pl.BlockSpec((E, 4 * CAP, D), lambda k: (0, k, 0))),
        compiler_params=params(60, dimension_semantics=("arbitrary",)),
        cost_estimate=cost(2 * BLOCKS * T * PAIR * D, 1e7),
        name="dispatch",
    )(rank, dy_all)


def experts_kernel(rank_ref, hot_ref, dy_ref, h2_hbm, wg_ref, wu_ref, wd_ref, out_ref, grads_hbm, h2s, xs, gs, stage, sems, outs):
    e = pl.program_id(0)
    rank = rank_ref[0]
    slot = e & 1

    def result(slot, group):
        to = pl.ds(pl.multiple_of(group * 2 * FF, 128), 2 * FF)
        return pltpu.make_async_copy(stage.at[slot], grads_hbm.at[:, to], outs.at[slot])

    @pl.when(e == 0)
    def _():
        copies = []
        for k in range(0, BLOCKS, 2):
            at = pl.ds(k * T, 2 * T)
            copies.append(pltpu.make_async_copy(h2_hbm.at[at, :], h2s.at[at, :], sems.at[k // 2]))
        for copy in copies:
            copy.start()
        named = rank * E + ((rows((PAIR, EXTRA)) & (E * CAP - 1)) >> 4)
        column = lanes((PAIR, EXTRA))
        mine = (column == named) | (column == named + 64)
        for k in range(0, BLOCKS, 2):
            at = slice(k * T, (k + 2) * T)
            copies[k // 2].wait()
            x = dot_tn(hot_ref[at, :], h2s[at, :])
            g = jnp.sum(jnp.where(mine, x[:, D:], 0.0), axis=1, keepdims=True)
            g = jnp.broadcast_to(g, (PAIR, 128))
            x = x[:, :D].astype(BF16)
            for j in range(2):
                to = slice((k + j) * CAP, (k + j + 1) * CAP)
                for i in range(E):
                    cut = slice((j * E + i) * CAP, (j * E + i + 1) * CAP)
                    xs[i, to, :] = x[cut]
                    gs[i, to, :] = g[cut]

    x = xs[e]
    g = gs[e][:, :1]
    eg = dot_nt(x, wg_ref[0])
    eu = dot_nt(x, wu_ref[0])
    act, slope = silu_parts(eg)
    eh = act * eu
    geh = (g * eh).astype(BF16)
    eh = eh.astype(BF16)
    dy = dy_ref[0]
    deh = dot_nt(dy, wd_ref[0])
    dgate = jnp.sum(eh.astype(F32) * deh, axis=1, keepdims=True)
    deh = g * deh
    deg = (deh * eu * slope).astype(BF16)
    deu = (deh * act).astype(BF16)
    shape = (BLOCKS, CAP, -1)
    out_ref[:, 0, :, D + EXTRA :] = (g * dot(eh, wd_ref[0])).astype(BF16).reshape(shape)
    out_ref[:, 0, :, :D] = (dot(deg, wg_ref[0]) + dot(deu, wu_ref[0])).astype(BF16).reshape(shape)
    column = lanes((BLOCKS * CAP, EXTRA))
    expert = rank * E + e
    first = dgate.astype(BF16).astype(F32)
    placed = jnp.where(column == expert, first, jnp.where(column == expert + 64, dgate - first, 0.0))
    out_ref[:, 0, :, D : D + EXTRA] = placed.astype(BF16).reshape(shape)

    @pl.when(e >= 2)
    def _():
        result(slot, e - 2).wait()

    dgu = jnp.concatenate([deg, deu], axis=1)
    for r in range(0, D, 256):
        stage[slot, r : r + 256, :] = dot_tn(x[:, r : r + 256], dgu).astype(BF16)
    result(slot, e).start()

    @pl.when(slot == 0)
    def _():
        @pl.when(e == 2)
        def _():
            result(2, E).wait()

        for r in range(0, D, 256):
            stage[2, r : r + 256, :FF] = dot_tn(dy[:, r : r + 256], geh).astype(BF16)

    @pl.when(slot == 1)
    def _():
        for r in range(0, D, 256):
            stage[2, r : r + 256, FF:] = dot_tn(dy[:, r : r + 256], geh).astype(BF16)
        result(2, E + (e >> 1)).start()

    @pl.when(e == E - 1)
    def _():
        result(0, E - 2).wait()
        result(1, E - 1).wait()
        result(2, E + 1).wait()


GRADS = 6
BACK = D + EXTRA + D


def experts(rank, hot, dy, h2_all, wg, wu, wd):
    n = BLOCKS * CAP
    per = lambda shape: pl.BlockSpec((1, *shape), lambda e: (e, 0, 0))
    held = lambda shape: pl.BlockSpec(shape, lambda e: (0,) * len(shape), pipeline_mode=pl.Buffered(1))
    return pl.pallas_call(
        experts_kernel,
        out_shape=(
            jax.ShapeDtypeStruct((BLOCKS, E, CAP, BACK), BF16),
            jax.ShapeDtypeStruct((D, GRADS * 2 * FF), BF16),
        ),
        grid=(E,),
        in_specs=[SMEM, held((BLOCKS * T, PAIR)), per((n, D)), ANY, per((FF, D)), per((FF, D)), per((FF, D))],
        out_specs=(pl.BlockSpec((BLOCKS, 1, CAP, BACK), lambda e: (0, e, 0, 0)), ANY),
        scratch_shapes=[
            pltpu.VMEM((BLOCKS * T, D + EXTRA), BF16),
            pltpu.VMEM((E, n, D), BF16),
            pltpu.VMEM((E, n, 128), F32),
            pltpu.VMEM((3, D, 2 * FF), BF16),
            pltpu.SemaphoreType.DMA((BLOCKS // 2,)),
            pltpu.SemaphoreType.DMA((3,)),
        ],
        compiler_params=params(58, dimension_semantics=("arbitrary",)),
        cost_estimate=cost(2 * E * n * D * FF * 9, 5e7),
        name="experts",
    )(rank, hot, dy, h2_all, wg, wu, wd)


def combine_kernel(place_ref, back_ref, dh_ref, out_ref, back_out_ref, mixed_ref):
    total = dot(place_ref[...], back_ref[...])
    back_out_ref[:, :D] = (total[:, :D] + dh_ref[...]).astype(BF16)
    back_out_ref[:, D:] = total[:, D : D + EXTRA].astype(BF16)
    mixed_ref[...] = (total[:, D + EXTRA :] + out_ref[...]).astype(BF16)


def combine(place, back, dh, out):
    return pl.pallas_call(
        combine_kernel,
        out_shape=(jax.ShapeDtypeStruct((T, D + EXTRA), BF16), jax.ShapeDtypeStruct((T, D), BF16)),
        in_specs=[VMEM] * 4,
        out_specs=(VMEM,) * 2,
        compiler_params=params(24),
        cost_estimate=cost(2 * T * COUNT * BACK, 7e6),
        name="combine",
    )(place, back.reshape(COUNT, BACK), dh, out)


def middle_kernel(a_ref, b_ref, r_ref, dy_ref, h2p_ref, gates_ref, g_ref, wr_ref, wo_ref, o_ref, stats_ref, dr_ref, da_ref, dop_ref, dlog_ref, gain_ref):
    both = a_ref[...].astype(F32) + b_ref[...].astype(F32)
    gates = gates_ref[...]
    dgate = both[:, D:] + pltpu.roll(both[:, D:], 64, 1)
    dsel = gates * (dgate - jnp.sum(gates * dgate, axis=1, keepdims=True))
    dlog = dsel.astype(BF16)
    dlog_ref[...] = dlog
    dh2 = both[:, :D] + dot(dlog, wr_ref[...])
    r = r_ref[...]
    inverse = lax.rsqrt(jnp.mean(r * r, axis=1, keepdims=True) + EPSILON)
    unit = r * inverse
    gain_ref[...] = (dh2 * unit).astype(BF16)
    e2 = dh2 * g_ref[...]
    dr = dy_ref[...].astype(F32) + inverse * (e2 - unit * jnp.mean(e2 * unit, axis=1, keepdims=True))
    dr_ref[...] = dr
    da = dr.astype(BF16)
    da_ref[...] = da
    do = dot_nt(da, wo_ref[...]).astype(BF16)
    dop_ref[:, :HW] = do
    stats = []
    both = do.astype(F32) * o_ref[...]
    for h in range(HEADS):
        stats += list(split3(-jnp.sum(both[:, h * 128 : (h + 1) * 128], axis=1, keepdims=True)))
    dop_ref[:, HW:] = per_token(stats) + stats_ref[...]


def middle(a, b, r, dy, h2p, gates, gain, wr, wo, o, stats):
    return pl.pallas_call(
        middle_kernel,
        out_shape=(
            jax.ShapeDtypeStruct((T, D), F32),
            jax.ShapeDtypeStruct((T, D), BF16),
            jax.ShapeDtypeStruct((T, HW + EXTRA), BF16),
            jax.ShapeDtypeStruct((T, EXTRA), BF16),
            jax.ShapeDtypeStruct((T, D), BF16),
        ),
        in_specs=[VMEM] * 11,
        out_specs=(VMEM,) * 5,
        compiler_params=params(24),
        cost_estimate=cost(2 * T * D * (HW + 128), 5e6),
        name="middle",
    )(a, b, r, dy, h2p, gates, gain, wr, wo, o, stats)


HALF = 3 * HW // 2
PADDED = 1024


def attend_back_kernel(*refs):
    at_ref, q_hbm, kv_hbm, do_hbm, refs = refs[0], refs[1], refs[2], refs[3 : 3 + WINDOW], refs[3 + WINDOW :]
    w_hbm, refs = refs[:3], refs[3:]
    kv_ref, qbias_ref, kbias_ref, cos_ref, sin_ref, mine_ref, theirs_ref, part_ref, kvs, qs, dos, ws, sems = refs
    keys_at = pl.ds(pl.multiple_of(at_ref[WINDOW], T), KEYS)
    copies = [pltpu.make_async_copy(v, dos.at[i], sems.at[i]) for i, v in enumerate(do_hbm)]
    for i in range(WINDOW):
        source = q_hbm.at[pl.ds(pl.multiple_of(at_ref[i], T), T), :]
        copies.append(pltpu.make_async_copy(source, qs.at[i], sems.at[WINDOW + i]))
    copies += [pltpu.make_async_copy(v, ws.at[i], sems.at[2 * WINDOW + i]) for i, v in enumerate(w_hbm)]
    copies.append(pltpu.make_async_copy(kv_hbm.at[keys_at, :], kvs, sems.at[2 * WINDOW + 3]))
    early = [2 * WINDOW + 3, 0, WINDOW]
    late = [i for i in range(2 * WINDOW) if i not in early]
    weights = [2 * WINDOW, 2 * WINDOW + 1, 2 * WINDOW + 2]
    for i in early + late + weights:
        copies[i].start()
    for i in early:
        copies[i].wait()
    lane = lanes((T, EXTRA))
    extra = dos[0, :, HW:]
    stats = extra.astype(F32)
    side = lambda parts: jnp.concatenate(parts, axis=1)
    block = lambda v, i: v[:, i * T : (i + 1) * T]
    every = range(WINDOW)
    heads = [(slice(h * 128, (h + 1) * 128), slice(HW + h * 128, HW + (h + 1) * 128)) for h in range(HEADS)]
    its = lambda first: (lane >= first) & (lane < first + 3)
    dqs, dks, dvs = [], [], []
    for h, (cut, vcut) in enumerate(heads):
        less_dot = jnp.sum(jnp.where(its(3 * h), stats, 0.0), axis=1, keepdims=True)
        less = jnp.sum(jnp.where(its(3 * (HEADS + h)), stats, 0.0), axis=1, keepdims=True)
        q, do = qs[0, :, cut], dos[0, :, cut]
        p = jnp.exp((dot_nt(q, kvs[:, cut]) + less) * SCALE + qbias_ref[...])
        dp = dot_nt(do, kvs[:, vcut]) + less_dot
        ds = (p * dp * SCALE).astype(BF16)
        dqs.append(dot(ds, kvs[:, cut]))
    for i in late:
        copies[i].wait()
    for h, (cut, vcut) in enumerate(heads):
        k_wide = side([kv_ref[:, cut], its(3 * (HEADS + h)).astype(BF16)])
        v_wide = side([kv_ref[:, vcut], its(3 * h).astype(BF16)])
        pt = side([dot_nt(k_wide, side([qs[i, :, cut], dos[i, :, HW:]])) for i in every])
        pt = jnp.exp(pt * SCALE + kbias_ref[...])
        dpt = side([dot_nt(v_wide, side([dos[i, :, cut], dos[i, :, HW:]])) for i in every])
        dst = (pt * dpt * SCALE).astype(BF16)
        pt = pt.astype(BF16)
        dks.append(sum(dot(block(dst, i), qs[i, :, cut]) for i in every))
        dvs.append(sum(dot(block(pt, i), dos[i, :, cut]) for i in every))
    cosine, sine = cos_ref[...], -sin_ref[...]
    dq = turn(side(dqs), cosine, sine).astype(BF16)
    dk = turn(side(dks), cosine, sine).astype(BF16)
    dv = side(dvs).astype(BF16)
    dqkv = side([dq, dk, dv])
    none = jnp.zeros((T, PADDED - HALF), BF16)
    low, high = side([dqkv[:, :HALF], none]), side([dqkv[:, HALF:], none])
    first = at_ref[WINDOW + 1] == 0
    mine_ref[...] = jnp.where(first, low, high)
    theirs_ref[...] = jnp.where(first, high, low)
    for i in weights:
        copies[i].wait()
    part = dot_nt(dq, ws[0]) + dot_nt(dk, ws[1]) + dot_nt(dv, ws[2])
    part_ref[...] = part.astype(BF16)


def attend_back(at, q_all, kv_all, dos, kv, qbias, kbias, cosine, sine, wq, wk, wv):
    return pl.pallas_call(
        attend_back_kernel,
        out_shape=(
            jax.ShapeDtypeStruct((T, PADDED), BF16),
            jax.ShapeDtypeStruct((T, PADDED), BF16),
            jax.ShapeDtypeStruct((T, D), BF16),
        ),
        in_specs=[SMEM] + [ANY] * (5 + WINDOW) + [VMEM] * 5,
        out_specs=(VMEM,) * 3,
        scratch_shapes=[
            pltpu.VMEM((KEYS, 2 * HW), BF16),
            pltpu.VMEM((WINDOW, T, HW), BF16),
            pltpu.VMEM((WINDOW, T, HW + EXTRA), BF16),
            pltpu.VMEM((3, D, HW), BF16),
            pltpu.SemaphoreType.DMA((2 * WINDOW + 4,)),
        ],
        compiler_params=params(56),
        cost_estimate=cost(16 * T * KEYS * HW + 6 * T * HW * D, 2e7),
        name="attend_back",
    )(at, q_all, kv_all, *dos, wq, wk, wv, kv, qbias, kbias, cosine, sine)


WIDE = 384


def chunks_kernel(h1_ref, out_ref):
    at = lanes((1, WIDE))
    part = jnp.zeros((1, WIDE), jnp.int32)
    for j in range(1, 8):
        part += (at >= 40 * j).astype(jnp.int32)
    for z in range(4):
        source = part * 160 + z * 40 + (at - part * 40)
        place = ((rows((D, WIDE)) == source) & (at < 320)).astype(BF16)
        out_ref[z] = dot(h1_ref[...], place).astype(BF16)


def chunks(h1):
    return pl.pallas_call(
        chunks_kernel,
        out_shape=jax.ShapeDtypeStruct((4, h1.shape[0], WIDE), BF16),
        in_specs=[VMEM],
        out_specs=VMEM,
        compiler_params=params(16),
        cost_estimate=cost(2 * h1.shape[0] * D * 4 * WIDE, 2e6),
        name="chunks",
    )(h1)


SUM_B, SUM_A = 384, 768
USED_B, USED_A = (HW + 64) // 2, 3 * FF // 2
GRADS_WIDTH = GRADS * 2 * FF


def projection_grads_kernel(*refs):
    left_hbm, parts, grads_hbm = refs[0], refs[1:6], refs[6]
    out_ref, expert_outs, (left, right, grads, ready, sems, out_sems) = refs[7], refs[8:11], refs[11:]
    copies = [pltpu.make_async_copy(grads_hbm, grads, sems.at[6])]
    copies.append(pltpu.make_async_copy(left_hbm, left, sems.at[0]))
    at = 0
    for i, part in enumerate(parts):
        n = part.shape[0]
        copies.append(pltpu.make_async_copy(part, right.at[pl.ds(at, n), :], sems.at[1 + i]))
        at += n
    for copy in copies:
        copy.start()
    copies[0].wait()
    writes = []
    for e in range(E):
        gate_up = grads[:, e * 2 * FF : (e + 1) * 2 * FF].astype(F32)
        start = (2 * E + e) * FF
        if e % 2 == 0:
            down = grads[:, start : start + 2 * FF].astype(F32)
        ready[e % 2, 0] = gate_up[:, :FF]
        ready[e % 2, 1] = gate_up[:, FF:]
        ready[e % 2, 2] = down[:, (e % 2) * FF : (e % 2 + 1) * FF]
        for i, out in enumerate(expert_outs):
            writes.append(pltpu.make_async_copy(ready.at[e % 2, i], out.at[e], out_sems.at[e % 2, i]))
            writes[-1].start()
        if e in (1, 2):
            for write in writes[3 * (e - 1) : 3 * e]:
                write.wait()
    for copy in copies[1:]:
        copy.wait()
    out_ref[...] = dot_tn(left[...], right[...])[:320].astype(BF16)
    for write in writes[6:]:
        write.wait()


def projection_grads(left, parts, grads):
    expert = jax.ShapeDtypeStruct((E, D // 4, FF), F32)
    return pl.pallas_call(
        projection_grads_kernel,
        out_shape=(jax.ShapeDtypeStruct((320, PADDED), BF16), expert, expert, expert),
        in_specs=[ANY] * 7,
        out_specs=(VMEM, ANY, ANY, ANY),
        scratch_shapes=[
            pltpu.VMEM((8 * T, WIDE), BF16),
            pltpu.VMEM((8 * T, PADDED), BF16),
            pltpu.VMEM((320, GRADS_WIDTH), BF16),
            pltpu.VMEM((2, 3, 320, FF), F32),
            pltpu.SemaphoreType.DMA((7,)),
            pltpu.SemaphoreType.DMA((2, 3)),
        ],
        compiler_params=params(56),
        cost_estimate=cost(2 * 8 * T * WIDE * PADDED, 2e7),
        name="projection_grads",
    )(left, *parts, grads)


def other_sums_kernel(left_ref, right_ref, sums_ref, out_ref):
    out_ref[:, :USED_A] = sums_ref[:, :USED_A]
    out_ref[:, USED_A:] = dot_tn(left_ref[...], right_ref[...])[:, :USED_B].astype(BF16)


def other_sums(left, right, sums):
    return pl.pallas_call(
        other_sums_kernel,
        out_shape=jax.ShapeDtypeStruct((D, USED_A + USED_B), BF16),
        in_specs=[VMEM] * 3,
        out_specs=VMEM,
        compiler_params=params(24),
        cost_estimate=cost(2 * left.shape[0] * D * SUM_B, 8e6),
        name="other_sums",
    )(left, right, sums)


def own_and_others(core_ref, parts_ref, keep_ref, give_ref):
    total = parts_ref[0].astype(F32)
    for i in range(1, 8):
        total += parts_ref[i].astype(F32)
    first = core_ref[0] == 0
    keep_ref[...] = jnp.where(first, total[:20], total[20:])
    give_ref[...] = jnp.where(first, total[20:], total[:20])
    return total


def add_up_kernel(core_ref, parts_ref, keep_ref, give_ref):
    own_and_others(core_ref, parts_ref, keep_ref, give_ref)


def add_up_gain_kernel(core_ref, parts_ref, weight_ref, keep_ref, give_ref, gain_ref):
    total = own_and_others(core_ref, parts_ref, keep_ref, give_ref)
    gain_ref[...] = jnp.broadcast_to(jnp.sum(total * weight_ref[...], axis=1, keepdims=True), (40, 128))


def add_up(core, parts, *weight):
    half = jax.ShapeDtypeStruct((20, parts.shape[2]), F32)
    outs = (half, half) + (jax.ShapeDtypeStruct((40, 128), F32),) * len(weight)
    return pl.pallas_call(
        add_up_gain_kernel if weight else add_up_kernel,
        out_shape=outs,
        in_specs=[SMEM] + [VMEM] * (1 + len(weight)),
        out_specs=(VMEM,) * len(outs),
        compiler_params=params(24),
        cost_estimate=cost(1e6, 2e6),
        name="add_up",
    )(core, parts, *weight)


def dense_outputs_kernel(core_ref, keep_ref, got_ref, keep2_ref, got2_ref, g0, g1, g2, g3, q_ref, k_ref, v_ref, o_ref, router_ref, gate_ref, up_ref, down_ref, gains_ref):
    first = core_ref[0] == 0

    def halves(keep, got):
        low, high = jnp.where(first, keep, got), jnp.where(first, got, keep)
        return lambda at, n: jnp.concatenate([low[:, at : at + n], high[:, at : at + n]], axis=1)

    qkv = halves(keep_ref[...], got_ref[...])(0, HALF)
    q_ref[...] = qkv[:, :HW]
    k_ref[...] = qkv[:, HW : 2 * HW]
    v_ref[...] = qkv[:, 2 * HW :]
    columns = halves(keep2_ref[...], got2_ref[...])
    other = columns(USED_A, USED_B)
    o_ref[...] = other[:, :HW]
    router_ref[...] = other[:, HW : HW + 63]
    expert = columns(0, USED_A)
    gate_ref[...] = expert[:, :FF]
    up_ref[...] = expert[:, FF : 2 * FF]
    down_ref[...] = expert[:, 2 * FF :]
    gain = g0[...] + g1[...] + g2[...] + g3[...]
    gain = jnp.where(first, gain[:20], gain[20:])
    lane = lanes((20, 128))
    both = jnp.where(lane == 0, gain, 0.0) + jnp.where(lane == 1, other[:, HW + 63 :], 0.0)
    same = (rows((20, 20)) == lanes((20, 20))).astype(F32)
    gains_ref[...] = lax.dot_general(both, same, (((0,), (0,)), ((), ())), precision=lax.Precision.HIGHEST, preferred_element_type=F32)


def dense_outputs(core, qkv, others, gains):
    out = lambda n: jax.ShapeDtypeStruct((20, n), F32)
    return pl.pallas_call(
        dense_outputs_kernel,
        out_shape=(out(HW), out(HW), out(HW), out(HW), out(63), out(FF), out(FF), out(FF), jax.ShapeDtypeStruct((128, 20), F32)),
        in_specs=[SMEM] + [VMEM] * 8,
        out_specs=(VMEM,) * 9,
        compiler_params=params(16),
        cost_estimate=cost(1e6, 1e6),
        name="dense_outputs",
    )(core, *qkv, *others, *gains)


def ep_perm(dyl, dz, dc):
    at = lambda yl, z, c: (yl * 4 + z) * 2 + c
    return [
        (at(yl, z, c), at(yl ^ dyl, (z + dz) % 4, c ^ dc)) for yl in range(2) for z in range(4) for c in range(2)
    ]


CORE = ep_perm(0, 0, 1)


def send(value, perm):
    return lax.ppermute(value, EP, perm)


def swap(value, axis):
    return lax.ppermute(value, axis, [(0, 1), (1, 0)])


def to_owners(value):
    return lax.all_to_all(value, EP, split_axis=0, concat_axis=0, tiled=True)


def window_perm(step, back):
    pairs = [(i, i + step) for i in range(8 - step) if i + step < 5 or i >= 3]
    pairs = [(j, i) if back else (i, j) for i, j in pairs]
    return [(2 * i + c, 2 * j + c) for i, j in pairs for c in range(2)]


def window(value, back):
    own = [value] + [send(value, window_perm(step, back)) for step in range(1, 5)]
    return own


def with_other_core(own):
    return list(own) + [send(v, CORE) for v in own]


def both_cores(left):
    return jnp.concatenate([left, swap(left, "c")], axis=0)


def dense_right(right, core):
    half = right.shape[1] // 2
    mine = jnp.where(core == 0, right[:, :half], right[:, half:])
    theirs = jnp.where(core == 0, right[:, half:], right[:, :half])
    return both_cores_of(mine, theirs)


def both_cores_of(mine, theirs):
    return jnp.concatenate([mine, swap(theirs, "c")], axis=0)


def products(left, right):
    return dot_tn(left, right).astype(BF16)


UP = [(0, 1), (1, 2), (2, 3), (3, 0)]
DOWN = [(1, 0), (2, 1), (3, 2), (0, 3)]


def z_gather_far(below, above):
    half = below.shape[0] // 2
    return lax.ppermute(below[:half], "z", UP), lax.ppermute(above[half:], "z", DOWN)


def xy_sum(part):
    parts = lax.all_to_all(part, ("x", "yl"), split_axis=0, concat_axis=0, tiled=True)
    return jnp.sum(parts.astype(F32), axis=0)


def rotation(positions):
    half = HEAD_DIM // 2
    frequency = BASE ** (-(jnp.arange(half, dtype=F32) * 2.0) / HEAD_DIM)
    angles = positions.astype(F32)[:, None] * frequency[None, :]
    cosine, sine = jnp.cos(angles), jnp.sin(angles)
    return jnp.concatenate([cosine, cosine], axis=1), jnp.concatenate([-sine, sine], axis=1)


def after(values, ready):
    return lax.optimization_barrier((values, ready))


def local(
    tokens, grad_out, doc_ids, piece_starts, piece_ends, routes, norm1_gain, norm2_gain, query_weight, key_weight, value_weight,
    output_weight, router_weight, shared_gate, shared_up, shared_down, expert_gate, expert_up, expert_down,
):
    core, z = lax.axis_index("c"), lax.axis_index("z")
    rank = lax.axis_index(EP).astype(jnp.int32)
    gain1, gain2 = norm1_gain[None, :], norm2_gain[None, :]
    wr = jnp.pad(router_weight.T, ((0, EXTRA - router_weight.shape[1]), (0, 0)))
    cosine, sine = rotation(rank * T + jnp.arange(T, dtype=jnp.int32))
    keys_at = jnp.where(rank < 10, 0, 768).astype(jnp.int32)
    info = jnp.concatenate([jnp.stack([rank // 2, rank % 2, keys_at]), piece_starts[0], piece_ends[0]]).astype(jnp.int32)
    entry = jnp.arange(WINDOW, dtype=jnp.int32)
    seen_from = jnp.minimum(rank // 2 + entry % 5, 7) * 2 + (rank % 2) ^ (entry // 5)
    group = lambda v: lax.all_gather(v, EP, axis=0, tiled=True)

    h1, kv = project(tokens, norm1_gain, key_weight, value_weight, cosine, sine)
    kv_all = group(kv)
    q = project_q(h1, query_weight, cosine, sine)
    h1_left = lax.all_to_all(chunks(h1), "z", split_axis=0, concat_axis=0, tiled=True)
    h1_left = jnp.stack([h1_left, swap(h1_left, "c")], axis=1)
    pick = lambda i: lax.dynamic_slice_in_dim(h1_left, i % 4, 1, 0)
    h1_left = jnp.concatenate([pick(z), pick(z + 3), pick(z + 1), pick(z + 2)], axis=0)
    dyp, hot, place = slots(routes.T, grad_out)
    qbias, kbias = masks(info, doc_ids)
    at = lax.axis_index("x") * 320 + lax.axis_index("yl") * 160 + z * 40
    here = lambda v: lax.dynamic_slice_in_dim(v, at, 40, 0)
    weight = jnp.concatenate([here(query_weight), here(key_weight), here(value_weight)], axis=1).astype(F32)
    weight = jnp.where(core == 0, weight[:, :HALF], weight[:, HALF:]) / here(norm1_gain)[:, None]
    weight = jnp.pad(weight, ((0, 0), (0, PADDED - HALF)))
    (dyp, q, h1_left, qbias, kbias, weight), kv_all = after((dyp, q, h1_left, qbias, kbias, weight), kv_all)
    dy_all = group(dyp)
    o, part, stats = attend(keys_at[None], q, kv_all, qbias, output_weight)
    r, h2p, gates = gate(tokens, part, swap(part, "yh"), gain2, wr, hot)
    h2_all = group(h2p)
    shared_out, shared_dh, sh, dsg, dsu = shared(h2p, grad_out, shared_gate.T, shared_up.T, shared_down)
    places, dys = dispatch(rank[None], dy_all)

    put = lambda v, before, width: jnp.pad(v, ((0, 0), (before, width - before - v.shape[1])))
    both = 3 * FF // 2
    halves = lambda v, used, padded: jnp.concatenate([put(v[:, :used], 0, padded), put(v[:, used:], 0, padded)], axis=1)
    right = jnp.concatenate([put(jnp.concatenate([dsg, dsu], axis=1), 0, 3 * FF), put(sh, 2 * FF, 3 * FF)], axis=0)
    sums_a = products(
        both_cores(jnp.concatenate([h2p[:, :D], grad_out], axis=0)), dense_right(halves(right, both, 768), core)
    )
    (places, dys, sums_a, late_q), h2_all = after((places, dys, sums_a, q), h2_all)
    q_all = group(late_q)
    back, grads = experts(
        rank[None], places, dys, h2_all, expert_gate.transpose(0, 2, 1), expert_up.transpose(0, 2, 1), expert_down
    )
    grads = lax.psum_scatter(grads, "x", scatter_dimension=0, tiled=True)
    back, mixed = combine(place, to_owners(back.reshape(BLOCKS, E * CAP, BACK)), shared_dh, shared_out)
    dr, da, dop, dlog, gain2_terms = middle(
        back, swap(back, "yh"), r, grad_out, h2p, gates, gain2, wr, output_weight, o, stats
    )
    dos = with_other_core(window(dop, True))

    one = jnp.ones((T, 1), BF16)
    width = HW + 64
    other = jnp.concatenate(
        [put(o.astype(BF16), 0, width), put(dlog[:, :63], HW, width), put(one, width - 1, width)], axis=0
    )
    other_left = both_cores(jnp.concatenate([da, h2p[:, :D], gain2_terms], axis=0))
    other_right = dense_right(halves(other, width // 2, SUM_B), core)
    dos, h1_left, other_left, other_right = lax.optimization_barrier(
        (dos, h1_left.reshape(8 * T, WIDE), other_left, other_right)
    )

    mine, theirs, dh1_part = attend_back(
        jnp.concatenate([seen_from * T, keys_at[None], core.astype(jnp.int32)[None]]), q_all, kv_all, dos, kv, qbias, kbias, cosine, sine, query_weight, key_weight, value_weight
    )
    right = both_cores_of(mine, theirs)
    (other_left, other_right), right = after((other_left, other_right), right)
    sums_ab = other_sums(other_left, other_right, sums_a)
    sums_ab = sums_ab.reshape(8, 4, 40, USED_A + USED_B).transpose(1, 0, 2, 3).reshape(D, USED_A + USED_B)
    sums_ab = lax.psum_scatter(sums_ab, "z", scatter_dimension=0, tiled=True)
    (dh1_part, mixed), right = after((dh1_part, mixed), right)
    output = (r + (mixed.astype(F32) + swap(mixed, "yh").astype(F32))).astype(BF16)
    below, above = lax.ppermute(right, "z", UP), lax.ppermute(right, "z", DOWN)
    rights = [right, below, above, *z_gather_far(below, above)]
    sums_c, gate_grads, up_grads, down_grads = projection_grads(h1_left, rights, grads)
    spread_out = lambda v: lax.all_to_all(v.reshape(8, 40, -1), ("x", "yl"), split_axis=0, concat_axis=0, tiled=True)
    parts = spread_out(sums_c)
    dh1 = dh1_part.astype(F32) + swap(dh1_part, "yh").astype(F32)
    x = tokens.astype(F32)
    inverse = lax.rsqrt(jnp.mean(x * x, axis=1, keepdims=True) + EPSILON)
    unit = x * inverse
    e1 = dh1 * gain1
    grad_tokens = dr + inverse * (e1 - unit * jnp.mean(e1 * unit, axis=1, keepdims=True))
    others, (parts, output, grad_tokens) = after(sums_ab, (parts, output, grad_tokens))
    others = spread_out(others)
    which = core.astype(jnp.int32)[None]
    keep, give, gain = add_up(which, parts, weight)
    across = lax.ppermute(gain, ("c", "yh"), [(0, 3), (1, 2), (2, 1), (3, 0)])
    gains = gain, swap(gain, "yh"), swap(gain, "c"), across
    qkv = keep, swap(give, "c")
    (keep, give), gains = after(add_up(which, others), gains)
    dense = dense_outputs(which, qkv, (keep, swap(give, "c")), gains)

    return (
        output,
        grad_tokens,
        dense[8][0],
        dense[8][1],
        dense[0],
        dense[1],
        dense[2],
        dense[3].T,
        dense[4],
        dense[5],
        dense[6],
        dense[7].T,
        gate_grads,
        up_grads,
        down_grads.transpose(0, 2, 1),
    )


def solution(mesh):
    fine = Mesh(mesh.devices.reshape(4, 2, 4, 2, 2), ("x", "yl", "z", "c", "yh"))
    rows64 = ("x", "yl", "z", "c")
    in_specs = (
        P(rows64, None),
        P(rows64, None),
        P("x", None),
        P("x", None),
        P("x", None),
        P(rows64, None),
        P(),
        P(),
        P(None, "yh"),
        P(None, "yh"),
        P(None, "yh"),
        P("yh", None),
        P(),
        P(None, "yh"),
        P(None, "yh"),
        P("yh", None),
        P(EP, None, "yh"),
        P(EP, None, "yh"),
        P(EP, "yh", None),
    )
    out_specs = (
        P(rows64, None),
        P(rows64, None),
        P(rows64),
        P(rows64),
        P(rows64, "yh"),
        P(rows64, "yh"),
        P(rows64, "yh"),
        P("yh", rows64),
        P(rows64, None),
        P(rows64, "yh"),
        P(rows64, "yh"),
        P("yh", rows64),
        P(EP, "x", "yh"),
        P(EP, "x", "yh"),
        P(EP, "yh", "x"),
    )
    return jax.shard_map(local, mesh=fine, in_specs=in_specs, out_specs=out_specs, check_vma=False)
```
